32 devices in a mesh: blk: 4 (over y, core), grp: 2 (over x), tp: 4 (over z).
Axes of the slice: x: 2, y: 2, z: 4, core: 2. Of those that a mesh axis runs over, the one named last changes fastest.
Arguments:
- dispatched: bfloat16 [2048, 5120], P(('blk', 'grp'), 'tp'), may hold values from -6 to 6
- route_prob: bfloat16 [2048], P(('blk', 'grp')), may hold values from 0.099609375 to 1
- peer_rows: int32 [16], P(('blk', 'grp')), may hold values from 1 to 128, as said below
- gate_weight: bfloat16 [2, 5120, 768], P('grp', 'blk', 'tp'), may hold values from -0.078125 to 0.078125
- up_weight: bfloat16 [2, 5120, 768], P('grp', 'blk', 'tp'), may hold values from -0.078125 to 0.078125
- down_weight: bfloat16 [2, 768, 5120], P('grp', None, 'tp'), may hold values from -0.21875 to 0.21875
Outputs:
- expert_out: bfloat16 [2048, 5120], P(('blk', 'grp'), 'tp')
The draws below stay inside these ranges and needn't reach their ends.
Inputs may be any that keep to these rules, and one draw needn't show every extreme that they name: `peer_rows`: in every draw one expert group receives 128 live rows from every source device.
All inputs are finite; a program needn't handle non-finite values.
Results may differ from the reference program's by a relative error of at most 0.0049.
Values may be sent and summed in bfloat16 or wider, within the bound.
No kernel may reach another device: no remote copies, remote signals or barrier semaphores. Data moves between devices by JAX's collectives and lax.ppermute only.
A program may use at most 64 MiB of HBM per device.

```python
import math
import jax
import jax.numpy as jnp
from jax import lax

D = 5120
HID = 768
ROWS = 256
ROWS_PEER = 128
SOURCES = 8
N_BLK = 4
N_GRP = 2


def draw_peer_rows(key, part):
    key_cap = jax.random.fold_in(key, 11)
    key_full = jax.random.fold_in(key, 12)
    key_rows = jax.random.fold_in(key, 13)
    sources = N_BLK * N_GRP
    caps = jax.random.randint(key_cap, (N_GRP,), ROWS_PEER // 2, ROWS_PEER + 1)
    fullest = jax.random.randint(key_full, (), 0, N_GRP)
    is_full = jnp.arange(N_GRP, dtype=jnp.int32) == fullest
    caps = jnp.where(is_full, ROWS_PEER, jnp.maximum(caps, 1))
    raw = jax.random.randint(key_rows, (sources, N_GRP), 0, 1 << 20)
    counts = 1 + raw % caps[None, :]
    counts = jnp.where(is_full[None, :], ROWS_PEER, counts)
    return counts.reshape(sources * N_GRP).astype(jnp.int32)


def level_of(own_key, shape, shards, least, largest):
    gain = 1.0
    for dim, blocks in shards:
        heights = jax.random.uniform(jax.random.fold_in(jax.random.fold_in(own_key, 6), dim), (blocks,), jnp.float32, least / len(shards), largest / len(shards))
        gain = gain * jnp.repeat(jnp.exp(heights), shape[dim] // blocks).reshape((-1,) + (1,) * (len(shape) - 1 - dim))
    return gain


def normal_values(key, extent, deviation, bound, shards=(), kind=jnp.bfloat16):
    drawn = deviation * jax.random.normal(key, extent, jnp.float32)
    if shards:
        drawn = drawn * level_of(key, extent, shards, -0.22, 0.18)
    return jnp.clip(drawn, -bound, bound).astype(kind)


def setup_inputs(seed: int = 0) -> dict:
    splits = jax.random.split(jax.random.key(seed), 7)
    dispatched = normal_values(splits[0], (SOURCES * ROWS, D), 1.0, 6.0, ((0, 8), (1, 4)))
    route_prob = jnp.clip(jnp.exp(math.log(1.0) - 2.306499 * jax.random.uniform(splits[1], (SOURCES * ROWS,), jnp.float32) ** level_of(splits[1], (SOURCES * ROWS,), ((0, 8),), -0.2, 0.2)), 0.099609375, 1.0).astype(jnp.bfloat16)
    peer_rows = draw_peer_rows(jax.random.fold_in(splits[6], 71), 0)
    gate_weight = normal_values(splits[3], (N_GRP, D, HID), D ** -0.5, 0.078125, ((0, 2), (1, 4), (2, 4)))
    up_weight = normal_values(splits[4], (N_GRP, D, HID), D ** -0.5, 0.078125, ((0, 2), (1, 4), (2, 4)))
    down_weight = normal_values(splits[5], (N_GRP, HID, D), HID ** -0.5, 0.21875, ((0, 2), (2, 4)))
    return {"dispatched": dispatched, "route_prob": route_prob, "peer_rows": peer_rows, "gate_weight": gate_weight, "up_weight": up_weight, "down_weight": down_weight}


def reference(dispatched, route_prob, peer_rows, gate_weight, up_weight, down_weight):
    rows_peer = ROWS_PEER
    tokens = dispatched.reshape(N_BLK, N_GRP, N_GRP, rows_peer, D).transpose(2, 0, 1, 3, 4)
    chances = route_prob.astype(jnp.float32).reshape(N_BLK, N_GRP, N_GRP, rows_peer).transpose(2, 0, 1, 3)
    tallies = peer_rows.reshape(N_BLK, N_GRP, N_GRP).transpose(2, 0, 1)
    live_rows = (jnp.arange(rows_peer, dtype=jnp.int32)[None, None, None, :] < tallies[..., None]).astype(jnp.float32)

    def expert(inputs):
        rows_in, chance, living, w_gate, w_up, w_down = inputs
        flat = rows_in.reshape(-1, D)
        gate = jnp.dot(flat, w_gate, preferred_element_type=jnp.float32)
        upward = jnp.dot(flat, w_up, preferred_element_type=jnp.float32)
        weighting = (chance * living).reshape(-1)
        hidden_rows = (jax.nn.silu(gate) * upward * weighting[:, None]).astype(jnp.bfloat16)
        total = jnp.dot(hidden_rows, w_down, preferred_element_type=jnp.float32)
        return total.astype(jnp.bfloat16).reshape(N_BLK, N_GRP, rows_peer, D)

    result = lax.map(expert, (tokens, chances, live_rows, gate_weight, up_weight, down_weight))
    return result.transpose(1, 0, 2, 3, 4).reshape(N_BLK * N_GRP * N_GRP * rows_peer, D)
```

```python
import jax
import jax.numpy as jnp
from jax import lax
from jax.sharding import PartitionSpec as P


def dot32(a, b):
    return jnp.dot(a, b, preferred_element_type=jnp.float32)


def local(dispatched, route_prob, peer_rows, gate_weight, up_weight, down_weight):
    groups, width = lax.axis_size("grp"), lax.axis_size("tp")
    group, place = lax.axis_index("grp"), lax.axis_index("tp")
    per_peer = dispatched.shape[0] // groups
    depth = dispatched.shape[1]

    live = jnp.arange(per_peer, dtype=jnp.int32)[None, :] < peer_rows[:, None]
    scales = jnp.where(live, route_prob.reshape(groups, per_peer), 0)
    blocks = dispatched.reshape(groups, per_peer, depth)

    rows, weights = [], []
    for step in range(groups):
        block = lax.dynamic_index_in_dim(blocks, (group + step) % groups, 0, keepdims=False)
        scale = lax.dynamic_index_in_dim(scales, (group + step) % groups, 0, keepdims=False)
        if step:
            there = [(i, (i + step) % groups) for i in range(groups)]
            block = lax.ppermute(block, "grp", there)
            scale = lax.ppermute(scale, "grp", there)
        rows.append(block)
        weights.append(scale.astype(jnp.float32))

    gate_full = lax.all_gather(gate_weight[0], "blk", axis=0, tiled=True)
    up_full = lax.all_gather(up_weight[0], "blk", axis=0, tiled=True)

    def pick(full, k):
        return lax.dynamic_slice_in_dim(full, k * depth, depth, 0)

    def hidden_of(block, scale):
        pieces = [(block, place)]
        right = left = block
        rights, lefts = {}, {}
        for step in range(1, width):
            right = lax.ppermute(right, "tp", [(i, i + 1) for i in range(step - 1, width - 1)])
            left = lax.ppermute(left, "tp", [(i + 1, i) for i in range(width - step)])
            rights[step], lefts[step] = right, left
        for step in range(1, width):
            other = width - step
            if step <= other:
                if step == other:
                    pieces.append((jnp.where(place >= step, rights[step], lefts[step]), (place - step) % width))
                else:
                    pieces.append((rights[step], (place - step) % width))
                    pieces.append((lefts[step], (place + step) % width))
            else:
                took = jnp.where(place >= step, rights[step], lefts[step])
                pieces.append((took, jnp.where(place >= step, place - step, (place + step) % width)))
        gate = sum(dot32(x, pick(gate_full, k)) for x, k in pieces)
        up = sum(dot32(x, pick(up_full, k)) for x, k in pieces)
        return (jax.nn.silu(gate) * up * scale[:, None]).astype(jnp.bfloat16)

    outs = []
    for block, scale in zip(rows, weights):
        hidden = hidden_of(block, scale)
        hid = hidden.shape[1]
        down = down_weight[0]
        total = dot32(hidden, lax.dynamic_slice_in_dim(down, place * hid, hid, 0))
        for step in range(1, width):
            came = lax.ppermute(hidden, "tp", [(i, (i + step) % width) for i in range(width)])
            total += dot32(came, lax.dynamic_slice_in_dim(down, (place - step) % width * hid, hid, 0))
        outs.append(total.astype(jnp.bfloat16))
    out = jnp.stack(outs)
    order = (group - jnp.arange(groups)) % groups
    return jnp.take(out, order, axis=0).reshape(groups * per_peer, -1)


def solution(mesh):
    return jax.shard_map(
        local,
        mesh=mesh,
        in_specs=(
            P(("blk", "grp"), "tp"),
            P(("blk", "grp")),
            P(("blk", "grp")),
            P("grp", "blk", "tp"),
            P("grp", "blk", "tp"),
            P("grp", None, "tp"),
        ),
        out_specs=P(("blk", "grp"), "tp"),
        check_vma=False,
    )
```

```python
import functools

import jax
import jax.numpy as jnp
from jax import lax
from jax.experimental import pallas as pl
from jax.experimental.pallas import tpu as pltpu
from jax.sharding import PartitionSpec as P

VMEM_LIMIT = 48 << 20


def dot32(a, b):
    return jnp.dot(a, b, preferred_element_type=jnp.float32)


def swap(x, axis, bit):
    return lax.ppermute(x, axis, [(i, i ^ bit) for i in range(lax.axis_size(axis))])


def gather_blocks(w):
    n = lax.axis_size("blk")
    have = {0: w}
    bit = n // 2
    while bit:
        for j in list(have):
            have[j ^ bit] = swap(have[j], "blk", bit)
        bit //= 2
    return [have[j] for j in range(n)]


def travel(block):
    n = lax.axis_size("tp")
    right = left = block
    pieces = [(block, None, 0)]
    for step in range(1, n):
        right = lax.ppermute(right, "tp", [(i, i + 1) for i in range(step - 1, n - 1)])
        left = lax.ppermute(left, "tp", [(i + 1, i) for i in range(n - step)])
        pieces.append((right, left, step))
    return pieces


def hidden_kernel(width, blocks, steps, *refs):
    xs = refs[: len(steps)]
    ws = refs[len(steps) : len(steps) + blocks]
    scale_ref, out_ref, panel, sems = refs[len(steps) + blocks :]
    place, mine = lax.axis_index("tp"), lax.axis_index("blk")
    depth = xs[0].shape[1]
    high, hid = ws[0].shape[0], out_ref.shape[1]

    copies = []
    for j in range(blocks):
        to = pl.ds(pl.multiple_of(jnp.bitwise_xor(mine, j) * high, high), high)
        copies.append(pltpu.make_async_copy(ws[j], panel.at[to, :], sems.at[j]))
        copies[-1].start()
    for copy in copies:
        copy.wait()

    total = jnp.zeros((out_ref.shape[0], 2 * hid), jnp.float32)
    for x_ref, (step, both) in zip(xs, steps):
        if both:
            k = jnp.where(place >= step, place - step, jnp.minimum(place + step, width - 1))
        else:
            k = jnp.clip(place + step, 0, width - 1)
        part = panel[pl.ds(pl.multiple_of(k * depth, depth), depth), :]
        total += dot32(x_ref[...], part)
    gate, up = total[:, :hid], total[:, hid:]
    out_ref[...] = (gate / (1.0 + jnp.exp(-gate)) * up * scale_ref[...]).astype(out_ref.dtype)


def hidden_rows(pieces, blocks, scale):
    width = lax.axis_size("tp")
    place = lax.axis_index("tp")
    xs, steps = [], []
    for right, left, step in pieces:
        if step == 0:
            xs.append(right)
            steps.append((0, False))
        elif 2 * step < width:
            xs += [right, left]
            steps += [(-step, False), (step, False)]
        else:
            xs.append(jnp.where(place >= step, right, left))
            steps.append((step, True))
    rows, depth = xs[0].shape
    high, double = blocks[0].shape
    hid = double // 2
    n = len(blocks)
    vmem = pl.BlockSpec(memory_space=pltpu.VMEM)
    whole = pl.BlockSpec(memory_space=pl.ANY)
    return pl.pallas_call(
        functools.partial(hidden_kernel, width, n, steps),
        out_shape=jax.ShapeDtypeStruct((rows, hid), jnp.bfloat16),
        in_specs=[vmem] * len(xs) + [whole] * n + [vmem],
        out_specs=vmem,
        scratch_shapes=[pltpu.VMEM((n * high, double), jnp.bfloat16), pltpu.SemaphoreType.DMA((n,))],
        compiler_params=pltpu.CompilerParams(vmem_limit_bytes=VMEM_LIMIT),
        cost_estimate=pl.CostEstimate(
            flops=2 * rows * depth * double * len(xs),
            bytes_accessed=2 * (n * high * double + len(xs) * rows * depth),
            transcendentals=rows * hid,
        ),
        name="hidden_rows",
    )(*xs, *blocks, scale)


def down_kernel(groups, width, *refs):
    hiddens = refs[: groups * width]
    down_ref, out_ref = refs[groups * width :]
    place, group = lax.axis_index("tp"), lax.axis_index("grp")
    rows, hid = hiddens[0].shape
    for g in range(groups):
        total = jnp.zeros((rows, out_ref.shape[1]), jnp.float32)
        for step in range(width):
            k = lax.rem(place - step + width, width)
            part = down_ref[pl.ds(pl.multiple_of(k * hid, hid), hid), :]
            total += dot32(hiddens[g * width + step][...], part)
        at = lax.rem(group - g + groups, groups) * rows
        out_ref[pl.ds(pl.multiple_of(at, rows), rows), :] = total.astype(out_ref.dtype)


def project_down(hiddens, down):
    groups, width = lax.axis_size("grp"), lax.axis_size("tp")
    rows, hid = hiddens[0].shape
    vmem = pl.BlockSpec(memory_space=pltpu.VMEM)
    return pl.pallas_call(
        functools.partial(down_kernel, groups, width),
        out_shape=jax.ShapeDtypeStruct((groups * rows, down.shape[1]), jnp.bfloat16),
        in_specs=[vmem] * (len(hiddens) + 1),
        out_specs=vmem,
        compiler_params=pltpu.CompilerParams(vmem_limit_bytes=VMEM_LIMIT),
        cost_estimate=pl.CostEstimate(
            flops=2 * groups * rows * down.shape[0] * down.shape[1],
            bytes_accessed=2 * (down.size + groups * rows * (down.shape[0] + down.shape[1])),
            transcendentals=0,
        ),
        name="project_down",
    )(*hiddens, down)


def local(dispatched, route_prob, peer_rows, gate_weight, up_weight, down_weight):
    groups, width = lax.axis_size("grp"), lax.axis_size("tp")
    group = lax.axis_index("grp")
    per_peer = dispatched.shape[0] // groups
    depth = dispatched.shape[1]

    live = jnp.arange(per_peer, dtype=jnp.int32)[None, :] < peer_rows[:, None]
    scales = jnp.where(live, route_prob.reshape(groups, per_peer), 0)
    tokens = dispatched.reshape(groups, per_peer, depth)

    rows, weights = [], []
    for step in range(groups):
        block = lax.dynamic_index_in_dim(tokens, (group + step) % groups, 0, keepdims=False)
        scale = lax.dynamic_index_in_dim(scales, (group + step) % groups, 0, keepdims=False)
        if step:
            there = [(i, (i + step) % groups) for i in range(groups)]
            block = lax.ppermute(block, "grp", there)
            scale = lax.ppermute(scale, "grp", there)
        rows.append(block)
        weights.append(scale.astype(jnp.float32)[:, None])

    blocks = gather_blocks(jnp.concatenate([gate_weight[0], up_weight[0]], axis=1))
    hiddens = []
    for block, scale in zip(rows, weights):
        hidden = hidden_rows(travel(block), blocks, scale)
        hiddens.append(hidden)
        for step in range(1, width):
            hiddens.append(lax.ppermute(hidden, "tp", [(i, (i + step) % width) for i in range(width)]))
    return project_down(hiddens, down_weight[0])


def solution(mesh):
    return jax.shard_map(
        local,
        mesh=mesh,
        in_specs=(
            P(("blk", "grp"), "tp"),
            P(("blk", "grp")),
            P(("blk", "grp")),
            P("grp", "blk", "tp"),
            P("grp", "blk", "tp"),
            P("grp", None, "tp"),
        ),
        out_specs=P(("blk", "grp"), "tp"),
        check_vma=False,
    )
```

```python
import functools

import jax
import jax.numpy as jnp
from jax import lax
from jax.experimental import pallas as pl
from jax.experimental.pallas import tpu as pltpu
from jax.sharding import PartitionSpec as P

PARAMS = pltpu.CompilerParams(vmem_limit_bytes=16 << 20)
VMEM = pl.BlockSpec(memory_space=pltpu.VMEM)
WHOLE = pl.BlockSpec(memory_space=pl.ANY)
FAR = pl.BlockSpec(memory_space=pltpu.HBM)
DMA = pltpu.SemaphoreType.DMA


def cost(flops, values, exps=0):
    return pl.CostEstimate(flops=flops, bytes_accessed=2 * values, transcendentals=exps)


def rows_at(index, size):
    return pl.ds(pl.multiple_of(index * size, size), size)


def after(x, *done):
    return lax.optimization_barrier((x, *done))[0]


def prepare_kernel(groups, tokens, gate, up, *refs):
    outs, panel, sems = refs[:groups], refs[groups], refs[groups + 1]
    group = lax.axis_index("grp")
    rows, hid = outs[0].shape[0], gate.shape[0]
    copies = []
    for step, out in enumerate(outs):
        source = tokens.at[rows_at(lax.rem(group + step, groups), rows), :]
        copies.append(pltpu.make_async_copy(source, out, sems.at[step]))
    copies.append(pltpu.make_async_copy(gate, panel.at[:hid, :], sems.at[groups]))
    copies.append(pltpu.make_async_copy(up, panel.at[hid:, :], sems.at[groups + 1]))
    for copy in copies:
        copy.start()
    for copy in copies:
        copy.wait()


def prepare(tokens, gate, up, groups):
    rows, depth = tokens.shape
    hid, high = gate.shape
    *split, panel = pl.pallas_call(
        functools.partial(prepare_kernel, groups),
        out_shape=[jax.ShapeDtypeStruct((rows // groups, depth), tokens.dtype)] * groups
        + [jax.ShapeDtypeStruct((2 * hid, high), gate.dtype)],
        in_specs=[FAR] * 3,
        out_specs=[VMEM] * (groups + 1),
        scratch_shapes=[DMA((groups + 2,))],
        compiler_params=PARAMS,
        cost_estimate=cost(0, 2 * rows * depth + 4 * high * hid),
        name="prepare",
    )(tokens, gate, up)
    return split, panel


def order_kernel(*refs):
    blocks, panel, sems = refs[:-2], refs[-2], refs[-1]
    mine = lax.axis_index("blk")
    copies = []
    for j, block in enumerate(blocks):
        to = panel.at[jnp.bitwise_xor(mine, j)]
        copies.append(pltpu.make_async_copy(block, to, sems.at[j]))
        copies[-1].start()
    for copy in copies:
        copy.wait()


def in_order(blocks):
    n = len(blocks)
    return pl.pallas_call(
        order_kernel,
        out_shape=jax.ShapeDtypeStruct((n, *blocks[0].shape), blocks[0].dtype),
        in_specs=[VMEM] * n,
        out_specs=VMEM,
        scratch_shapes=[DMA((n,))],
        compiler_params=PARAMS,
        cost_estimate=cost(0, 2 * n * blocks[0].size),
        name="weights_in_order",
    )(*blocks)


def swap(x, axis, bit):
    return lax.ppermute(x, axis, [(i, i ^ bit) for i in range(lax.axis_size(axis))])


def hop(block):
    right = lax.ppermute(block, "tp", [(0, 1), (1, 2), (2, 3)])
    left = lax.ppermute(block, "tp", [(1, 0), (2, 1), (3, 2)])
    return right, left


def middle(here, right, left):
    place = lax.axis_index("tp")
    inner = jnp.where(place == 2, right, left)
    block = jnp.where(jnp.logical_or(place == 0, place == 3), here, inner)
    return lax.ppermute(block, "tp", [(0, 2), (3, 1), (2, 3), (1, 0)])


def outward(block):
    return lax.ppermute(block, "tp", [(2, 3), (1, 0)])


def product(panel, chunk, k):
    depth, high = chunk.shape[1], panel.shape[2]
    total = 0
    for i in range(depth // high):
        part = chunk[:, i * high : (i + 1) * high]
        total += lax.dot_general(
            panel[k * (depth // high) + i], part, (((1,), (1,)), ((), ())), preferred_element_type=jnp.float32
        )
    return total


def partial_sum(place, panel, x, right, left, opposite):
    first = place == 0
    total = product(panel, x[...], place)
    total += product(panel, jnp.where(first, left[...], right[...]), jnp.where(first, 1, place - 1))
    return total + product(panel, opposite[...], lax.rem(place + 2, 4))


def finish(place, panel, total, left, passed, scale):
    end = jnp.logical_or(place == 0, place == 3)
    k = jnp.where(place == 0, 3, lax.rem(place + 1, 4))
    total += product(panel, jnp.where(end, passed[...], left[...]), k)
    hid = total.shape[0] // 2
    gate, up = total[:hid], total[hid:]
    return gate / (1.0 + jnp.exp(-gate)) * up * scale[...]


def sum_kernel(panel, x, right, left, opposite, out):
    out[...] = partial_sum(lax.axis_index("tp"), panel, x, right, left, opposite)


def finish_kernel(panel, total, left, passed, scale, out):
    place = lax.axis_index("tp")
    out[...] = finish(place, panel, total[...], left, passed, scale).astype(out.dtype)


def hidden_kernel(panel, x, right, left, opposite, passed, scale, out):
    place = lax.axis_index("tp")
    total = partial_sum(place, panel, x, right, left, opposite)
    out[...] = finish(place, panel, total, left, passed, scale).astype(out.dtype)


def call_rows(kernel, chunks, name, out, panel, *operands):
    share = chunks * panel.size // 4
    return pl.pallas_call(
        kernel,
        out_shape=out,
        in_specs=[VMEM] * (1 + len(operands)),
        out_specs=VMEM,
        compiler_params=PARAMS,
        cost_estimate=cost(2 * out.shape[1] * share, share),
        name=name,
    )(panel, *operands)


def down_kernel(step, groups, *refs):
    hiddens = refs[:4]
    down, out, together, rows_here, sem = refs[-5:]
    place, group = lax.axis_index("tp"), lax.axis_index("grp")
    hid, rows = hiddens[0].shape
    for s, hidden in enumerate(hiddens):
        together[rows_at(lax.rem(place - s + 4, 4), hid), :] = hidden[...]
    total = lax.dot_general(
        together[...], down[...], (((0,), (0,)), ((), ())), preferred_element_type=jnp.float32
    )
    rows_here[...] = total.astype(rows_here.dtype)
    to = out.at[rows_at(lax.rem(group - step + groups, groups), rows), :]
    copy = pltpu.make_async_copy(rows_here, to, sem)
    copy.start()
    copy.wait()


def project_down(step, groups, hiddens, down, out):
    hid, rows = hiddens[0].shape
    wide = down.shape[1]
    earlier = [] if out is None else [out]
    return pl.pallas_call(
        functools.partial(down_kernel, step, groups),
        out_shape=jax.ShapeDtypeStruct((groups * rows, wide), jnp.bfloat16),
        in_specs=[VMEM] * 4 + [WHOLE] * len(earlier) + [VMEM],
        out_specs=WHOLE,
        scratch_shapes=[pltpu.VMEM((4 * hid, rows), jnp.bfloat16), pltpu.VMEM((rows, wide), jnp.bfloat16), DMA],
        input_output_aliases={4: 0} if earlier else {},
        compiler_params=PARAMS,
        cost_estimate=cost(2 * rows * down.size, down.size + rows * wide),
        name="project_down",
    )(*hiddens, *earlier, down)


def everywhere(hidden):
    return [hidden] + [lax.ppermute(hidden, "tp", [(i, (i + s) % 4) for i in range(4)]) for s in (1, 2, 3)]


def local(dispatched, route_prob, peer_rows, gate_weight, up_weight, down_weight):
    groups, blks = lax.axis_size("grp"), lax.axis_size("blk")
    group = lax.axis_index("grp")
    per_peer = dispatched.shape[0] // groups
    hid = gate_weight.shape[2]
    turns = [[(i, (i + step) % groups) for i in range(groups)] for step in range(groups)]

    rows, weight = prepare(dispatched, gate_weight[0].T, up_weight[0].T, groups)
    hops = [hop(rows[0])]
    for step in range(1, groups):
        rows[step] = lax.ppermute(rows[step], "grp", turns[step])
        hops.append(hop(rows[step]))

    live = jnp.arange(per_peer, dtype=jnp.int32)[None, :] < peer_rows[:, None]
    scales = jnp.where(live, route_prob.reshape(groups, per_peer), 0)
    weights = []
    for step in range(groups):
        scale = lax.dynamic_index_in_dim(scales, (group + step) % groups, 0)
        if step:
            scale = lax.ppermute(after(scale, *hops[0]), "grp", turns[step])
        weights.append(scale.astype(jnp.float32))

    spread = []
    for x, (right, left), scale in zip(rows, hops, weights):
        opposite = middle(x, right, left)
        spread.append((opposite, outward(after(opposite, scale))))

    have = {0: weight}
    bit = blks // 2
    while bit:
        for j in list(have):
            have[j ^ bit] = swap(have[j], "blk", bit)
        if bit == blks // 2:
            have[bit] = after(have[bit], *hops[-1])
        bit //= 2
    panel = in_order([have[j] for j in range(blks)])

    sums = jax.ShapeDtypeStruct((2 * hid, per_peer), jnp.float32)
    hidden = jax.ShapeDtypeStruct((hid, per_peer), jnp.bfloat16)
    out = None
    for step in range(groups):
        x, (right, left), (opposite, passed), scale = rows[step], hops[step], spread[step], weights[step]
        if step < groups - 1:
            done = call_rows(hidden_kernel, 4, "hidden_rows", hidden, panel, x, right, left, opposite, passed, scale)
        else:
            total = call_rows(sum_kernel, 3, "chunk_sums", sums, panel, x, right, left, opposite)
            done = call_rows(finish_kernel, 1, "last_chunk", hidden, panel, total, left, passed, scale)
        out = project_down(step, groups, everywhere(done), down_weight[0], out)
    return out


def solution(mesh):
    return jax.shard_map(
        local,
        mesh=mesh,
        in_specs=(
            P(("blk", "grp"), "tp"),
            P(("blk", "grp")),
            P(("blk", "grp")),
            P("grp", "blk", "tp"),
            P("grp", "blk", "tp"),
            P("grp", None, "tp"),
        ),
        out_specs=P(("blk", "grp"), "tp"),
        check_vma=False,
    )
```

```python
import functools

import jax
import jax.numpy as jnp
from jax import lax
from jax.experimental import pallas as pl
from jax.experimental.pallas import tpu as pltpu
from jax.sharding import PartitionSpec as P

PARAMS = pltpu.CompilerParams(vmem_limit_bytes=16 << 20)
VMEM = pl.BlockSpec(memory_space=pltpu.VMEM)
WHOLE = pl.BlockSpec(memory_space=pl.ANY)
DMA = pltpu.SemaphoreType.DMA


def cost(flops, values, exps=0):
    return pl.CostEstimate(flops=flops, bytes_accessed=2 * values, transcendentals=exps)


def rows_at(index, size):
    return pl.ds(pl.multiple_of(index * size, size), size)


def after(x, *done):
    return lax.optimization_barrier((x, *done))[0]


def copy_all(pairs, sems):
    copies = [pltpu.make_async_copy(source, to, sems.at[i]) for i, (source, to) in enumerate(pairs)]
    for copy in copies:
        copy.start()
    for copy in copies:
        copy.wait()


def split_kernel(tokens, *refs):
    outs, sems = refs[:-1], refs[-1]
    group, groups = lax.axis_index("grp"), len(outs)
    rows = outs[0].shape[0]
    sources = [tokens.at[rows_at(lax.rem(group + step, groups), rows), :] for step in range(groups)]
    copy_all(zip(sources, outs), sems)


def split_rows(tokens, groups):
    rows, depth = tokens.shape
    return pl.pallas_call(
        split_kernel,
        out_shape=[jax.ShapeDtypeStruct((rows // groups, depth), tokens.dtype)] * groups,
        in_specs=[WHOLE],
        out_specs=[VMEM] * groups,
        scratch_shapes=[DMA((groups,))],
        compiler_params=PARAMS,
        cost_estimate=cost(0, 2 * rows * depth),
        name="split_rows",
    )(pltpu.with_memory_space_constraint(tokens, pltpu.HBM))


def stack_kernel(gate, up, out, sems):
    hid = gate.shape[0]
    copy_all([(gate, out.at[:hid, :]), (up, out.at[hid:, :])], sems)


def stack(gate, up):
    hid, high = gate.shape
    return pl.pallas_call(
        stack_kernel,
        out_shape=jax.ShapeDtypeStruct((2 * hid, high), gate.dtype),
        in_specs=[WHOLE] * 2,
        out_specs=VMEM,
        scratch_shapes=[DMA((2,))],
        compiler_params=PARAMS,
        cost_estimate=cost(0, 4 * high * hid),
        name="gate_above_up",
    )(pltpu.with_memory_space_constraint(gate, pltpu.HBM), pltpu.with_memory_space_constraint(up, pltpu.HBM))


def order_kernel(*refs):
    blocks, panel, sems = refs[:-2], refs[-2], refs[-1]
    mine = lax.axis_index("blk")
    copy_all([(block, panel.at[jnp.bitwise_xor(mine, j)]) for j, block in enumerate(blocks)], sems)


def in_order(blocks):
    n = len(blocks)
    return pl.pallas_call(
        order_kernel,
        out_shape=jax.ShapeDtypeStruct((n, *blocks[0].shape), blocks[0].dtype),
        in_specs=[VMEM] * n,
        out_specs=VMEM,
        scratch_shapes=[DMA((n,))],
        compiler_params=PARAMS,
        cost_estimate=cost(0, 2 * n * blocks[0].size),
        name="weights_in_order",
    )(*blocks)


def swap(x, axis, bit):
    return lax.ppermute(x, axis, [(i, i ^ bit) for i in range(lax.axis_size(axis))])


def hop(block):
    right = lax.ppermute(block, "tp", [(0, 1), (1, 2), (2, 3)])
    left = lax.ppermute(block, "tp", [(1, 0), (2, 1), (3, 2)])
    return right, left


def middle(here, right, left):
    place = lax.axis_index("tp")
    inner = jnp.where(place == 2, right, left)
    block = jnp.where(jnp.logical_or(place == 0, place == 3), here, inner)
    return lax.ppermute(block, "tp", [(0, 2), (3, 1), (2, 3), (1, 0)])


def outward(block):
    return lax.ppermute(block, "tp", [(2, 3), (1, 0)])


def product(panel, chunk, k):
    depth, high = chunk.shape[1], panel.shape[2]
    total = 0
    for i in range(depth // high):
        part = chunk[:, i * high : (i + 1) * high]
        total += lax.dot_general(
            panel[k * (depth // high) + i], part, (((1,), (1,)), ((), ())), preferred_element_type=jnp.float32
        )
    return total


def partial_sum(place, panel, x, right, left, opposite):
    first = place == 0
    total = product(panel, x[...], place)
    total += product(panel, jnp.where(first, left[...], right[...]), jnp.where(first, 1, place - 1))
    return total + product(panel, opposite[...], lax.rem(place + 2, 4))


def finish(place, panel, total, left, passed, scale):
    end = jnp.logical_or(place == 0, place == 3)
    k = jnp.where(place == 0, 3, lax.rem(place + 1, 4))
    total += product(panel, jnp.where(end, passed[...], left[...]), k)
    hid = total.shape[0] // 2
    gate, up = total[:hid], total[hid:]
    return gate / (1.0 + jnp.exp(-gate)) * up * scale[...]


def sum_kernel(panel, x, right, left, opposite, out):
    out[...] = partial_sum(lax.axis_index("tp"), panel, x, right, left, opposite)


def finish_kernel(panel, total, left, passed, scale, out):
    place = lax.axis_index("tp")
    out[...] = finish(place, panel, total[...], left, passed, scale).astype(out.dtype)


def hidden_kernel(panel, x, right, left, opposite, passed, scale, out):
    place = lax.axis_index("tp")
    total = partial_sum(place, panel, x, right, left, opposite)
    out[...] = finish(place, panel, total, left, passed, scale).astype(out.dtype)


def call_rows(kernel, chunks, name, out, panel, *operands):
    share = chunks * panel.size // 4
    return pl.pallas_call(
        kernel,
        out_shape=out,
        in_specs=[VMEM] * (1 + len(operands)),
        out_specs=VMEM,
        compiler_params=PARAMS,
        cost_estimate=cost(2 * out.shape[1] * share, share),
        name=name,
    )(panel, *operands)


def down_kernel(step, groups, *refs):
    hiddens = refs[:4]
    down, out, together, rows_here, sem = refs[-5:]
    place, group = lax.axis_index("tp"), lax.axis_index("grp")
    hid, rows = hiddens[0].shape
    for s, hidden in enumerate(hiddens):
        together[rows_at(lax.rem(place - s + 4, 4), hid), :] = hidden[...]
    total = lax.dot_general(
        together[...], down[...], (((0,), (0,)), ((), ())), preferred_element_type=jnp.float32
    )
    rows_here[...] = total.astype(rows_here.dtype)
    to = out.at[rows_at(lax.rem(group - step + groups, groups), rows), :]
    copy = pltpu.make_async_copy(rows_here, to, sem)
    copy.start()
    copy.wait()


def project_down(step, groups, hiddens, down, out):
    hid, rows = hiddens[0].shape
    wide = down.shape[1]
    earlier = [] if out is None else [out]
    return pl.pallas_call(
        functools.partial(down_kernel, step, groups),
        out_shape=jax.ShapeDtypeStruct((groups * rows, wide), jnp.bfloat16),
        in_specs=[VMEM] * 4 + [WHOLE] * len(earlier) + [VMEM],
        out_specs=WHOLE,
        scratch_shapes=[pltpu.VMEM((4 * hid, rows), jnp.bfloat16), pltpu.VMEM((rows, wide), jnp.bfloat16), DMA],
        input_output_aliases={4: 0} if earlier else {},
        compiler_params=PARAMS,
        cost_estimate=cost(2 * rows * down.size, down.size + rows * wide),
        name="project_down",
    )(*hiddens, *earlier, down)


def everywhere(hidden):
    return [hidden] + [lax.ppermute(hidden, "tp", [(i, (i + s) % 4) for i in range(4)]) for s in (1, 2, 3)]


def local(dispatched, route_prob, peer_rows, gate_weight, up_weight, down_weight):
    groups, blks = lax.axis_size("grp"), lax.axis_size("blk")
    group = lax.axis_index("grp")
    per_peer = dispatched.shape[0] // groups
    hid = gate_weight.shape[2]
    turns = [[(i, (i + step) % groups) for i in range(groups)] for step in range(groups)]

    rows = list(split_rows(dispatched, groups))
    hops = [hop(rows[0])]
    for step in range(1, groups):
        rows[step] = lax.ppermute(rows[step], "grp", turns[step])
        hops.append(hop(rows[step]))

    spread = []
    for x, (right, left), later in zip(rows, hops, hops[1:] + [()]):
        opposite = middle(after(x, *[done for done, _ in spread]), right, left)
        spread.append((opposite, outward(after(opposite, *later))))

    live = jnp.arange(per_peer, dtype=jnp.int32)[None, :] < peer_rows[:, None]
    scales = jnp.where(live, route_prob.reshape(groups, per_peer), 0)
    weights = []
    for step in range(groups):
        scale = lax.dynamic_index_in_dim(scales, (group + step) % groups, 0)
        if step:
            scale = lax.ppermute(after(scale, spread[-1][0]), "grp", turns[step])
        weights.append(scale.astype(jnp.float32))

    have = {0: stack(*after((gate_weight[0].T, up_weight[0].T), *hops[0]))}
    bit = blks // 2
    while bit:
        for j in list(have):
            have[j ^ bit] = swap(have[j], "blk", bit)
        if bit == blks // 2:
            have[bit] = after(have[bit], spread[0][1], spread[-1][0])
        bit //= 2
    panel = in_order([after(have[0], *weights)] + [have[j] for j in range(1, blks)])

    sums = jax.ShapeDtypeStruct((2 * hid, per_peer), jnp.float32)
    hidden = jax.ShapeDtypeStruct((hid, per_peer), jnp.bfloat16)
    out = None
    for step in range(groups):
        x, (right, left), (opposite, passed), scale = rows[step], hops[step], spread[step], weights[step]
        if step < groups - 1:
            done = call_rows(hidden_kernel, 4, "hidden_rows", hidden, panel, x, right, left, opposite, passed, scale)
        else:
            total = call_rows(sum_kernel, 3, "chunk_sums", sums, panel, x, right, left, opposite)
            done = call_rows(finish_kernel, 1, "last_chunk", hidden, panel, total, left, passed, scale)
        out = project_down(step, groups, everywhere(done), down_weight[0], out)
    return out


def solution(mesh):
    return jax.shard_map(
        local,
        mesh=mesh,
        in_specs=(
            P(("blk", "grp"), "tp"),
            P(("blk", "grp")),
            P(("blk", "grp")),
            P("grp", "blk", "tp"),
            P("grp", "blk", "tp"),
            P("grp", None, "tp"),
        ),
        out_specs=P(("blk", "grp"), "tp"),
        check_vma=False,
    )
```

```python
import functools

import jax
import jax.numpy as jnp
from jax import lax
from jax.experimental import pallas as pl
from jax.experimental.pallas import tpu as pltpu
from jax.sharding import PartitionSpec as P

PARAMS = pltpu.CompilerParams(vmem_limit_bytes=16 << 20)
VMEM = pl.BlockSpec(memory_space=pltpu.VMEM)
WHOLE = pl.BlockSpec(memory_space=pl.ANY)
DMA = pltpu.SemaphoreType.DMA


def cost(flops, values, exps=0):
    return pl.CostEstimate(flops=flops, bytes_accessed=2 * values, transcendentals=exps)


def rows_at(index, size):
    return pl.ds(pl.multiple_of(index * size, size), size)


def after(x, *done):
    return lax.optimization_barrier((x, *done))[0]


def copy_all(pairs, sems):
    copies = [pltpu.make_async_copy(source, to, sems.at[i]) for i, (source, to) in enumerate(pairs)]
    for copy in copies:
        copy.start()
    for copy in copies:
        copy.wait()


def prepare_kernel(groups, tokens, gate, up, *refs):
    outs, panel, sems = refs[:groups], refs[groups], refs[groups + 1]
    group = lax.axis_index("grp")
    rows, hid = outs[0].shape[0], gate.shape[0]
    pairs = [(tokens.at[rows_at(lax.rem(group + step, groups), rows), :], out) for step, out in enumerate(outs)]
    copy_all(pairs + [(gate, panel.at[:hid, :]), (up, panel.at[hid:, :])], sems)


def prepare(tokens, gate, up, groups):
    rows, depth = tokens.shape
    hid, high = gate.shape
    *split, panel = pl.pallas_call(
        functools.partial(prepare_kernel, groups),
        out_shape=[jax.ShapeDtypeStruct((rows // groups, depth), tokens.dtype)] * groups
        + [jax.ShapeDtypeStruct((2 * hid, high), gate.dtype)],
        in_specs=[WHOLE] * 3,
        out_specs=[VMEM] * (groups + 1),
        scratch_shapes=[DMA((groups + 2,))],
        compiler_params=PARAMS,
        cost_estimate=cost(0, 2 * rows * depth + 4 * high * hid),
        name="prepare",
    )(*(pltpu.with_memory_space_constraint(x, pltpu.HBM) for x in (tokens, gate, up)))
    return split, panel


def order_kernel(*refs):
    blocks, panel, sems = refs[:-2], refs[-2], refs[-1]
    mine = lax.axis_index("blk")
    copy_all([(block, panel.at[jnp.bitwise_xor(mine, j)]) for j, block in enumerate(blocks)], sems)


def in_order(blocks):
    n = len(blocks)
    return pl.pallas_call(
        order_kernel,
        out_shape=jax.ShapeDtypeStruct((n, *blocks[0].shape), blocks[0].dtype),
        in_specs=[VMEM] * n,
        out_specs=VMEM,
        scratch_shapes=[DMA((n,))],
        compiler_params=PARAMS,
        cost_estimate=cost(0, 2 * n * blocks[0].size),
        name="weights_in_order",
    )(*blocks)


def swap(x, axis, bit):
    return lax.ppermute(x, axis, [(i, i ^ bit) for i in range(lax.axis_size(axis))])


def hop(block):
    right = lax.ppermute(block, "tp", [(0, 1), (1, 2), (2, 3)])
    left = lax.ppermute(block, "tp", [(1, 0), (2, 1), (3, 2)])
    return right, left


def middle(here, right, left):
    place = lax.axis_index("tp")
    inner = jnp.where(place == 2, right, left)
    block = jnp.where(jnp.logical_or(place == 0, place == 3), here, inner)
    return lax.ppermute(block, "tp", [(0, 2), (3, 1), (2, 3), (1, 0)])


def outward(block):
    return lax.ppermute(block, "tp", [(2, 3), (1, 0)])


def product(panel, chunk, k):
    depth, high = chunk.shape[1], panel.shape[2]
    total = 0
    for i in range(depth // high):
        part = chunk[:, i * high : (i + 1) * high]
        total += lax.dot_general(
            panel[k * (depth // high) + i], part, (((1,), (1,)), ((), ())), preferred_element_type=jnp.float32
        )
    return total


def partial_sum(place, panel, x, right, left, opposite):
    first = place == 0
    total = product(panel, x[...], place)
    total += product(panel, jnp.where(first, left[...], right[...]), jnp.where(first, 1, place - 1))
    return total + product(panel, opposite[...], lax.rem(place + 2, 4))


def finish(place, panel, total, left, passed, scale):
    end = jnp.logical_or(place == 0, place == 3)
    k = jnp.where(place == 0, 3, lax.rem(place + 1, 4))
    total += product(panel, jnp.where(end, passed[...], left[...]), k)
    hid = total.shape[0] // 2
    gate, up = total[:hid], total[hid:]
    return gate / (1.0 + jnp.exp(-gate)) * up * scale[...]


def sum_kernel(panel, x, right, left, opposite, out):
    out[...] = partial_sum(lax.axis_index("tp"), panel, x, right, left, opposite)


def finish_kernel(panel, total, left, passed, scale, out):
    place = lax.axis_index("tp")
    out[...] = finish(place, panel, total[...], left, passed, scale).astype(out.dtype)


def hidden_kernel(panel, x, right, left, opposite, passed, scale, out):
    place = lax.axis_index("tp")
    total = partial_sum(place, panel, x, right, left, opposite)
    out[...] = finish(place, panel, total, left, passed, scale).astype(out.dtype)


def call_rows(kernel, chunks, name, out, panel, *operands):
    share = chunks * panel.size // 4
    return pl.pallas_call(
        kernel,
        out_shape=out,
        in_specs=[VMEM] * (1 + len(operands)),
        out_specs=VMEM,
        compiler_params=PARAMS,
        cost_estimate=cost(2 * out.shape[1] * share, share),
        name=name,
    )(panel, *operands)


def down_kernel(step, groups, *refs):
    hiddens = refs[:4]
    down, out, together, rows_here, sem = refs[-5:]
    place, group = lax.axis_index("tp"), lax.axis_index("grp")
    hid, rows = hiddens[0].shape
    for s, hidden in enumerate(hiddens):
        together[rows_at(lax.rem(place - s + 4, 4), hid), :] = hidden[...]
    total = lax.dot_general(
        together[...], down[...], (((0,), (0,)), ((), ())), preferred_element_type=jnp.float32
    )
    rows_here[...] = total.astype(rows_here.dtype)
    to = out.at[rows_at(lax.rem(group - step + groups, groups), rows), :]
    copy = pltpu.make_async_copy(rows_here, to, sem)
    copy.start()
    copy.wait()


def project_down(step, groups, hiddens, down, out):
    hid, rows = hiddens[0].shape
    wide = down.shape[1]
    earlier = [] if out is None else [out]
    return pl.pallas_call(
        functools.partial(down_kernel, step, groups),
        out_shape=jax.ShapeDtypeStruct((groups * rows, wide), jnp.bfloat16),
        in_specs=[VMEM] * 4 + [WHOLE] * len(earlier) + [VMEM],
        out_specs=WHOLE,
        scratch_shapes=[pltpu.VMEM((4 * hid, rows), jnp.bfloat16), pltpu.VMEM((rows, wide), jnp.bfloat16), DMA],
        input_output_aliases={4: 0} if earlier else {},
        compiler_params=PARAMS,
        cost_estimate=cost(2 * rows * down.size, down.size + rows * wide),
        name="project_down",
    )(*hiddens, *earlier, down)


def everywhere(hidden):
    return [hidden] + [lax.ppermute(hidden, "tp", [(i, (i + s) % 4) for i in range(4)]) for s in (1, 2, 3)]


def local(dispatched, route_prob, peer_rows, gate_weight, up_weight, down_weight):
    groups, blks = lax.axis_size("grp"), lax.axis_size("blk")
    group = lax.axis_index("grp")
    per_peer = dispatched.shape[0] // groups
    hid = gate_weight.shape[2]
    turns = [[(i, (i + step) % groups) for i in range(groups)] for step in range(groups)]

    rows, weight = prepare(dispatched, gate_weight[0].T, up_weight[0].T, groups)
    spread = []
    for step in range(groups):
        if step:
            rows[step] = lax.ppermute(rows[step], "grp", turns[step])
        right, left = hop(rows[step])
        opposite = middle(rows[step], right, left)
        spread.append((right, left, opposite, outward(opposite)))

    live = jnp.arange(per_peer, dtype=jnp.int32)[None, :] < peer_rows[:, None]
    scales = jnp.where(live, route_prob.reshape(groups, per_peer), 0)
    weights = []
    for step in range(groups):
        scale = lax.dynamic_index_in_dim(scales, (group + step) % groups, 0)
        if step:
            scale = lax.ppermute(after(scale, spread[-1][2]), "grp", turns[step])
        weights.append(scale.astype(jnp.float32))

    have = {0: weight}
    bit = blks // 2
    while bit:
        for j in list(have):
            have[j ^ bit] = swap(have[j], "blk", bit)
        if bit == blks // 2:
            have[bit] = after(have[bit], *spread[-1][:2])
        bit //= 2
    panel = in_order([after(have[0], *weights)] + [have[j] for j in range(1, blks)])

    sums = jax.ShapeDtypeStruct((2 * hid, per_peer), jnp.float32)
    hidden = jax.ShapeDtypeStruct((hid, per_peer), jnp.bfloat16)
    out = None
    for step in range(groups):
        x, (right, left, opposite, passed), scale = rows[step], spread[step], weights[step]
        if step < groups - 1:
            done = call_rows(hidden_kernel, 4, "hidden_rows", hidden, panel, x, right, left, opposite, passed, scale)
        else:
            total = call_rows(sum_kernel, 3, "chunk_sums", sums, panel, x, right, left, opposite)
            done = call_rows(finish_kernel, 1, "last_chunk", hidden, panel, total, left, passed, scale)
        out = project_down(step, groups, everywhere(done), down_weight[0], out)
    return out


def solution(mesh):
    return jax.shard_map(
        local,
        mesh=mesh,
        in_specs=(
            P(("blk", "grp"), "tp"),
            P(("blk", "grp")),
            P(("blk", "grp")),
            P("grp", "blk", "tp"),
            P("grp", "blk", "tp"),
            P("grp", None, "tp"),
        ),
        out_specs=P(("blk", "grp"), "tp"),
        check_vma=False,
    )
```

```python
import functools

import jax
import jax.numpy as jnp
from jax import lax
from jax.experimental import pallas as pl
from jax.experimental.pallas import tpu as pltpu
from jax.sharding import PartitionSpec as P

PARAMS = pltpu.CompilerParams(vmem_limit_bytes=16 << 20)
VMEM = pl.BlockSpec(memory_space=pltpu.VMEM)
WHOLE = pl.BlockSpec(memory_space=pl.ANY)
DMA = pltpu.SemaphoreType.DMA
EXTRA = 16


def cost(flops, values, exps=0):
    return pl.CostEstimate(flops=flops, bytes_accessed=2 * values, transcendentals=exps)


def rows_at(index, size):
    return pl.ds(pl.multiple_of(index * size, size), size)


def after(x, *done):
    return lax.optimization_barrier((x, *done))[0]


def copy_all(pairs, sems):
    copies = [pltpu.make_async_copy(source, to, sems.at[i]) for i, (source, to) in enumerate(pairs)]
    for copy in copies:
        copy.start()
    for copy in copies:
        copy.wait()


def prepare_kernel(groups, tokens, gate, up, *refs):
    outs, panel, sems = refs[:groups], refs[groups], refs[groups + 1]
    group = lax.axis_index("grp")
    rows, hid = outs[0].shape[0], gate.shape[0]
    pairs = [(tokens.at[rows_at(lax.rem(group + step, groups), rows), :], out) for step, out in enumerate(outs)]
    copy_all(pairs + [(gate, panel.at[:hid, :]), (up, panel.at[hid:, :])], sems)


def prepare(tokens, gate, up, groups):
    rows, depth = tokens.shape
    hid, high = gate.shape
    *split, panel = pl.pallas_call(
        functools.partial(prepare_kernel, groups),
        out_shape=[jax.ShapeDtypeStruct((rows // groups, depth), tokens.dtype)] * groups
        + [jax.ShapeDtypeStruct((2 * hid, high), gate.dtype)],
        in_specs=[WHOLE] * 3,
        out_specs=[VMEM] * (groups + 1),
        scratch_shapes=[DMA((groups + 2,))],
        compiler_params=PARAMS,
        cost_estimate=cost(0, 2 * rows * depth + 4 * high * hid),
        name="prepare",
    )(*(pltpu.with_memory_space_constraint(x, pltpu.HBM) for x in (tokens, gate, up)))
    return split, panel


def attach_kernel(step, tokens, scales, out, sem):
    rows = tokens.shape[0] // scales.shape[0]
    index = lax.rem(lax.axis_index("grp") + step, scales.shape[0])
    copy = pltpu.make_async_copy(tokens.at[rows_at(index, rows), :], out.at[:rows, :], sem)
    copy.start()
    scale = scales[pl.ds(index, 1), :].astype(out.dtype)
    lanes = out.shape[1]
    line = jnp.concatenate([scale, jnp.zeros((1, lanes - rows), out.dtype)], axis=1)
    out[rows:, :] = jnp.broadcast_to(line, (EXTRA, lanes))
    copy.wait()


def attach(step, tokens, scales):
    groups, rows = scales.shape
    depth = tokens.shape[1]
    return pl.pallas_call(
        functools.partial(attach_kernel, step),
        out_shape=jax.ShapeDtypeStruct((rows + EXTRA, depth), tokens.dtype),
        in_specs=[WHOLE, VMEM],
        out_specs=VMEM,
        scratch_shapes=[DMA],
        compiler_params=PARAMS,
        cost_estimate=cost(0, 2 * rows * depth),
        name="attach_weights",
    )(pltpu.with_memory_space_constraint(tokens, pltpu.HBM), scales)


def order_kernel(*refs):
    blocks, panel, sems = refs[:-2], refs[-2], refs[-1]
    mine = lax.axis_index("blk")
    copy_all([(block, panel.at[jnp.bitwise_xor(mine, j)]) for j, block in enumerate(blocks)], sems)


def in_order(blocks):
    n = len(blocks)
    return pl.pallas_call(
        order_kernel,
        out_shape=jax.ShapeDtypeStruct((n, *blocks[0].shape), blocks[0].dtype),
        in_specs=[VMEM] * n,
        out_specs=VMEM,
        scratch_shapes=[DMA((n,))],
        compiler_params=PARAMS,
        cost_estimate=cost(0, 2 * n * blocks[0].size),
        name="weights_in_order",
    )(*blocks)


def swap(x, axis, bit):
    return lax.ppermute(x, axis, [(i, i ^ bit) for i in range(lax.axis_size(axis))])


def along(step, moves, straight=()):
    groups = lax.axis_size("grp")
    pairs = []
    for g in range(groups):
        pairs += [(g * 4 + a, (g + step) % groups * 4 + b) for a, b in moves]
        pairs += [(g * 4 + a, g * 4 + b) for a, b in straight]
    return pairs


def hop(block, step):
    right = lax.ppermute(block, ("grp", "tp"), along(step, [(0, 1), (1, 2), (2, 3)]))
    left = lax.ppermute(block, ("grp", "tp"), along(step, [(1, 0), (2, 1), (3, 2)]))
    return right, left


def middle(here, right, left, step):
    place = lax.axis_index("tp")
    inner = jnp.where(place == 2, right, left)
    block = jnp.where(jnp.logical_or(place == 0, place == 3), here, inner)
    return lax.ppermute(block, ("grp", "tp"), along(step, [(0, 2), (3, 1)], [(2, 3), (1, 0)]))


def outward(block):
    return lax.ppermute(block, "tp", [(2, 3), (1, 0)])


def product(panel, chunk, k):
    depth, high = chunk.shape[1], panel.shape[2]
    total = 0
    for i in range(depth // high):
        part = chunk[:, i * high : (i + 1) * high]
        total += lax.dot_general(
            panel[k * (depth // high) + i], part, (((1,), (1,)), ((), ())), preferred_element_type=jnp.float32
        )
    return total


def sum_kernel(groups, panel, *refs):
    out = refs[-1]
    place = lax.axis_index("tp")
    first = place == 0
    rows = out.shape[1] // groups
    for step in range(groups):
        x, right, left, opposite = refs[4 * step : 4 * step + 4]
        total = product(panel, x[:rows, :], place)
        total += product(panel, jnp.where(first, left[...], right[...]), jnp.where(first, 1, place - 1))
        total += product(panel, opposite[...], lax.rem(place + 2, 4))
        out[:, step * rows : (step + 1) * rows] = total


def finish_kernel(groups, panel, totals, scale, *refs):
    out = refs[-1]
    place = lax.axis_index("tp")
    end = jnp.logical_or(place == 0, place == 3)
    k = jnp.where(place == 0, 3, lax.rem(place + 1, 4))
    hid, rows = out.shape[0], out.shape[1] // groups
    for step in range(groups):
        x, left, passed = refs[3 * step : 3 * step + 3]
        at = slice(step * rows, (step + 1) * rows)
        total = totals[:, at] + product(panel, jnp.where(end, passed[...], left[...]), k)
        gate, up = total[:hid], total[hid:]
        weight = scale[...] if step == 0 else x[rows : rows + 1, :rows].astype(jnp.float32)
        out[:, at] = (gate / (1.0 + jnp.exp(-gate)) * up * weight).astype(out.dtype)


def call_rows(kernel, chunks, name, out, panel, *operands):
    share = chunks * panel.size // 4
    return pl.pallas_call(
        functools.partial(kernel, lax.axis_size("grp")),
        out_shape=out,
        in_specs=[VMEM] * (1 + len(operands)),
        out_specs=VMEM,
        compiler_params=PARAMS,
        cost_estimate=cost(2 * out.shape[1] * share, share),
        name=name,
    )(panel, *operands)


def down_kernel(groups, *refs):
    hiddens = refs[:4]
    down, out, together, rows_here, sems = refs[4:]
    place, group = lax.axis_index("tp"), lax.axis_index("grp")
    hid, rows = hiddens[0].shape[0], hiddens[0].shape[1] // groups
    for s, hidden in enumerate(hiddens):
        together[rows_at(lax.rem(place - s + 4, 4), hid), :] = hidden[...]
    total = lax.dot_general(
        together[...], down[...], (((0,), (0,)), ((), ())), preferred_element_type=jnp.float32
    )
    rows_here[...] = total.astype(rows_here.dtype)
    pairs = []
    for step in range(groups):
        to = out.at[rows_at(lax.rem(group - step + groups, groups), rows), :]
        pairs.append((rows_here.at[step * rows : (step + 1) * rows, :], to))
    copy_all(pairs, sems)


def project_down(groups, hiddens, down):
    hid, rows = hiddens[0].shape
    wide = down.shape[1]
    return pl.pallas_call(
        functools.partial(down_kernel, groups),
        out_shape=jax.ShapeDtypeStruct((rows, wide), jnp.bfloat16),
        in_specs=[VMEM] * 5,
        out_specs=WHOLE,
        scratch_shapes=[pltpu.VMEM((4 * hid, rows), jnp.bfloat16), pltpu.VMEM((rows, wide), jnp.bfloat16), DMA((groups,))],
        compiler_params=PARAMS,
        cost_estimate=cost(2 * rows * down.size, down.size + rows * wide),
        name="project_down",
    )(*hiddens, down)


def everywhere(hidden):
    return [hidden] + [lax.ppermute(hidden, "tp", [(i, (i + s) % 4) for i in range(4)]) for s in (1, 2, 3)]


def local(dispatched, route_prob, peer_rows, gate_weight, up_weight, down_weight):
    groups, blks = lax.axis_size("grp"), lax.axis_size("blk")
    group = lax.axis_index("grp")
    per_peer = dispatched.shape[0] // groups
    hid = gate_weight.shape[2]

    rows, weight = prepare(dispatched, gate_weight[0].T, up_weight[0].T, groups)
    hops = [hop(rows[step], step) for step in range(groups)]

    spread = []
    for step, (right, left) in enumerate(hops):
        opposite = middle(rows[step], right, left, step)
        later = hops[step + 1] if step + 1 < groups else ()
        spread.append((opposite, outward(after(opposite, *later))))

    live = jnp.arange(per_peer, dtype=jnp.int32)[None, :] < peer_rows[:, None]
    scales = jnp.where(live, route_prob.reshape(groups, per_peer), 0).astype(jnp.float32)
    scale = lax.dynamic_index_in_dim(scales, group, 0)
    for step in range(1, groups):
        block = attach(step, after(dispatched, *hops[0]), scales)
        rows[step] = lax.ppermute(block, "grp", [(i, (i + step) % groups) for i in range(groups)])

    have = {0: weight}
    bit = blks // 2
    while bit:
        for j in list(have):
            have[j ^ bit] = swap(have[j], "blk", bit)
        if bit == blks // 2:
            have[bit] = after(have[bit], *hops[-1])
        bit //= 2
    panel = in_order([have[j] for j in range(blks)])

    first, last = [], []
    for x, (right, left), (opposite, passed) in zip(rows, hops, spread):
        first += [x, right, left, opposite]
        last += [x, left, passed]
    count = groups * per_peer
    sums = jax.ShapeDtypeStruct((2 * hid, count), jnp.float32)
    hidden = jax.ShapeDtypeStruct((hid, count), jnp.bfloat16)
    totals = call_rows(sum_kernel, 3, "chunk_sums", sums, panel, *first)
    done = call_rows(finish_kernel, 1, "last_chunk", hidden, panel, totals, scale, *last)
    return project_down(groups, everywhere(done), down_weight[0])


def solution(mesh):
    return jax.shard_map(
        local,
        mesh=mesh,
        in_specs=(
            P(("blk", "grp"), "tp"),
            P(("blk", "grp")),
            P(("blk", "grp")),
            P("grp", "blk", "tp"),
            P("grp", "blk", "tp"),
            P("grp", None, "tp"),
        ),
        out_specs=P(("blk", "grp"), "tp"),
        check_vma=False,
    )
```

```python
import functools

import jax
import jax.numpy as jnp
from jax import lax
from jax.experimental import pallas as pl
from jax.experimental.pallas import tpu as pltpu
from jax.sharding import PartitionSpec as P

PARAMS = pltpu.CompilerParams(vmem_limit_bytes=16 << 20)
VMEM = pl.BlockSpec(memory_space=pltpu.VMEM)
WHOLE = pl.BlockSpec(memory_space=pl.ANY)
DMA = pltpu.SemaphoreType.DMA
EXTRA = 16


def cost(flops, values, exps=0):
    return pl.CostEstimate(flops=flops, bytes_accessed=2 * values, transcendentals=exps)


def rows_at(index, size):
    return pl.ds(pl.multiple_of(index * size, size), size)


def after(x, *done):
    return lax.optimization_barrier((x, *done))[0]


def copy_all(pairs, sems):
    copies = [pltpu.make_async_copy(source, to, sems.at[i]) for i, (source, to) in enumerate(pairs)]
    for copy in copies:
        copy.start()
    for copy in copies:
        copy.wait()


def prepare_kernel(groups, tokens, gate, up, *refs):
    outs, panel, sems = refs[:groups], refs[groups], refs[groups + 1]
    group = lax.axis_index("grp")
    rows, hid = outs[0].shape[0], gate.shape[0]
    pairs = [(tokens.at[rows_at(lax.rem(group + step, groups), rows), :], out) for step, out in enumerate(outs)]
    copy_all(pairs + [(gate, panel.at[:hid, :]), (up, panel.at[hid:, :])], sems)


def prepare(tokens, gate, up, groups):
    rows, depth = tokens.shape
    hid, high = gate.shape
    *split, panel = pl.pallas_call(
        functools.partial(prepare_kernel, groups),
        out_shape=[jax.ShapeDtypeStruct((rows // groups, depth), tokens.dtype)] * groups
        + [jax.ShapeDtypeStruct((2 * hid, high), gate.dtype)],
        in_specs=[WHOLE] * 3,
        out_specs=[VMEM] * (groups + 1),
        scratch_shapes=[DMA((groups + 2,))],
        compiler_params=PARAMS,
        cost_estimate=cost(0, 2 * rows * depth + 4 * high * hid),
        name="prepare",
    )(*(pltpu.with_memory_space_constraint(x, pltpu.HBM) for x in (tokens, gate, up)))
    return split, panel


def attach_kernel(step, tokens, scales, out, sem):
    rows = tokens.shape[0] // scales.shape[0]
    index = lax.rem(lax.axis_index("grp") + step, scales.shape[0])
    copy = pltpu.make_async_copy(tokens.at[rows_at(index, rows), :], out.at[:rows, :], sem)
    copy.start()
    scale = scales[pl.ds(index, 1), :].astype(out.dtype)
    lanes = out.shape[1]
    line = jnp.concatenate([scale, jnp.zeros((1, lanes - rows), out.dtype)], axis=1)
    out[rows:, :] = jnp.broadcast_to(line, (EXTRA, lanes))
    copy.wait()


def attach(step, tokens, scales):
    groups, rows = scales.shape
    depth = tokens.shape[1]
    return pl.pallas_call(
        functools.partial(attach_kernel, step),
        out_shape=jax.ShapeDtypeStruct((rows + EXTRA, depth), tokens.dtype),
        in_specs=[WHOLE, VMEM],
        out_specs=VMEM,
        scratch_shapes=[DMA],
        compiler_params=PARAMS,
        cost_estimate=cost(0, 2 * rows * depth),
        name="attach_weights",
    )(pltpu.with_memory_space_constraint(tokens, pltpu.HBM), scales)


def order_kernel(*refs):
    blocks, panel, sems = refs[:-2], refs[-2], refs[-1]
    mine = lax.axis_index("blk")
    copy_all([(block, panel.at[jnp.bitwise_xor(mine, j)]) for j, block in enumerate(blocks)], sems)


def in_order(blocks):
    n = len(blocks)
    return pl.pallas_call(
        order_kernel,
        out_shape=jax.ShapeDtypeStruct((n, *blocks[0].shape), blocks[0].dtype),
        in_specs=[VMEM] * n,
        out_specs=VMEM,
        scratch_shapes=[DMA((n,))],
        compiler_params=PARAMS,
        cost_estimate=cost(0, 2 * n * blocks[0].size),
        name="weights_in_order",
    )(*blocks)


def swap(x, axis, bit):
    return lax.ppermute(x, axis, [(i, i ^ bit) for i in range(lax.axis_size(axis))])


def along(step, moves, straight=()):
    groups = lax.axis_size("grp")
    pairs = []
    for g in range(groups):
        pairs += [(g * 4 + a, (g + step) % groups * 4 + b) for a, b in moves]
        pairs += [(g * 4 + a, g * 4 + b) for a, b in straight]
    return pairs


def ring(block, step):
    right = lax.ppermute(block, ("grp", "tp"), along(step, [(i, (i + 1) % 4) for i in range(4)]))
    left = lax.ppermute(block, ("grp", "tp"), along(step, [(i, (i + 3) % 4) for i in range(4)]))
    return right, left


def middle(here, right, left, step):
    place = lax.axis_index("tp")
    inner = jnp.where(place == 2, right, left)
    block = jnp.where(jnp.logical_or(place == 0, place == 3), here, inner)
    return lax.ppermute(block, ("grp", "tp"), along(step, [(0, 2), (3, 1)], [(2, 3), (1, 0)]))


def product(panel, chunk, k):
    depth, high = chunk.shape[1], panel.shape[2]
    total = 0
    for i in range(depth // high):
        part = chunk[:, i * high : (i + 1) * high]
        total += lax.dot_general(
            panel[k * (depth // high) + i], part, (((1,), (1,)), ((), ())), preferred_element_type=jnp.float32
        )
    return total


def partial_sum(place, panel, x, right, left):
    total = product(panel, x[: right.shape[0], :], place)
    total += product(panel, right[...], lax.rem(place + 3, 4))
    return total + product(panel, left[...], lax.rem(place + 1, 4))


def finish(place, panel, total, opposite, weight):
    total += product(panel, opposite[...], lax.rem(place + 2, 4))
    hid = total.shape[0] // 2
    gate, up = total[:hid], total[hid:]
    return gate / (1.0 + jnp.exp(-gate)) * up * weight


def sum_kernel(panel, x, right, left, out):
    out[...] = partial_sum(lax.axis_index("tp"), panel, x, right, left)


def finish_kernel(panel, total, opposite, x, out):
    rows = out.shape[1]
    weight = x[rows : rows + 1, :rows].astype(jnp.float32)
    out[...] = finish(lax.axis_index("tp"), panel, total[...], opposite, weight).astype(out.dtype)


def hidden_kernel(panel, x, right, left, opposite, scale, out):
    place = lax.axis_index("tp")
    total = partial_sum(place, panel, x, right, left)
    out[...] = finish(place, panel, total, opposite, scale[...]).astype(out.dtype)


def call_rows(kernel, chunks, name, out, panel, *operands):
    share = chunks * panel.size // 4
    return pl.pallas_call(
        kernel,
        out_shape=out,
        in_specs=[VMEM] * (1 + len(operands)),
        out_specs=VMEM,
        compiler_params=PARAMS,
        cost_estimate=cost(2 * out.shape[1] * share, share),
        name=name,
    )(panel, *operands)


def down_kernel(step, groups, *refs):
    hiddens = refs[:4]
    down, out, together, rows_here, sem = refs[-5:]
    place, group = lax.axis_index("tp"), lax.axis_index("grp")
    hid, rows = hiddens[0].shape
    for s, hidden in enumerate(hiddens):
        together[rows_at(lax.rem(place - s + 4, 4), hid), :] = hidden[...]
    total = lax.dot_general(
        together[...], down[...], (((0,), (0,)), ((), ())), preferred_element_type=jnp.float32
    )
    rows_here[...] = total.astype(rows_here.dtype)
    to = out.at[rows_at(lax.rem(group - step + groups, groups), rows), :]
    copy = pltpu.make_async_copy(rows_here, to, sem)
    copy.start()
    copy.wait()


def project_down(step, groups, hiddens, down, out):
    hid, rows = hiddens[0].shape
    wide = down.shape[1]
    earlier = [] if out is None else [out]
    return pl.pallas_call(
        functools.partial(down_kernel, step, groups),
        out_shape=jax.ShapeDtypeStruct((groups * rows, wide), jnp.bfloat16),
        in_specs=[VMEM] * 4 + [WHOLE] * len(earlier) + [VMEM],
        out_specs=WHOLE,
        scratch_shapes=[pltpu.VMEM((4 * hid, rows), jnp.bfloat16), pltpu.VMEM((rows, wide), jnp.bfloat16), DMA],
        input_output_aliases={4: 0} if earlier else {},
        compiler_params=PARAMS,
        cost_estimate=cost(2 * rows * down.size, down.size + rows * wide),
        name="project_down",
    )(*hiddens, *earlier, down)


def everywhere(hidden):
    return [hidden] + [lax.ppermute(hidden, "tp", [(i, (i + s) % 4) for i in range(4)]) for s in (1, 2, 3)]


def local(dispatched, route_prob, peer_rows, gate_weight, up_weight, down_weight):
    groups, blks = lax.axis_size("grp"), lax.axis_size("blk")
    group = lax.axis_index("grp")
    per_peer = dispatched.shape[0] // groups
    hid = gate_weight.shape[2]

    rows, weight = prepare(dispatched, gate_weight[0].T, up_weight[0].T, groups)
    hops = [ring(rows[step], step) for step in range(groups)]
    opposites = [middle(rows[step], *hops[step], step) for step in range(groups)]

    live = jnp.arange(per_peer, dtype=jnp.int32)[None, :] < peer_rows[:, None]
    scales = jnp.where(live, route_prob.reshape(groups, per_peer), 0).astype(jnp.float32)
    scale = lax.dynamic_index_in_dim(scales, group, 0)
    for step in range(1, groups):
        block = attach(step, after(dispatched, *hops[0]), scales)
        rows[step] = lax.ppermute(block, "grp", [(i, (i + step) % groups) for i in range(groups)])

    have = {0: weight}
    bit = blks // 2
    while bit:
        for j in list(have):
            have[j ^ bit] = swap(have[j], "blk", bit)
        if bit == blks // 2:
            have[bit] = after(have[bit], *hops[0])
        bit //= 2
    panel = in_order([have[j] for j in range(blks)])

    sums = jax.ShapeDtypeStruct((2 * hid, per_peer), jnp.float32)
    hidden = jax.ShapeDtypeStruct((hid, per_peer), jnp.bfloat16)
    out = None
    for step, (x, (right, left), opposite) in enumerate(zip(rows, hops, opposites)):
        if step == 0:
            done = call_rows(hidden_kernel, 4, "hidden_rows", hidden, panel, x, right, left, opposite, scale)
        else:
            total = call_rows(sum_kernel, 3, "chunk_sums", sums, panel, x, right, left)
            done = call_rows(finish_kernel, 1, "last_chunk", hidden, panel, total, opposite, x)
        out = project_down(step, groups, everywhere(done), down_weight[0], out)
    return out


def solution(mesh):
    return jax.shard_map(
        local,
        mesh=mesh,
        in_specs=(
            P(("blk", "grp"), "tp"),
            P(("blk", "grp")),
            P(("blk", "grp")),
            P("grp", "blk", "tp"),
            P("grp", "blk", "tp"),
            P("grp", None, "tp"),
        ),
        out_specs=P(("blk", "grp"), "tp"),
        check_vma=False,
    )
```

```python
import functools

import jax
import jax.numpy as jnp
from jax import lax
from jax.experimental import pallas as pl
from jax.experimental.pallas import tpu as pltpu
from jax.sharding import PartitionSpec as P

PARAMS = pltpu.CompilerParams(vmem_limit_bytes=8 << 20)
VMEM = pl.BlockSpec(memory_space=pltpu.VMEM)
WHOLE = pl.BlockSpec(memory_space=pl.ANY)
DMA = pltpu.SemaphoreType.DMA
EXTRA = 16


def cost(flops, values, exps=0):
    return pl.CostEstimate(flops=flops, bytes_accessed=2 * values, transcendentals=exps)


def rows_at(index, size):
    return pl.ds(pl.multiple_of(index * size, size), size)


def after(x, *done):
    return lax.optimization_barrier((x, *done))[0]


def copy_all(pairs, sems):
    copies = [pltpu.make_async_copy(source, to, sems.at[i]) for i, (source, to) in enumerate(pairs)]
    for copy in copies:
        copy.start()
    for copy in copies:
        copy.wait()


def prepare_kernel(groups, tokens, gate, up, *refs):
    outs, panel, sems = refs[:groups], refs[groups], refs[groups + 1]
    group = lax.axis_index("grp")
    rows, hid = outs[0].shape[0], gate.shape[0]
    pairs = [(tokens.at[rows_at(lax.rem(group + step, groups), rows), :], out) for step, out in enumerate(outs)]
    copy_all(pairs + [(gate, panel.at[:hid, :]), (up, panel.at[hid:, :])], sems)


def prepare(tokens, gate, up, groups):
    rows, depth = tokens.shape
    hid, high = gate.shape
    *split, panel = pl.pallas_call(
        functools.partial(prepare_kernel, groups),
        out_shape=[jax.ShapeDtypeStruct((rows // groups, depth), tokens.dtype)] * groups
        + [jax.ShapeDtypeStruct((2 * hid, high), gate.dtype)],
        in_specs=[WHOLE] * 3,
        out_specs=[VMEM] * (groups + 1),
        scratch_shapes=[DMA((groups + 2,))],
        compiler_params=PARAMS,
        cost_estimate=cost(0, 2 * rows * depth + 4 * high * hid),
        name="prepare",
    )(*(pltpu.with_memory_space_constraint(x, pltpu.HBM) for x in (tokens, gate, up)))
    return split, panel


def weigh_kernel(tokens, chances, counts, scale, *refs):
    outs, sems = refs[:-1], refs[-1]
    group, (groups, rows) = lax.axis_index("grp"), chances.shape
    lanes = tokens.shape[1]
    copies = []
    for step, out in enumerate(outs, 1):
        source = tokens.at[rows_at(lax.rem(group + step, groups), rows), :]
        copies.append(pltpu.make_async_copy(source, out.at[:rows, :], sems.at[step - 1]))
        copies[-1].start()
    every = chances[...].astype(jnp.float32)
    line = lax.broadcasted_iota(jnp.int32, every.shape, 0)
    slot = lax.broadcasted_iota(jnp.int32, (1, rows), 1)
    for step in range(groups):
        index = lax.rem(group + step, groups)
        chance = jnp.sum(jnp.where(line == index, every, 0.0), axis=0, keepdims=True)
        weight = jnp.where(slot < counts[index], chance, 0.0)
        if step == 0:
            scale[...] = weight
        else:
            wide = jnp.concatenate([weight, jnp.zeros((1, lanes - rows), jnp.float32)], axis=1)
            outs[step - 1][rows:, :] = jnp.broadcast_to(wide, (EXTRA, lanes)).astype(outs[0].dtype)
    for copy in copies:
        copy.wait()


def weigh(tokens, chances, counts):
    groups, rows = chances.shape
    depth = tokens.shape[1]
    scale, *blocks = pl.pallas_call(
        weigh_kernel,
        out_shape=[jax.ShapeDtypeStruct((1, rows), jnp.float32)]
        + [jax.ShapeDtypeStruct((rows + EXTRA, depth), tokens.dtype)] * (groups - 1),
        in_specs=[WHOLE, VMEM, pl.BlockSpec(memory_space=pltpu.SMEM)],
        out_specs=[VMEM] * groups,
        scratch_shapes=[DMA((groups - 1,))],
        compiler_params=PARAMS,
        cost_estimate=cost(0, 2 * tokens.size),
        name="weigh",
    )(pltpu.with_memory_space_constraint(tokens, pltpu.HBM), chances, counts)
    return scale, blocks


def order_kernel(*refs):
    blocks, panel, sems = refs[:-2], refs[-2], refs[-1]
    mine = lax.axis_index("blk")
    copy_all([(block, panel.at[jnp.bitwise_xor(mine, j)]) for j, block in enumerate(blocks)], sems)


def in_order(blocks):
    n = len(blocks)
    return pl.pallas_call(
        order_kernel,
        out_shape=jax.ShapeDtypeStruct((n, *blocks[0].shape), blocks[0].dtype),
        in_specs=[WHOLE] * n,
        out_specs=VMEM,
        scratch_shapes=[DMA((n,))],
        compiler_params=PARAMS,
        cost_estimate=cost(0, 2 * n * blocks[0].size),
        name="weights_in_order",
    )(*blocks)


def swap(x, axis, bit):
    return lax.ppermute(x, axis, [(i, i ^ bit) for i in range(lax.axis_size(axis))])


def along(step, moves, straight=()):
    groups = lax.axis_size("grp")
    pairs = []
    for g in range(groups):
        pairs += [(g * 4 + a, (g + step) % groups * 4 + b) for a, b in moves]
        pairs += [(g * 4 + a, g * 4 + b) for a, b in straight]
    return pairs


def ring(block, step):
    right = lax.ppermute(block, ("grp", "tp"), along(step, [(i, (i + 1) % 4) for i in range(4)]))
    left = lax.ppermute(block, ("grp", "tp"), along(step, [(i, (i + 3) % 4) for i in range(4)]))
    return right, left


def choose_kernel(here, right, left, out):
    place = lax.axis_index("tp")
    inner = jnp.where(place == 2, right[...], left[...])
    out[...] = jnp.where(jnp.logical_or(place == 0, place == 3), here[...], inner)


def choose(here, right, left):
    return pl.pallas_call(
        choose_kernel,
        out_shape=jax.ShapeDtypeStruct(here.shape, here.dtype),
        in_specs=[VMEM] * 3,
        out_specs=VMEM,
        compiler_params=PARAMS,
        cost_estimate=cost(0, 4 * here.size),
        name="choose",
    )(here, right, left)


def middle(block, step):
    return lax.ppermute(block, ("grp", "tp"), along(step, [(0, 2), (3, 1)], [(2, 3), (1, 0)]))


def product(panel, chunk, k):
    depth, high = chunk.shape[1], panel.shape[2]
    total = 0
    for i in range(depth // high):
        part = chunk[:, i * high : (i + 1) * high]
        total += lax.dot_general(
            panel[k * (depth // high) + i], part, (((1,), (1,)), ((), ())), preferred_element_type=jnp.float32
        )
    return total


def partial_sum(place, panel, x, right, left):
    total = product(panel, x[: right.shape[0], :], place)
    total += product(panel, right[...], lax.rem(place + 3, 4))
    return total + product(panel, left[...], lax.rem(place + 1, 4))


def finish(place, panel, total, opposite, weight):
    total += product(panel, opposite[...], lax.rem(place + 2, 4))
    hid = total.shape[0] // 2
    gate, up = total[:hid], total[hid:]
    return gate / (1.0 + jnp.exp(-gate)) * up * weight


def sum_kernel(panel, x, right, left, out):
    out[...] = partial_sum(lax.axis_index("tp"), panel, x, right, left)


def finish_kernel(panel, total, opposite, x, out):
    rows = out.shape[1]
    weight = x[rows : rows + 1, :rows].astype(jnp.float32)
    out[...] = finish(lax.axis_index("tp"), panel, total[...], opposite, weight).astype(out.dtype)


def hidden_kernel(panel, x, right, left, opposite, scale, out):
    place = lax.axis_index("tp")
    total = partial_sum(place, panel, x, right, left)
    out[...] = finish(place, panel, total, opposite, scale[...]).astype(out.dtype)


def call_rows(kernel, chunks, name, out, panel, *operands):
    share = chunks * panel.size // 4
    return pl.pallas_call(
        kernel,
        out_shape=out,
        in_specs=[VMEM] * (1 + len(operands)),
        out_specs=VMEM,
        compiler_params=PARAMS,
        cost_estimate=cost(2 * out.shape[1] * share, share),
        name=name,
    )(panel, *operands)


def down_kernel(step, groups, *refs):
    hiddens = refs[:4]
    down, out, together, rows_here, sem = refs[-5:]
    place, group = lax.axis_index("tp"), lax.axis_index("grp")
    hid, rows = hiddens[0].shape
    for s, hidden in enumerate(hiddens):
        together[rows_at(lax.rem(place - s + 4, 4), hid), :] = hidden[...]
    total = lax.dot_general(
        together[...], down[...], (((0,), (0,)), ((), ())), preferred_element_type=jnp.float32
    )
    rows_here[...] = total.astype(rows_here.dtype)
    to = out.at[rows_at(lax.rem(group - step + groups, groups), rows), :]
    copy = pltpu.make_async_copy(rows_here, to, sem)
    copy.start()
    copy.wait()


def project_down(step, groups, hiddens, down, out):
    hid, rows = hiddens[0].shape
    wide = down.shape[1]
    earlier = [] if out is None else [out]
    return pl.pallas_call(
        functools.partial(down_kernel, step, groups),
        out_shape=jax.ShapeDtypeStruct((groups * rows, wide), jnp.bfloat16),
        in_specs=[VMEM] * 4 + [WHOLE] * len(earlier) + [VMEM],
        out_specs=WHOLE,
        scratch_shapes=[pltpu.VMEM((4 * hid, rows), jnp.bfloat16), pltpu.VMEM((rows, wide), jnp.bfloat16), DMA],
        input_output_aliases={4: 0} if earlier else {},
        compiler_params=PARAMS,
        cost_estimate=cost(2 * rows * down.size, down.size + rows * wide),
        name="project_down",
    )(*hiddens, *earlier, down)


def everywhere(hidden):
    return [hidden] + [lax.ppermute(hidden, "tp", [(i, (i + s) % 4) for i in range(4)]) for s in (1, 2, 3)]


def local(dispatched, route_prob, peer_rows, gate_weight, up_weight, down_weight):
    groups, blks = lax.axis_size("grp"), lax.axis_size("blk")
    group = lax.axis_index("grp")
    per_peer = dispatched.shape[0] // groups
    hid = gate_weight.shape[2]

    rows, weight = prepare(dispatched, gate_weight[0].T, up_weight[0].T, groups)
    hops = [ring(rows[step], step) for step in range(groups)]
    chosen = [choose(rows[step], *hops[step]) for step in range(groups)]
    opposites = [middle(chosen[step], step) for step in range(groups)]

    scale, blocks = weigh(after(dispatched, chosen[-1]), route_prob.reshape(groups, per_peer), peer_rows)
    for step in range(1, groups):
        rows[step] = lax.ppermute(blocks[step - 1], "grp", [(i, (i + step) % groups) for i in range(groups)])

    have = {0: weight}
    bit = blks // 2
    while bit:
        for j in list(have):
            have[j ^ bit] = swap(have[j], "blk", bit)
        if bit == blks // 2:
            have = {j: after(block, *hops[-1], opposites[0], chosen[-1]) for j, block in have.items()}
        bit //= 2
    panel = in_order([have[j] for j in range(blks)])

    sums = jax.ShapeDtypeStruct((2 * hid, per_peer), jnp.float32)
    hidden = jax.ShapeDtypeStruct((hid, per_peer), jnp.bfloat16)
    out = None
    for step, (x, (right, left), opposite) in enumerate(zip(rows, hops, opposites)):
        if step == 0:
            done = call_rows(hidden_kernel, 4, "hidden_rows", hidden, panel, x, right, left, opposite, scale)
        else:
            total = call_rows(sum_kernel, 3, "chunk_sums", sums, panel, x, right, left)
            done = call_rows(finish_kernel, 1, "last_chunk", hidden, panel, total, opposite, x)
        out = project_down(step, groups, everywhere(done), down_weight[0], out)
    return out


def solution(mesh):
    return jax.shard_map(
        local,
        mesh=mesh,
        in_specs=(
            P(("blk", "grp"), "tp"),
            P(("blk", "grp")),
            P(("blk", "grp")),
            P("grp", "blk", "tp"),
            P("grp", "blk", "tp"),
            P("grp", None, "tp"),
        ),
        out_specs=P(("blk", "grp"), "tp"),
        check_vma=False,
    )
```

```python
import functools

import jax
import jax.numpy as jnp
from jax import lax
from jax.experimental import pallas as pl
from jax.experimental.pallas import tpu as pltpu
from jax.sharding import PartitionSpec as P

PARAMS = pltpu.CompilerParams(vmem_limit_bytes=6 << 20)
VMEM = pl.BlockSpec(memory_space=pltpu.VMEM)
WHOLE = pl.BlockSpec(memory_space=pl.ANY)
DMA = pltpu.SemaphoreType.DMA
EXTRA = 16


def cost(flops, values, exps=0):
    return pl.CostEstimate(flops=flops, bytes_accessed=2 * values, transcendentals=exps)


def rows_at(index, size):
    return pl.ds(pl.multiple_of(index * size, size), size)


def after(x, *done):
    return lax.optimization_barrier((x, *done))[0]


def copy_all(pairs, sems):
    copies = [pltpu.make_async_copy(source, to, sems.at[i]) for i, (source, to) in enumerate(pairs)]
    for copy in copies:
        copy.start()
    for copy in copies:
        copy.wait()


def prepare_kernel(groups, tokens, gate, up, *refs):
    outs, panel, sems = refs[:groups], refs[groups], refs[groups + 1]
    group = lax.axis_index("grp")
    rows, hid = outs[0].shape[0], gate.shape[0]
    pairs = [(tokens.at[rows_at(lax.rem(group + step, groups), rows), :], out) for step, out in enumerate(outs)]
    copy_all(pairs + [(gate, panel.at[:hid, :]), (up, panel.at[hid:, :])], sems)


def prepare(tokens, gate, up, groups):
    rows, depth = tokens.shape
    hid, high = gate.shape
    *split, panel = pl.pallas_call(
        functools.partial(prepare_kernel, groups),
        out_shape=[jax.ShapeDtypeStruct((rows // groups, depth), tokens.dtype)] * groups
        + [jax.ShapeDtypeStruct((2 * hid, high), gate.dtype)],
        in_specs=[WHOLE] * 3,
        out_specs=[VMEM] * (groups + 1),
        scratch_shapes=[DMA((groups + 2,))],
        compiler_params=PARAMS,
        cost_estimate=cost(0, 2 * rows * depth + 4 * high * hid),
        name="prepare",
    )(*(pltpu.with_memory_space_constraint(x, pltpu.HBM) for x in (tokens, gate, up)))
    return split, panel


def attach_kernel(step, tokens, scales, out, sem):
    rows = tokens.shape[0] // scales.shape[0]
    index = lax.rem(lax.axis_index("grp") + step, scales.shape[0])
    copy = pltpu.make_async_copy(tokens.at[rows_at(index, rows), :], out.at[:rows, :], sem)
    copy.start()
    scale = scales[pl.ds(index, 1), :].astype(out.dtype)
    lanes = out.shape[1]
    line = jnp.concatenate([scale, jnp.zeros((1, lanes - rows), out.dtype)], axis=1)
    out[rows:, :] = jnp.broadcast_to(line, (EXTRA, lanes))
    copy.wait()


def attach(step, tokens, scales):
    groups, rows = scales.shape
    depth = tokens.shape[1]
    return pl.pallas_call(
        functools.partial(attach_kernel, step),
        out_shape=jax.ShapeDtypeStruct((rows + EXTRA, depth), tokens.dtype),
        in_specs=[WHOLE, VMEM],
        out_specs=VMEM,
        scratch_shapes=[DMA],
        compiler_params=PARAMS,
        cost_estimate=cost(0, 2 * rows * depth),
        name="attach_weights",
    )(pltpu.with_memory_space_constraint(tokens, pltpu.HBM), scales)


def order_kernel(*refs):
    blocks, panel, sems = refs[:-2], refs[-2], refs[-1]
    mine = lax.axis_index("blk")
    copy_all([(block, panel.at[jnp.bitwise_xor(mine, j)]) for j, block in enumerate(blocks)], sems)


def in_order(blocks):
    n = len(blocks)
    return pl.pallas_call(
        order_kernel,
        out_shape=jax.ShapeDtypeStruct((n, *blocks[0].shape), blocks[0].dtype),
        in_specs=[WHOLE] * n,
        out_specs=VMEM,
        scratch_shapes=[DMA((n,))],
        compiler_params=PARAMS,
        cost_estimate=cost(0, 2 * n * blocks[0].size),
        name="weights_in_order",
    )(*blocks)


def swap(x, axis, bit):
    return lax.ppermute(x, axis, [(i, i ^ bit) for i in range(lax.axis_size(axis))])


def along(step, moves, straight=()):
    groups = lax.axis_size("grp")
    pairs = []
    for g in range(groups):
        pairs += [(g * 4 + a, (g + step) % groups * 4 + b) for a, b in moves]
        pairs += [(g * 4 + a, g * 4 + b) for a, b in straight]
    return pairs


def ring(block, step):
    right = lax.ppermute(block, ("grp", "tp"), along(step, [(i, (i + 1) % 4) for i in range(4)]))
    left = lax.ppermute(block, ("grp", "tp"), along(step, [(i, (i + 3) % 4) for i in range(4)]))
    return right, left


def middle(here, right, left, step):
    place = lax.axis_index("tp")
    inner = jnp.where(place == 2, right, left)
    block = jnp.where(jnp.logical_or(place == 0, place == 3), here, inner)
    came = lax.ppermute(block, ("grp", "tp"), along(step, [(0, 2), (3, 1)], [(2, 3), (1, 0)]))
    return pltpu.with_memory_space_constraint(came, pltpu.VMEM)


def product(panel, chunk, k):
    depth, high = chunk.shape[1], panel.shape[2]
    total = 0
    for i in range(depth // high):
        part = chunk[:, i * high : (i + 1) * high]
        total += lax.dot_general(
            panel[k * (depth // high) + i], part, (((1,), (1,)), ((), ())), preferred_element_type=jnp.float32
        )
    return total


def partial_sum(place, panel, x, right, left):
    total = product(panel, x[: right.shape[0], :], place)
    total += product(panel, right[...], lax.rem(place + 3, 4))
    return total + product(panel, left[...], lax.rem(place + 1, 4))


def finish(place, panel, total, opposite, weight):
    total += product(panel, opposite[...], lax.rem(place + 2, 4))
    hid = total.shape[0] // 2
    gate, up = total[:hid], total[hid:]
    return gate / (1.0 + jnp.exp(-gate)) * up * weight


def sum_kernel(panel, x, right, left, out):
    out[...] = partial_sum(lax.axis_index("tp"), panel, x, right, left)


def finish_kernel(panel, total, opposite, x, out):
    rows = out.shape[1]
    weight = x[rows : rows + 1, :rows].astype(jnp.float32)
    out[...] = finish(lax.axis_index("tp"), panel, total[...], opposite, weight).astype(out.dtype)


def hidden_kernel(panel, x, right, left, opposite, scale, out):
    place = lax.axis_index("tp")
    total = partial_sum(place, panel, x, right, left)
    out[...] = finish(place, panel, total, opposite, scale[...]).astype(out.dtype)


def call_rows(kernel, chunks, name, out, panel, *operands):
    share = chunks * panel.size // 4
    return pl.pallas_call(
        kernel,
        out_shape=out,
        in_specs=[VMEM] * (1 + len(operands)),
        out_specs=VMEM,
        compiler_params=PARAMS,
        cost_estimate=cost(2 * out.shape[1] * share, share),
        name=name,
    )(panel, *operands)


def down_kernel(step, groups, *refs):
    hiddens = refs[:4]
    down, out, together, rows_here, sem = refs[-5:]
    place, group = lax.axis_index("tp"), lax.axis_index("grp")
    hid, rows = hiddens[0].shape
    for s, hidden in enumerate(hiddens):
        together[rows_at(lax.rem(place - s + 4, 4), hid), :] = hidden[...]
    total = lax.dot_general(
        together[...], down[...], (((0,), (0,)), ((), ())), preferred_element_type=jnp.float32
    )
    rows_here[...] = total.astype(rows_here.dtype)
    to = out.at[rows_at(lax.rem(group - step + groups, groups), rows), :]
    copy = pltpu.make_async_copy(rows_here, to, sem)
    copy.start()
    copy.wait()


def project_down(step, groups, hiddens, down, out):
    hid, rows = hiddens[0].shape
    wide = down.shape[1]
    earlier = [] if out is None else [out]
    return pl.pallas_call(
        functools.partial(down_kernel, step, groups),
        out_shape=jax.ShapeDtypeStruct((groups * rows, wide), jnp.bfloat16),
        in_specs=[VMEM] * 4 + [WHOLE] * len(earlier) + [VMEM],
        out_specs=WHOLE,
        scratch_shapes=[pltpu.VMEM((4 * hid, rows), jnp.bfloat16), pltpu.VMEM((rows, wide), jnp.bfloat16), DMA],
        input_output_aliases={4: 0} if earlier else {},
        compiler_params=PARAMS,
        cost_estimate=cost(2 * rows * down.size, down.size + rows * wide),
        name="project_down",
    )(*hiddens, *earlier, down)


def everywhere(hidden):
    return [hidden] + [lax.ppermute(hidden, "tp", [(i, (i + s) % 4) for i in range(4)]) for s in (1, 2, 3)]


def local(dispatched, route_prob, peer_rows, gate_weight, up_weight, down_weight):
    groups, blks = lax.axis_size("grp"), lax.axis_size("blk")
    group = lax.axis_index("grp")
    per_peer = dispatched.shape[0] // groups
    hid = gate_weight.shape[2]

    rows, weight = prepare(dispatched, gate_weight[0].T, up_weight[0].T, groups)
    hops = [ring(rows[step], step) for step in range(groups)]
    opposites = [middle(rows[step], *hops[step], step) for step in range(groups)]

    live = jnp.arange(per_peer, dtype=jnp.int32)[None, :] < peer_rows[:, None]
    scales = jnp.where(live, route_prob.reshape(groups, per_peer), 0).astype(jnp.float32)
    scale = lax.dynamic_index_in_dim(scales, group, 0)
    for step in range(1, groups):
        block = attach(step, after(dispatched, *hops[0]), scales)
        rows[step] = lax.ppermute(block, "grp", [(i, (i + step) % groups) for i in range(groups)])

    have = {0: weight}
    bit = blks // 2
    while bit:
        for j in list(have):
            have[j ^ bit] = swap(have[j], "blk", bit)
        if bit == blks // 2:
            have[bit] = after(have[bit], *hops[0])
        bit //= 2
    panel = in_order([have[j] for j in range(blks)])

    sums = jax.ShapeDtypeStruct((2 * hid, per_peer), jnp.float32)
    hidden = jax.ShapeDtypeStruct((hid, per_peer), jnp.bfloat16)
    out = None
    for step, (x, (right, left), opposite) in enumerate(zip(rows, hops, opposites)):
        if step == 0:
            done = call_rows(hidden_kernel, 4, "hidden_rows", hidden, panel, x, right, left, opposite, scale)
        else:
            total = call_rows(sum_kernel, 3, "chunk_sums", sums, panel, x, right, left)
            done = call_rows(finish_kernel, 1, "last_chunk", hidden, panel, total, opposite, x)
        out = project_down(step, groups, everywhere(done), down_weight[0], out)
    return out


def solution(mesh):
    return jax.shard_map(
        local,
        mesh=mesh,
        in_specs=(
            P(("blk", "grp"), "tp"),
            P(("blk", "grp")),
            P(("blk", "grp")),
            P("grp", "blk", "tp"),
            P("grp", "blk", "tp"),
            P("grp", None, "tp"),
        ),
        out_specs=P(("blk", "grp"), "tp"),
        check_vma=False,
    )
```

```python
import functools

import jax
import jax.numpy as jnp
from jax import lax
from jax.experimental import pallas as pl
from jax.experimental.pallas import tpu as pltpu
from jax.sharding import PartitionSpec as P

PARAMS = pltpu.CompilerParams(vmem_limit_bytes=6 << 20)
VMEM = pl.BlockSpec(memory_space=pltpu.VMEM)
WHOLE = pl.BlockSpec(memory_space=pl.ANY)
DMA = pltpu.SemaphoreType.DMA
EXTRA = 16


def cost(flops, values, exps=0):
    return pl.CostEstimate(flops=flops, bytes_accessed=2 * values, transcendentals=exps)


def rows_at(index, size):
    return pl.ds(pl.multiple_of(index * size, size), size)


def after(x, *done):
    return lax.optimization_barrier((x, *done))[0]


def copy_all(pairs, sems):
    copies = [pltpu.make_async_copy(source, to, sems.at[i]) for i, (source, to) in enumerate(pairs)]
    for copy in copies:
        copy.start()
    for copy in copies:
        copy.wait()


def prepare_kernel(groups, tokens, gate, up, *refs):
    outs, panel, sems = refs[:groups], refs[groups], refs[groups + 1]
    group = lax.axis_index("grp")
    rows, hid = outs[0].shape[0], gate.shape[0]
    pairs = [(tokens.at[rows_at(lax.rem(group + step, groups), rows), :], out) for step, out in enumerate(outs)]
    copy_all(pairs + [(gate, panel.at[:hid, :]), (up, panel.at[hid:, :])], sems)


def prepare(tokens, gate, up, groups):
    rows, depth = tokens.shape
    hid, high = gate.shape
    *split, panel = pl.pallas_call(
        functools.partial(prepare_kernel, groups),
        out_shape=[jax.ShapeDtypeStruct((rows // groups, depth), tokens.dtype)] * groups
        + [jax.ShapeDtypeStruct((2 * hid, high), gate.dtype)],
        in_specs=[WHOLE] * 3,
        out_specs=[VMEM] * (groups + 1),
        scratch_shapes=[DMA((groups + 2,))],
        compiler_params=PARAMS,
        cost_estimate=cost(0, 2 * rows * depth + 4 * high * hid),
        name="prepare",
    )(*(pltpu.with_memory_space_constraint(x, pltpu.HBM) for x in (tokens, gate, up)))
    return split, panel


def weigh_kernel(chances, counts, out):
    group, (groups, rows) = lax.axis_index("grp"), chances.shape
    every = chances[...].astype(jnp.float32)
    line = lax.broadcasted_iota(jnp.int32, every.shape, 0)
    slot = lax.broadcasted_iota(jnp.int32, (1, rows), 1)
    for step in range(groups):
        index = lax.rem(group + step, groups)
        chance = jnp.sum(jnp.where(line == index, every, 0.0), axis=0, keepdims=True)
        out[step : step + 1, :] = jnp.where(slot < counts[index], chance, 0.0)


def weigh(chances, counts):
    return pl.pallas_call(
        weigh_kernel,
        out_shape=jax.ShapeDtypeStruct(chances.shape, jnp.float32),
        in_specs=[VMEM, pl.BlockSpec(memory_space=pltpu.SMEM)],
        out_specs=VMEM,
        compiler_params=PARAMS,
        cost_estimate=cost(0, chances.size),
        name="weigh",
    )(chances, counts)


def attach_kernel(step, tokens, scales, out, sem):
    groups, rows = scales.shape
    index = lax.rem(lax.axis_index("grp") + step, groups)
    copy = pltpu.make_async_copy(tokens.at[rows_at(index, rows), :], out.at[:rows, :], sem)
    copy.start()
    lanes = out.shape[1]
    line = jnp.concatenate([scales[step : step + 1, :], jnp.zeros((1, lanes - rows), jnp.float32)], axis=1)
    out[rows:, :] = jnp.broadcast_to(line, (EXTRA, lanes)).astype(out.dtype)
    copy.wait()


def attach(step, tokens, scales):
    groups, rows = scales.shape
    depth = tokens.shape[1]
    return pl.pallas_call(
        functools.partial(attach_kernel, step),
        out_shape=jax.ShapeDtypeStruct((rows + EXTRA, depth), tokens.dtype),
        in_specs=[WHOLE, VMEM],
        out_specs=VMEM,
        scratch_shapes=[DMA],
        compiler_params=PARAMS,
        cost_estimate=cost(0, 2 * rows * depth),
        name="attach_weights",
    )(pltpu.with_memory_space_constraint(tokens, pltpu.HBM), scales)


def order_kernel(*refs):
    blocks, panel, sems = refs[:-2], refs[-2], refs[-1]
    mine = lax.axis_index("blk")
    copy_all([(block, panel.at[jnp.bitwise_xor(mine, j)]) for j, block in enumerate(blocks)], sems)


def in_order(blocks):
    n = len(blocks)
    return pl.pallas_call(
        order_kernel,
        out_shape=jax.ShapeDtypeStruct((n, *blocks[0].shape), blocks[0].dtype),
        in_specs=[WHOLE] * n,
        out_specs=VMEM,
        scratch_shapes=[DMA((n,))],
        compiler_params=PARAMS,
        cost_estimate=cost(0, 2 * n * blocks[0].size),
        name="weights_in_order",
    )(*blocks)


def swap(x, axis, bit):
    return lax.ppermute(x, axis, [(i, i ^ bit) for i in range(lax.axis_size(axis))])


def along(step, moves, straight=()):
    groups = lax.axis_size("grp")
    pairs = []
    for g in range(groups):
        pairs += [(g * 4 + a, (g + step) % groups * 4 + b) for a, b in moves]
        pairs += [(g * 4 + a, g * 4 + b) for a, b in straight]
    return pairs


def ring(block, step):
    right = lax.ppermute(block, ("grp", "tp"), along(step, [(i, (i + 1) % 4) for i in range(4)]))
    left = lax.ppermute(block, ("grp", "tp"), along(step, [(i, (i + 3) % 4) for i in range(4)]))
    return right, left


def choose_kernel(here, right, left, out):
    place = lax.axis_index("tp")
    inner = jnp.where(place == 2, right[...], left[...])
    out[...] = jnp.where(jnp.logical_or(place == 0, place == 3), here[...], inner)


def choose(here, right, left):
    return pl.pallas_call(
        choose_kernel,
        out_shape=jax.ShapeDtypeStruct(here.shape, here.dtype),
        in_specs=[VMEM] * 3,
        out_specs=VMEM,
        compiler_params=PARAMS,
        cost_estimate=cost(8000000000, 4 * here.size),
        name="choose",
    )(here, right, left)


def middle(block, step):
    return lax.ppermute(block, ("grp", "tp"), along(step, [(0, 2), (3, 1)], [(2, 3), (1, 0)]))


def product(panel, chunk, k):
    depth, high = chunk.shape[1], panel.shape[2]
    total = 0
    for i in range(depth // high):
        part = chunk[:, i * high : (i + 1) * high]
        total += lax.dot_general(
            panel[k * (depth // high) + i], part, (((1,), (1,)), ((), ())), preferred_element_type=jnp.float32
        )
    return total


def partial_sum(place, panel, x, right, left):
    total = product(panel, x[: right.shape[0], :], place)
    total += product(panel, right[...], lax.rem(place + 3, 4))
    return total + product(panel, left[...], lax.rem(place + 1, 4))


def finish(place, panel, total, opposite, weight):
    total += product(panel, opposite[...], lax.rem(place + 2, 4))
    hid = total.shape[0] // 2
    gate, up = total[:hid], total[hid:]
    return gate / (1.0 + jnp.exp(-gate)) * up * weight


def sum_kernel(groups, panel, *refs):
    out, place = refs[-1], lax.axis_index("tp")
    rows = out.shape[1] // groups
    for step in range(groups):
        out[:, step * rows : (step + 1) * rows] = partial_sum(place, panel, *refs[3 * step : 3 * step + 3])


def finish_kernel(groups, panel, totals, scales, *refs):
    out, place = refs[-1], lax.axis_index("tp")
    rows = out.shape[1] // groups
    for step in range(groups):
        at = slice(step * rows, (step + 1) * rows)
        if step == 0:
            weight = scales[:1, :]
        else:
            weight = refs[groups + step - 1][rows : rows + 1, :rows].astype(jnp.float32)
        out[:, at] = finish(place, panel, totals[:, at], refs[step], weight).astype(out.dtype)


def call_rows(kernel, chunks, name, out, panel, *operands):
    share = chunks * panel.size // 4
    return pl.pallas_call(
        functools.partial(kernel, lax.axis_size("grp")),
        out_shape=out,
        in_specs=[VMEM] * (1 + len(operands)),
        out_specs=VMEM,
        compiler_params=PARAMS,
        cost_estimate=cost(2 * out.shape[1] * share, share),
        name=name,
    )(panel, *operands)


def down_kernel(groups, *refs):
    hiddens = refs[:4]
    down, out, together, rows_here, sems = refs[4:]
    place, group = lax.axis_index("tp"), lax.axis_index("grp")
    hid, rows = hiddens[0].shape[0], hiddens[0].shape[1] // groups
    for s, hidden in enumerate(hiddens):
        together[rows_at(lax.rem(place - s + 4, 4), hid), :] = hidden[...]
    total = lax.dot_general(
        together[...], down[...], (((0,), (0,)), ((), ())), preferred_element_type=jnp.float32
    )
    rows_here[...] = total.astype(rows_here.dtype)
    pairs = []
    for step in range(groups):
        to = out.at[rows_at(lax.rem(group - step + groups, groups), rows), :]
        pairs.append((rows_here.at[step * rows : (step + 1) * rows, :], to))
    copy_all(pairs, sems)


def project_down(groups, hiddens, down):
    hid, rows = hiddens[0].shape
    wide = down.shape[1]
    return pl.pallas_call(
        functools.partial(down_kernel, groups),
        out_shape=jax.ShapeDtypeStruct((rows, wide), jnp.bfloat16),
        in_specs=[VMEM] * 5,
        out_specs=WHOLE,
        scratch_shapes=[pltpu.VMEM((4 * hid, rows), jnp.bfloat16), pltpu.VMEM((rows, wide), jnp.bfloat16), DMA((groups,))],
        compiler_params=PARAMS,
        cost_estimate=cost(2 * rows * down.size, down.size + rows * wide),
        name="project_down",
    )(*hiddens, down)


def everywhere(hidden):
    return [hidden] + [lax.ppermute(hidden, "tp", [(i, (i + s) % 4) for i in range(4)]) for s in (1, 2, 3)]


def local(dispatched, route_prob, peer_rows, gate_weight, up_weight, down_weight):
    groups, blks = lax.axis_size("grp"), lax.axis_size("blk")
    per_peer = dispatched.shape[0] // groups
    hid = gate_weight.shape[2]

    rows, weight = prepare(dispatched, gate_weight[0].T, up_weight[0].T, groups)
    hops = [ring(rows[step], step) for step in range(groups)]
    opposites = [middle(choose(rows[step], *hops[step]), step) for step in range(groups)]

    scales = weigh(route_prob.reshape(groups, per_peer), peer_rows)
    for step in range(1, groups):
        block = attach(step, after(dispatched, *hops[0]), scales)
        rows[step] = lax.ppermute(block, "grp", [(i, (i + step) % groups) for i in range(groups)])

    have = {0: weight}
    bit = blks // 2
    while bit:
        for j in list(have):
            have[j ^ bit] = swap(have[j], "blk", bit)
        if bit == blks // 2:
            have[bit] = after(have[bit], *hops[0])
            have[0] = after(have[0], have[bit])
        bit //= 2
    panel = in_order([have[j] for j in range(blks)])

    count = groups * per_peer
    sums = jax.ShapeDtypeStruct((2 * hid, count), jnp.float32)
    hidden = jax.ShapeDtypeStruct((hid, count), jnp.bfloat16)
    near = [chunk for x, (right, left) in zip(rows, hops) for chunk in (x, right, left)]
    totals = call_rows(sum_kernel, 3, "chunk_sums", sums, panel, *near)
    done = call_rows(finish_kernel, 1, "last_chunk", hidden, panel, totals, scales, *opposites, *rows[1:])
    return project_down(groups, everywhere(done), down_weight[0])


def solution(mesh):
    return jax.shard_map(
        local,
        mesh=mesh,
        in_specs=(
            P(("blk", "grp"), "tp"),
            P(("blk", "grp")),
            P(("blk", "grp")),
            P("grp", "blk", "tp"),
            P("grp", "blk", "tp"),
            P("grp", None, "tp"),
        ),
        out_specs=P(("blk", "grp"), "tp"),
        check_vma=False,
    )
```

```python
import functools

import jax
import jax.numpy as jnp
from jax import lax
from jax.experimental import pallas as pl
from jax.experimental.pallas import tpu as pltpu
from jax.sharding import PartitionSpec as P

PARAMS = pltpu.CompilerParams(vmem_limit_bytes=6 << 20)
VMEM = pl.BlockSpec(memory_space=pltpu.VMEM)
WHOLE = pl.BlockSpec(memory_space=pl.ANY)
DMA = pltpu.SemaphoreType.DMA
EXTRA = 16


def cost(flops, values, exps=0):
    return pl.CostEstimate(flops=flops, bytes_accessed=2 * values, transcendentals=exps)


def rows_at(index, size):
    return pl.ds(pl.multiple_of(index * size, size), size)


def after(x, *done):
    return lax.optimization_barrier((x, *done))[0]


def copy_all(pairs, sems):
    copies = [pltpu.make_async_copy(source, to, sems.at[i]) for i, (source, to) in enumerate(pairs)]
    for copy in copies:
        copy.start()
    for copy in copies:
        copy.wait()


def prepare_kernel(groups, tokens, gate, up, *refs):
    outs, panel, sems = refs[:groups], refs[groups], refs[groups + 1]
    group = lax.axis_index("grp")
    rows, hid = outs[0].shape[0], gate.shape[0]
    pairs = [(tokens.at[rows_at(lax.rem(group + step, groups), rows), :], out) for step, out in enumerate(outs)]
    copy_all(pairs + [(gate, panel.at[:hid, :]), (up, panel.at[hid:, :])], sems)


def prepare(tokens, gate, up, groups):
    rows, depth = tokens.shape
    hid, high = gate.shape
    *split, panel = pl.pallas_call(
        functools.partial(prepare_kernel, groups),
        out_shape=[jax.ShapeDtypeStruct((rows // groups, depth), tokens.dtype)] * groups
        + [jax.ShapeDtypeStruct((2 * hid, high), gate.dtype)],
        in_specs=[WHOLE] * 3,
        out_specs=[VMEM] * (groups + 1),
        scratch_shapes=[DMA((groups + 2,))],
        compiler_params=PARAMS,
        cost_estimate=cost(0, 2 * rows * depth + 4 * high * hid),
        name="prepare",
    )(*(pltpu.with_memory_space_constraint(x, pltpu.HBM) for x in (tokens, gate, up)))
    return split, panel


def weigh_kernel(chances, counts, out):
    group, (groups, rows) = lax.axis_index("grp"), chances.shape
    every = chances[...].astype(jnp.float32)
    line = lax.broadcasted_iota(jnp.int32, every.shape, 0)
    slot = lax.broadcasted_iota(jnp.int32, (1, rows), 1)
    for step in range(groups):
        index = lax.rem(group + step, groups)
        chance = jnp.sum(jnp.where(line == index, every, 0.0), axis=0, keepdims=True)
        out[step : step + 1, :] = jnp.where(slot < counts[index], chance, 0.0)


def weigh(chances, counts):
    return pl.pallas_call(
        weigh_kernel,
        out_shape=jax.ShapeDtypeStruct(chances.shape, jnp.float32),
        in_specs=[VMEM, pl.BlockSpec(memory_space=pltpu.SMEM)],
        out_specs=VMEM,
        compiler_params=PARAMS,
        cost_estimate=cost(0, chances.size),
        name="weigh",
    )(chances, counts)


def attach_kernel(step, tokens, scales, out, sem):
    groups, rows = scales.shape
    index = lax.rem(lax.axis_index("grp") + step, groups)
    copy = pltpu.make_async_copy(tokens.at[rows_at(index, rows), :], out.at[:rows, :], sem)
    copy.start()
    lanes = out.shape[1]
    line = jnp.concatenate([scales[step : step + 1, :], jnp.zeros((1, lanes - rows), jnp.float32)], axis=1)
    out[rows:, :] = jnp.broadcast_to(line, (EXTRA, lanes)).astype(out.dtype)
    copy.wait()


def attach(step, tokens, scales):
    groups, rows = scales.shape
    depth = tokens.shape[1]
    return pl.pallas_call(
        functools.partial(attach_kernel, step),
        out_shape=jax.ShapeDtypeStruct((rows + EXTRA, depth), tokens.dtype),
        in_specs=[WHOLE, VMEM],
        out_specs=VMEM,
        scratch_shapes=[DMA],
        compiler_params=PARAMS,
        cost_estimate=cost(0, 2 * rows * depth),
        name="attach_weights",
    )(pltpu.with_memory_space_constraint(tokens, pltpu.HBM), scales)


def order_kernel(*refs):
    blocks, panel, sems = refs[:-2], refs[-2], refs[-1]
    mine = lax.axis_index("blk")
    copy_all([(block, panel.at[jnp.bitwise_xor(mine, j)]) for j, block in enumerate(blocks)], sems)


def in_order(blocks):
    n = len(blocks)
    return pl.pallas_call(
        order_kernel,
        out_shape=jax.ShapeDtypeStruct((n, *blocks[0].shape), blocks[0].dtype),
        in_specs=[WHOLE] * n,
        out_specs=VMEM,
        scratch_shapes=[DMA((n,))],
        compiler_params=PARAMS,
        cost_estimate=cost(0, 2 * n * blocks[0].size),
        name="weights_in_order",
    )(*blocks)


def swap(x, axis, bit):
    return lax.ppermute(x, axis, [(i, i ^ bit) for i in range(lax.axis_size(axis))])


def along(step, moves, straight=()):
    groups = lax.axis_size("grp")
    pairs = []
    for g in range(groups):
        pairs += [(g * 4 + a, (g + step) % groups * 4 + b) for a, b in moves]
        pairs += [(g * 4 + a, g * 4 + b) for a, b in straight]
    return pairs


def ring(block, step):
    right = lax.ppermute(block, ("grp", "tp"), along(step, [(i, (i + 1) % 4) for i in range(4)]))
    left = lax.ppermute(block, ("grp", "tp"), along(step, [(i, (i + 3) % 4) for i in range(4)]))
    return right, left


def choose_kernel(here, right, left, out):
    place = lax.axis_index("tp")
    inner = jnp.where(place == 2, right[...], left[...])
    out[...] = jnp.where(jnp.logical_or(place == 0, place == 3), here[...], inner)


def choose(here, right, left):
    return pl.pallas_call(
        choose_kernel,
        out_shape=jax.ShapeDtypeStruct(here.shape, here.dtype),
        in_specs=[VMEM] * 3,
        out_specs=VMEM,
        compiler_params=PARAMS,
        cost_estimate=cost(8000000000, 4 * here.size),
        name="choose",
    )(here, right, left)


def middle(block, step):
    return lax.ppermute(block, ("grp", "tp"), along(step, [(0, 2), (3, 1)], [(2, 3), (1, 0)]))


def product(panel, chunk, k):
    depth, high = chunk.shape[1], panel.shape[2]
    total = 0
    for i in range(depth // high):
        part = chunk[:, i * high : (i + 1) * high]
        total += lax.dot_general(
            panel[k * (depth // high) + i], part, (((1,), (1,)), ((), ())), preferred_element_type=jnp.float32
        )
    return total


def near_sum(place, panel, right, left):
    return product(panel, right[...], lax.rem(place + 3, 4)) + product(panel, left[...], lax.rem(place + 1, 4))


def finish(place, panel, total, x, opposite, weight):
    total += product(panel, x, place)
    total += product(panel, opposite, lax.rem(place + 2, 4))
    hid = total.shape[0] // 2
    gate, up = total[:hid], total[hid:]
    return gate / (1.0 + jnp.exp(-gate)) * up * weight


def hidden_kernel(panel, right, left, x, opposite, scales, out):
    place = lax.axis_index("tp")
    total = near_sum(place, panel, right, left)
    out[...] = finish(place, panel, total, x[...], opposite[...], scales[:1, :]).astype(out.dtype)


def sum_kernel(panel, right, left, out):
    out[...] = near_sum(lax.axis_index("tp"), panel, right, left)


def finish_kernel(panel, total, x, opposite, out):
    rows = out.shape[1]
    weight = x[rows : rows + 1, :rows].astype(jnp.float32)
    out[...] = finish(lax.axis_index("tp"), panel, total[...], x[:rows, :], opposite[...], weight).astype(out.dtype)


def call_rows(kernel, chunks, name, out, panel, *operands):
    share = chunks * panel.size // 4
    return pl.pallas_call(
        kernel,
        out_shape=out,
        in_specs=[VMEM] * (1 + len(operands)),
        out_specs=VMEM,
        compiler_params=PARAMS,
        cost_estimate=cost(2 * out.shape[1] * share, share),
        name=name,
    )(panel, *operands)


def down_kernel(step, groups, *refs):
    hiddens = refs[:4]
    down, out, together, rows_here, sem = refs[-5:]
    place, group = lax.axis_index("tp"), lax.axis_index("grp")
    hid, rows = hiddens[0].shape
    for s, hidden in enumerate(hiddens):
        together[rows_at(lax.rem(place - s + 4, 4), hid), :] = hidden[...]
    total = lax.dot_general(
        together[...], down[...], (((0,), (0,)), ((), ())), preferred_element_type=jnp.float32
    )
    rows_here[...] = total.astype(rows_here.dtype)
    to = out.at[rows_at(lax.rem(group - step + groups, groups), rows), :]
    copy = pltpu.make_async_copy(rows_here, to, sem)
    copy.start()
    copy.wait()


def project_down(step, groups, hiddens, down, out):
    hid, rows = hiddens[0].shape
    wide = down.shape[1]
    earlier = [] if out is None else [out]
    return pl.pallas_call(
        functools.partial(down_kernel, step, groups),
        out_shape=jax.ShapeDtypeStruct((groups * rows, wide), jnp.bfloat16),
        in_specs=[VMEM] * 4 + [WHOLE] * len(earlier) + [VMEM],
        out_specs=WHOLE,
        scratch_shapes=[pltpu.VMEM((4 * hid, rows), jnp.bfloat16), pltpu.VMEM((rows, wide), jnp.bfloat16), DMA],
        input_output_aliases={4: 0} if earlier else {},
        compiler_params=PARAMS,
        cost_estimate=cost(2 * rows * down.size, down.size + rows * wide),
        name="project_down",
    )(*hiddens, *earlier, down)


def everywhere(hidden):
    return [hidden] + [lax.ppermute(hidden, "tp", [(i, (i + s) % 4) for i in range(4)]) for s in (1, 2, 3)]


def local(dispatched, route_prob, peer_rows, gate_weight, up_weight, down_weight):
    groups, blks = lax.axis_size("grp"), lax.axis_size("blk")
    per_peer = dispatched.shape[0] // groups
    hid = gate_weight.shape[2]

    rows, weight = prepare(dispatched, gate_weight[0].T, up_weight[0].T, groups)
    hops = [ring(rows[step], step) for step in range(groups)]
    opposites = [middle(choose(rows[step], *hops[step]), step) for step in range(groups)]

    scales = weigh(route_prob.reshape(groups, per_peer), peer_rows)
    for step in range(1, groups):
        block = attach(step, after(dispatched, *hops[0]), scales)
        rows[step] = lax.ppermute(block, "grp", [(i, (i + step) % groups) for i in range(groups)])

    have = {0: weight}
    bit = blks // 2
    while bit:
        for j in list(have):
            have[j ^ bit] = swap(have[j], "blk", bit)
        if bit == blks // 2:
            have[bit] = after(have[bit], *hops[0])
            have[0] = after(have[0], have[bit])
        bit //= 2
    panel = in_order([have[j] for j in range(blks)])

    sums = jax.ShapeDtypeStruct((2 * hid, per_peer), jnp.float32)
    hidden = jax.ShapeDtypeStruct((hid, per_peer), jnp.bfloat16)
    out = None
    for step, (x, (right, left), opposite) in enumerate(zip(rows, hops, opposites)):
        if step == 0:
            done = call_rows(hidden_kernel, 4, "hidden_rows", hidden, panel, right, left, x, opposite, scales)
        else:
            total = call_rows(sum_kernel, 2, "chunk_sums", sums, panel, right, left)
            done = call_rows(finish_kernel, 2, "last_chunks", hidden, panel, total, x, opposite)
        out = project_down(step, groups, everywhere(done), down_weight[0], out)
    return out


def solution(mesh):
    return jax.shard_map(
        local,
        mesh=mesh,
        in_specs=(
            P(("blk", "grp"), "tp"),
            P(("blk", "grp")),
            P(("blk", "grp")),
            P("grp", "blk", "tp"),
            P("grp", "blk", "tp"),
            P("grp", None, "tp"),
        ),
        out_specs=P(("blk", "grp"), "tp"),
        check_vma=False,
    )
```

```python
import functools

import jax
import jax.numpy as jnp
from jax import lax
from jax.experimental import pallas as pl
from jax.experimental.pallas import tpu as pltpu
from jax.sharding import PartitionSpec as P

PARAMS = pltpu.CompilerParams(vmem_limit_bytes=6 << 20)
VMEM = pl.BlockSpec(memory_space=pltpu.VMEM)
WHOLE = pl.BlockSpec(memory_space=pl.ANY)
DMA = pltpu.SemaphoreType.DMA
EXTRA = 16


def cost(flops, values, exps=0):
    return pl.CostEstimate(flops=flops, bytes_accessed=2 * values, transcendentals=exps)


def rows_at(index, size):
    return pl.ds(pl.multiple_of(index * size, size), size)


def after(x, *done):
    return lax.optimization_barrier((x, *done))[0]


def copy_all(pairs, sems):
    copies = [pltpu.make_async_copy(source, to, sems.at[i]) for i, (source, to) in enumerate(pairs)]
    for copy in copies:
        copy.start()
    for copy in copies:
        copy.wait()


def prepare_kernel(groups, tokens, gate, up, *refs):
    outs, panel, sems = refs[:groups], refs[groups], refs[groups + 1]
    group = lax.axis_index("grp")
    rows, hid = outs[0].shape[0], gate.shape[0]
    pairs = [(tokens.at[rows_at(lax.rem(group + step, groups), rows), :], out) for step, out in enumerate(outs)]
    copy_all(pairs + [(gate, panel.at[:hid, :]), (up, panel.at[hid:, :])], sems)


def prepare(tokens, gate, up, groups):
    rows, depth = tokens.shape
    hid, high = gate.shape
    *split, panel = pl.pallas_call(
        functools.partial(prepare_kernel, groups),
        out_shape=[jax.ShapeDtypeStruct((rows // groups, depth), tokens.dtype)] * groups
        + [jax.ShapeDtypeStruct((2 * hid, high), gate.dtype)],
        in_specs=[WHOLE] * 3,
        out_specs=[VMEM] * (groups + 1),
        scratch_shapes=[DMA((groups + 2,))],
        compiler_params=PARAMS,
        cost_estimate=cost(0, 2 * rows * depth + 4 * high * hid),
        name="prepare",
    )(*(pltpu.with_memory_space_constraint(x, pltpu.HBM) for x in (tokens, gate, up)))
    return split, panel


def weigh_kernel(chances, counts, out):
    group, (groups, rows) = lax.axis_index("grp"), chances.shape
    every = chances[...].astype(jnp.float32)
    line = lax.broadcasted_iota(jnp.int32, every.shape, 0)
    slot = lax.broadcasted_iota(jnp.int32, (1, rows), 1)
    for step in range(groups):
        index = lax.rem(group + step, groups)
        chance = jnp.sum(jnp.where(line == index, every, 0.0), axis=0, keepdims=True)
        out[step : step + 1, :] = jnp.where(slot < counts[index], chance, 0.0)


def weigh(chances, counts):
    return pl.pallas_call(
        weigh_kernel,
        out_shape=jax.ShapeDtypeStruct(chances.shape, jnp.float32),
        in_specs=[VMEM, pl.BlockSpec(memory_space=pltpu.SMEM)],
        out_specs=VMEM,
        compiler_params=PARAMS,
        cost_estimate=cost(0, chances.size),
        name="weigh",
    )(chances, counts)


def attach_kernel(step, tokens, scales, out, sem):
    groups, rows = scales.shape
    index = lax.rem(lax.axis_index("grp") + step, groups)
    copy = pltpu.make_async_copy(tokens.at[rows_at(index, rows), :], out.at[:rows, :], sem)
    copy.start()
    lanes = out.shape[1]
    line = jnp.concatenate([scales[step : step + 1, :], jnp.zeros((1, lanes - rows), jnp.float32)], axis=1)
    out[rows:, :] = jnp.broadcast_to(line, (EXTRA, lanes)).astype(out.dtype)
    copy.wait()


def attach(step, tokens, scales):
    groups, rows = scales.shape
    depth = tokens.shape[1]
    return pl.pallas_call(
        functools.partial(attach_kernel, step),
        out_shape=jax.ShapeDtypeStruct((rows + EXTRA, depth), tokens.dtype),
        in_specs=[WHOLE, VMEM],
        out_specs=VMEM,
        scratch_shapes=[DMA],
        compiler_params=PARAMS,
        cost_estimate=cost(0, 2 * rows * depth),
        name="attach_weights",
    )(pltpu.with_memory_space_constraint(tokens, pltpu.HBM), scales)


def order_kernel(*refs):
    blocks, panel, sems = refs[:-2], refs[-2], refs[-1]
    mine = lax.axis_index("blk")
    copy_all([(block, panel.at[jnp.bitwise_xor(mine, j)]) for j, block in enumerate(blocks)], sems)


def in_order(blocks):
    n = len(blocks)
    return pl.pallas_call(
        order_kernel,
        out_shape=jax.ShapeDtypeStruct((n, *blocks[0].shape), blocks[0].dtype),
        in_specs=[WHOLE] * n,
        out_specs=VMEM,
        scratch_shapes=[DMA((n,))],
        compiler_params=PARAMS,
        cost_estimate=cost(0, 2 * n * blocks[0].size),
        name="weights_in_order",
    )(*blocks)


def swap(x, axis, bit):
    return lax.ppermute(x, axis, [(i, i ^ bit) for i in range(lax.axis_size(axis))])


def along(step, moves, straight=()):
    groups = lax.axis_size("grp")
    pairs = []
    for g in range(groups):
        pairs += [(g * 4 + a, (g + step) % groups * 4 + b) for a, b in moves]
        pairs += [(g * 4 + a, g * 4 + b) for a, b in straight]
    return pairs


def exchange(block, step):
    return [lax.ppermute(block, ("grp", "tp"), along(step, [(i, i ^ bits) for i in range(4)])) for bits in (1, 3)]


def choose_kernel(here, inner, out):
    place = lax.axis_index("tp")
    out[...] = jnp.where(jnp.logical_or(place == 0, place == 3), here[...], inner[...])


def choose(here, inner):
    return pl.pallas_call(
        choose_kernel,
        out_shape=jax.ShapeDtypeStruct(here.shape, here.dtype),
        in_specs=[VMEM] * 2,
        out_specs=VMEM,
        compiler_params=PARAMS,
        cost_estimate=cost(8000000000, 4 * here.size),
        name="choose",
    )(here, inner)


def middle(block, step):
    return lax.ppermute(block, ("grp", "tp"), along(step, [(0, 2), (3, 1)], [(2, 3), (1, 0)]))


def product(panel, chunk, k):
    depth, high = chunk.shape[1], panel.shape[2]
    total = 0
    for i in range(depth // high):
        part = chunk[:, i * high : (i + 1) * high]
        total += lax.dot_general(
            panel[k * (depth // high) + i], part, (((1,), (1,)), ((), ())), preferred_element_type=jnp.float32
        )
    return total


def near_sum(place, panel, beside, across):
    return product(panel, beside[...], place ^ 1) + product(panel, across[...], place ^ 3)


def finish(place, panel, total, x, opposite, weight):
    total += product(panel, x, place)
    total += product(panel, opposite, place ^ 2)
    hid = total.shape[0] // 2
    gate, up = total[:hid], total[hid:]
    return gate / (1.0 + jnp.exp(-gate)) * up * weight


def hidden_kernel(panel, beside, across, x, opposite, scales, out):
    place = lax.axis_index("tp")
    total = near_sum(place, panel, beside, across)
    out[...] = finish(place, panel, total, x[...], opposite[...], scales[:1, :]).astype(out.dtype)


def sum_kernel(panel, beside, across, out):
    out[...] = near_sum(lax.axis_index("tp"), panel, beside, across)


def finish_kernel(panel, total, x, opposite, out):
    rows = out.shape[1]
    weight = x[rows : rows + 1, :rows].astype(jnp.float32)
    out[...] = finish(lax.axis_index("tp"), panel, total[...], x[:rows, :], opposite[...], weight).astype(out.dtype)


def call_rows(kernel, chunks, name, out, panel, *operands):
    share = chunks * panel.size // 4
    return pl.pallas_call(
        kernel,
        out_shape=out,
        in_specs=[VMEM] * (1 + len(operands)),
        out_specs=VMEM,
        compiler_params=PARAMS,
        cost_estimate=cost(2 * out.shape[1] * share, share),
        name=name,
    )(panel, *operands)


def down_kernel(step, groups, *refs):
    hiddens = refs[:4]
    down, out, together, rows_here, sem = refs[-5:]
    place, group = lax.axis_index("tp"), lax.axis_index("grp")
    hid, rows = hiddens[0].shape
    for s, hidden in enumerate(hiddens):
        together[rows_at(place ^ s, hid), :] = hidden[...]
    total = lax.dot_general(
        together[...], down[...], (((0,), (0,)), ((), ())), preferred_element_type=jnp.float32
    )
    rows_here[...] = total.astype(rows_here.dtype)
    to = out.at[rows_at(lax.rem(group - step + groups, groups), rows), :]
    copy = pltpu.make_async_copy(rows_here, to, sem)
    copy.start()
    copy.wait()


def project_down(step, groups, hiddens, down, out):
    hid, rows = hiddens[0].shape
    wide = down.shape[1]
    earlier = [] if out is None else [out]
    return pl.pallas_call(
        functools.partial(down_kernel, step, groups),
        out_shape=jax.ShapeDtypeStruct((groups * rows, wide), jnp.bfloat16),
        in_specs=[VMEM] * 4 + [WHOLE] * len(earlier) + [VMEM],
        out_specs=WHOLE,
        scratch_shapes=[pltpu.VMEM((4 * hid, rows), jnp.bfloat16), pltpu.VMEM((rows, wide), jnp.bfloat16), DMA],
        input_output_aliases={4: 0} if earlier else {},
        compiler_params=PARAMS,
        cost_estimate=cost(2 * rows * down.size, down.size + rows * wide),
        name="project_down",
    )(*hiddens, *earlier, down)


def everywhere(hidden):
    return [hidden] + [lax.ppermute(hidden, "tp", [(i, i ^ s) for i in range(4)]) for s in (1, 2, 3)]


def local(dispatched, route_prob, peer_rows, gate_weight, up_weight, down_weight):
    groups, blks = lax.axis_size("grp"), lax.axis_size("blk")
    per_peer = dispatched.shape[0] // groups
    hid = gate_weight.shape[2]

    rows, weight = prepare(dispatched, gate_weight[0].T, up_weight[0].T, groups)
    hops = [exchange(rows[step], step) for step in range(groups)]
    opposites = [middle(choose(rows[step], hops[step][1]), step) for step in range(groups)]

    scales = weigh(route_prob.reshape(groups, per_peer), peer_rows)
    for step in range(1, groups):
        block = attach(step, after(dispatched, *hops[0]), scales)
        rows[step] = lax.ppermute(block, "grp", [(i, (i + step) % groups) for i in range(groups)])

    have = {0: weight}
    bit = blks // 2
    while bit:
        for j in list(have):
            have[j ^ bit] = swap(have[j], "blk", bit)
        if bit == blks // 2:
            have[bit] = after(have[bit], *hops[0], *hops[-1])
            have[0] = after(have[0], have[bit])
        bit //= 2
    panel = in_order([have[j] for j in range(blks)])

    sums = jax.ShapeDtypeStruct((2 * hid, per_peer), jnp.float32)
    hidden = jax.ShapeDtypeStruct((hid, per_peer), jnp.bfloat16)
    out = None
    for step, (x, (beside, across), opposite) in enumerate(zip(rows, hops, opposites)):
        if step == 0:
            done = call_rows(hidden_kernel, 4, "hidden_rows", hidden, panel, beside, across, x, opposite, scales)
        else:
            total = call_rows(sum_kernel, 2, "chunk_sums", sums, panel, beside, across)
            done = call_rows(finish_kernel, 2, "last_chunks", hidden, panel, total, x, opposite)
        out = project_down(step, groups, everywhere(done), down_weight[0], out)
    return out


def solution(mesh):
    return jax.shard_map(
        local,
        mesh=mesh,
        in_specs=(
            P(("blk", "grp"), "tp"),
            P(("blk", "grp")),
            P(("blk", "grp")),
            P("grp", "blk", "tp"),
            P("grp", "blk", "tp"),
            P("grp", None, "tp"),
        ),
        out_specs=P(("blk", "grp"), "tp"),
        check_vma=False,
    )
```

```python
import functools

import jax
import jax.numpy as jnp
from jax import lax
from jax.experimental import pallas as pl
from jax.experimental.pallas import tpu as pltpu
from jax.sharding import PartitionSpec as P

PARAMS = pltpu.CompilerParams(vmem_limit_bytes=6 << 20)
VMEM = pl.BlockSpec(memory_space=pltpu.VMEM)
WHOLE = pl.BlockSpec(memory_space=pl.ANY)
DMA = pltpu.SemaphoreType.DMA
EXTRA = 16
DISTANCES = (0, 2, 1, 3)


def cost(flops, values, exps=0):
    return pl.CostEstimate(flops=flops, bytes_accessed=2 * values, transcendentals=exps)


def rows_at(index, size):
    return pl.ds(pl.multiple_of(index * size, size), size)


def after(x, *done):
    return lax.optimization_barrier((x, *done))[0]


def copy_all(pairs, sems):
    copies = [pltpu.make_async_copy(source, to, sems.at[i]) for i, (source, to) in enumerate(pairs)]
    for copy in copies:
        copy.start()
    for copy in copies:
        copy.wait()


def mine_kernel(tokens, out, sem):
    copy = pltpu.make_async_copy(tokens.at[rows_at(lax.axis_index("grp"), out.shape[0]), :], out, sem)
    copy.start()
    copy.wait()


def rest_kernel(groups, tokens, gate, up, first, *refs):
    outs, panel, sems = refs[: groups - 1], refs[groups - 1], refs[groups]
    group = lax.axis_index("grp")
    rows, hid = tokens.shape[0] // groups, gate.shape[0]
    pairs = [(tokens.at[rows_at(lax.rem(group + step, groups), rows), :], out) for step, out in enumerate(outs, 1)]
    copy_all(pairs + [(gate, panel.at[:hid, :]), (up, panel.at[hid:, :])], sems)


def prepare(tokens, gate, up, groups):
    rows, depth = tokens.shape
    hid, high = gate.shape
    block = jax.ShapeDtypeStruct((rows // groups, depth), tokens.dtype)
    tokens, gate, up = (pltpu.with_memory_space_constraint(x, pltpu.HBM) for x in (tokens, gate, up))
    mine = pl.pallas_call(
        mine_kernel,
        out_shape=block,
        in_specs=[WHOLE],
        out_specs=VMEM,
        scratch_shapes=[DMA],
        compiler_params=PARAMS,
        cost_estimate=cost(0, 2 * block.size),
        name="own_rows",
    )(tokens)
    *others, panel = pl.pallas_call(
        functools.partial(rest_kernel, groups),
        out_shape=[block] * (groups - 1) + [jax.ShapeDtypeStruct((2 * hid, high), gate.dtype)],
        in_specs=[WHOLE] * 4,
        out_specs=[VMEM] * groups,
        scratch_shapes=[DMA((groups + 1,))],
        compiler_params=PARAMS,
        cost_estimate=cost(0, 2 * rows * depth + 4 * high * hid),
        name="other_rows_and_weights",
    )(tokens, gate, up, mine)
    return [mine, *others], panel


def weigh_kernel(chances, counts, out):
    group, (groups, rows) = lax.axis_index("grp"), chances.shape
    every = chances[...].astype(jnp.float32)
    line = lax.broadcasted_iota(jnp.int32, every.shape, 0)
    slot = lax.broadcasted_iota(jnp.int32, (1, rows), 1)
    for step in range(groups):
        index = lax.rem(group + step, groups)
        chance = jnp.sum(jnp.where(line == index, every, 0.0), axis=0, keepdims=True)
        out[step : step + 1, :] = jnp.where(slot < counts[index], chance, 0.0)


def weigh(chances, counts):
    return pl.pallas_call(
        weigh_kernel,
        out_shape=jax.ShapeDtypeStruct(chances.shape, jnp.float32),
        in_specs=[VMEM, pl.BlockSpec(memory_space=pltpu.SMEM)],
        out_specs=VMEM,
        compiler_params=PARAMS,
        cost_estimate=cost(0, chances.size),
        name="weigh",
    )(chances, counts)


def attach_kernel(step, tokens, scales, out, sem):
    groups, rows = scales.shape
    index = lax.rem(lax.axis_index("grp") + step, groups)
    copy = pltpu.make_async_copy(tokens.at[rows_at(index, rows), :], out.at[:rows, :], sem)
    copy.start()
    lanes = out.shape[1]
    line = jnp.concatenate([scales[step : step + 1, :], jnp.zeros((1, lanes - rows), jnp.float32)], axis=1)
    out[rows:, :] = jnp.broadcast_to(line, (EXTRA, lanes)).astype(out.dtype)
    copy.wait()


def attach(step, tokens, scales):
    groups, rows = scales.shape
    depth = tokens.shape[1]
    return pl.pallas_call(
        functools.partial(attach_kernel, step),
        out_shape=jax.ShapeDtypeStruct((rows + EXTRA, depth), tokens.dtype),
        in_specs=[WHOLE, VMEM],
        out_specs=VMEM,
        scratch_shapes=[DMA],
        compiler_params=PARAMS,
        cost_estimate=cost(0, 2 * rows * depth),
        name="attach_weights",
    )(pltpu.with_memory_space_constraint(tokens, pltpu.HBM), scales)


def order_kernel(*refs):
    blocks, panel, sems = refs[:-2], refs[-2], refs[-1]
    mine = lax.axis_index("blk")
    copy_all([(block, panel.at[jnp.bitwise_xor(mine, j)]) for j, block in enumerate(blocks)], sems)


def in_order(blocks):
    n = len(blocks)
    return pl.pallas_call(
        order_kernel,
        out_shape=jax.ShapeDtypeStruct((n, *blocks[0].shape), blocks[0].dtype),
        in_specs=[WHOLE] * n,
        out_specs=VMEM,
        scratch_shapes=[DMA((n,))],
        compiler_params=PARAMS,
        cost_estimate=cost(0, 2 * n * blocks[0].size),
        name="weights_in_order",
    )(*blocks)


def swap(x, axis, bit):
    return lax.ppermute(x, axis, [(i, i ^ bit) for i in range(lax.axis_size(axis))])


def along(step, moves, straight=()):
    groups = lax.axis_size("grp")
    pairs = []
    for g in range(groups):
        pairs += [(g * 4 + a, (g + step) % groups * 4 + b) for a, b in moves]
        pairs += [(g * 4 + a, g * 4 + b) for a, b in straight]
    return pairs


def ring(block, step):
    right = lax.ppermute(block, ("grp", "tp"), along(step, [(i, (i + 1) % 4) for i in range(4)]))
    left = lax.ppermute(block, ("grp", "tp"), along(step, [(i, (i + 3) % 4) for i in range(4)]))
    return right, left


def choose_kernel(here, right, left, out):
    place = lax.axis_index("tp")
    inner = jnp.where(place == 2, right[...], left[...])
    out[...] = jnp.where(jnp.logical_or(place == 0, place == 3), here[...], inner)


def choose(here, right, left):
    return pl.pallas_call(
        choose_kernel,
        out_shape=jax.ShapeDtypeStruct(here.shape, here.dtype),
        in_specs=[VMEM] * 3,
        out_specs=VMEM,
        compiler_params=PARAMS,
        cost_estimate=cost(8000000000, 4 * here.size),
        name="choose",
    )(here, right, left)


def middle(block, step):
    return lax.ppermute(block, ("grp", "tp"), along(step, [(0, 2), (3, 1)], [(2, 3), (1, 0)]))


def product(panel, chunk, k):
    depth, high = chunk.shape[1], panel.shape[2]
    total = 0
    for i in range(depth // high):
        part = chunk[:, i * high : (i + 1) * high]
        total += lax.dot_general(
            panel[k * (depth // high) + i], part, (((1,), (1,)), ((), ())), preferred_element_type=jnp.float32
        )
    return total


def near_sum(place, panel, right, left):
    return product(panel, right[...], lax.rem(place + 3, 4)) + product(panel, left[...], lax.rem(place + 1, 4))


def finish(place, panel, total, x, opposite, weight):
    total += product(panel, x, place)
    total += product(panel, opposite, lax.rem(place + 2, 4))
    hid = total.shape[0] // 2
    gate, up = total[:hid], total[hid:]
    return gate / (1.0 + jnp.exp(-gate)) * up * weight


def hidden_kernel(panel, right, left, x, opposite, scales, out):
    place = lax.axis_index("tp")
    total = near_sum(place, panel, right, left)
    out[...] = finish(place, panel, total, x[...], opposite[...], scales[:1, :]).astype(out.dtype)


def sum_kernel(panel, right, left, out):
    out[...] = near_sum(lax.axis_index("tp"), panel, right, left)


def finish_kernel(panel, total, x, opposite, out):
    rows = out.shape[1]
    weight = x[rows : rows + 1, :rows].astype(jnp.float32)
    out[...] = finish(lax.axis_index("tp"), panel, total[...], x[:rows, :], opposite[...], weight).astype(out.dtype)


def call_rows(kernel, chunks, name, out, panel, *operands):
    share = chunks * panel.size // 4
    return pl.pallas_call(
        kernel,
        out_shape=out,
        in_specs=[VMEM] * (1 + len(operands)),
        out_specs=VMEM,
        compiler_params=PARAMS,
        cost_estimate=cost(2 * out.shape[1] * share, share),
        name=name,
    )(panel, *operands)


def down_kernel(step, groups, *refs):
    hiddens = refs[:4]
    down, out, together, rows_here, sem = refs[-5:]
    place, group = lax.axis_index("tp"), lax.axis_index("grp")
    hid, rows = hiddens[0].shape
    for s, hidden in zip(DISTANCES, hiddens):
        together[rows_at(lax.rem(place - s + 4, 4), hid), :] = hidden[...]
    total = lax.dot_general(
        together[...], down[...], (((0,), (0,)), ((), ())), preferred_element_type=jnp.float32
    )
    rows_here[...] = total.astype(rows_here.dtype)
    to = out.at[rows_at(lax.rem(group - step + groups, groups), rows), :]
    copy = pltpu.make_async_copy(rows_here, to, sem)
    copy.start()
    copy.wait()


def project_down(step, groups, hiddens, down, out):
    hid, rows = hiddens[0].shape
    wide = down.shape[1]
    earlier = [] if out is None else [out]
    return pl.pallas_call(
        functools.partial(down_kernel, step, groups),
        out_shape=jax.ShapeDtypeStruct((groups * rows, wide), jnp.bfloat16),
        in_specs=[VMEM] * 4 + [WHOLE] * len(earlier) + [VMEM],
        out_specs=WHOLE,
        scratch_shapes=[pltpu.VMEM((4 * hid, rows), jnp.bfloat16), pltpu.VMEM((rows, wide), jnp.bfloat16), DMA],
        input_output_aliases={4: 0} if earlier else {},
        compiler_params=PARAMS,
        cost_estimate=cost(2 * rows * down.size, down.size + rows * wide),
        name="project_down",
    )(*hiddens, *earlier, down)


def everywhere(hidden):
    return [lax.ppermute(hidden, "tp", [(i, (i + s) % 4) for i in range(4)]) if s else hidden for s in DISTANCES]


def local(dispatched, route_prob, peer_rows, gate_weight, up_weight, down_weight):
    groups, blks = lax.axis_size("grp"), lax.axis_size("blk")
    per_peer = dispatched.shape[0] // groups
    hid = gate_weight.shape[2]

    rows, weight = prepare(dispatched, gate_weight[0].T, up_weight[0].T, groups)
    hops = [ring(rows[step], step) for step in range(groups)]
    opposites = [middle(choose(rows[step], *hops[step]), step) for step in range(groups)]

    scales = weigh(route_prob.reshape(groups, per_peer), peer_rows)
    for step in range(1, groups):
        block = attach(step, after(dispatched, *hops[0]), scales)
        rows[step] = lax.ppermute(block, "grp", [(i, (i + step) % groups) for i in range(groups)])

    have = {0: weight}
    bit = blks // 2
    while bit:
        for j in list(have):
            have[j ^ bit] = swap(have[j], "blk", bit)
        if bit == blks // 2:
            have[bit] = after(have[bit], *hops[0])
            have[0] = after(have[0], have[bit])
        bit //= 2
    panel = in_order([have[j] for j in range(blks)])

    sums = jax.ShapeDtypeStruct((2 * hid, per_peer), jnp.float32)
    hidden = jax.ShapeDtypeStruct((hid, per_peer), jnp.bfloat16)
    out = None
    for step, (x, (right, left), opposite) in enumerate(zip(rows, hops, opposites)):
        if step == 0:
            done = call_rows(hidden_kernel, 4, "hidden_rows", hidden, panel, right, left, x, opposite, scales)
        else:
            total = call_rows(sum_kernel, 2, "chunk_sums", sums, panel, right, left)
            done = call_rows(finish_kernel, 2, "last_chunks", hidden, panel, total, x, opposite)
        out = project_down(step, groups, everywhere(done), down_weight[0], out)
    return out


def solution(mesh):
    return jax.shard_map(
        local,
        mesh=mesh,
        in_specs=(
            P(("blk", "grp"), "tp"),
            P(("blk", "grp")),
            P(("blk", "grp")),
            P("grp", "blk", "tp"),
            P("grp", "blk", "tp"),
            P("grp", None, "tp"),
        ),
        out_specs=P(("blk", "grp"), "tp"),
        check_vma=False,
    )
```

```python
import functools
import math

import jax
import jax.numpy as jnp
from jax import lax
from jax.experimental import pallas as pl
from jax.experimental.pallas import tpu as pltpu
from jax.sharding import PartitionSpec as P

PARAMS = pltpu.CompilerParams(vmem_limit_bytes=6 << 20)
VMEM = pl.BlockSpec(memory_space=pltpu.VMEM)
WHOLE = pl.BlockSpec(memory_space=pl.ANY)
DMA = pltpu.SemaphoreType.DMA
PIECES = 4
DOWN_BLOCKS = 5
EXTRA = 16
DISTANCES = (0, 2, 1, 3)


def cost(flops, values, exps=0):
    return pl.CostEstimate(flops=flops, bytes_accessed=2 * values, transcendentals=exps)


def rows_at(index, size):
    return pl.ds(pl.multiple_of(index * size, size), size)


def after(x, *done):
    return lax.optimization_barrier((x, *done))[0]


def copy_all(pairs, sems):
    copies = [pltpu.make_async_copy(source, to, sems.at[i]) for i, (source, to) in enumerate(pairs)]
    for copy in copies:
        copy.start()
    for copy in copies:
        copy.wait()


def pieces(source, to):
    rows = to.shape[0]
    count = math.gcd(rows // 16, PIECES)
    high = rows // count
    return [(source.at[i * high : (i + 1) * high, :], to.at[i * high : (i + 1) * high, :]) for i in range(count)]


def mine_kernel(tokens, out, sems):
    rows = out.shape[0]
    copy_all(pieces(tokens.at[rows_at(lax.axis_index("grp"), rows), :], out), sems)


def rest_kernel(groups, tokens, gate, up, first, *refs):
    outs, panel, sems = refs[: groups - 1], refs[groups - 1], refs[groups]
    group = lax.axis_index("grp")
    rows, hid = tokens.shape[0] // groups, gate.shape[0]
    pairs = pieces(gate, panel.at[:hid, :]) + pieces(up, panel.at[hid:, :])
    for step, out in enumerate(outs, 1):
        pairs += pieces(tokens.at[rows_at(lax.rem(group + step, groups), rows), :], out)
    copy_all(pairs, sems)


def prepare(tokens, gate, up, groups):
    rows, depth = tokens.shape
    hid, high = gate.shape
    block = jax.ShapeDtypeStruct((rows // groups, depth), tokens.dtype)
    tokens, gate, up = (pltpu.with_memory_space_constraint(x, pltpu.HBM) for x in (tokens, gate, up))
    mine = pl.pallas_call(
        mine_kernel,
        out_shape=block,
        in_specs=[WHOLE],
        out_specs=VMEM,
        scratch_shapes=[DMA((PIECES,))],
        compiler_params=PARAMS,
        cost_estimate=cost(0, 2 * block.size),
        name="own_rows",
    )(tokens)
    *others, panel = pl.pallas_call(
        functools.partial(rest_kernel, groups),
        out_shape=[block] * (groups - 1) + [jax.ShapeDtypeStruct((2 * hid, high), gate.dtype)],
        in_specs=[WHOLE] * 4,
        out_specs=[VMEM] * groups,
        scratch_shapes=[DMA(((groups + 1) * PIECES,))],
        compiler_params=PARAMS,
        cost_estimate=cost(0, 2 * rows * depth + 4 * high * hid),
        name="other_rows_and_weights",
    )(tokens, gate, up, mine)
    return [mine, *others], panel


def weigh_kernel(chances, counts, out):
    group, (groups, rows) = lax.axis_index("grp"), chances.shape
    every = chances[...].astype(jnp.float32)
    line = lax.broadcasted_iota(jnp.int32, every.shape, 0)
    slot = lax.broadcasted_iota(jnp.int32, (1, rows), 1)
    for step in range(groups):
        index = lax.rem(group + step, groups)
        chance = jnp.sum(jnp.where(line == index, every, 0.0), axis=0, keepdims=True)
        out[step : step + 1, :] = jnp.where(slot < counts[index], chance, 0.0)


def weigh(chances, counts):
    return pl.pallas_call(
        weigh_kernel,
        out_shape=jax.ShapeDtypeStruct(chances.shape, jnp.float32),
        in_specs=[VMEM, pl.BlockSpec(memory_space=pltpu.SMEM)],
        out_specs=VMEM,
        compiler_params=PARAMS,
        cost_estimate=cost(0, chances.size),
        name="weigh",
    )(chances, counts)


def attach_kernel(step, tokens, scales, out, sem):
    groups, rows = scales.shape
    index = lax.rem(lax.axis_index("grp") + step, groups)
    copy = pltpu.make_async_copy(tokens.at[rows_at(index, rows), :], out.at[:rows, :], sem)
    copy.start()
    lanes = out.shape[1]
    line = jnp.concatenate([scales[step : step + 1, :], jnp.zeros((1, lanes - rows), jnp.float32)], axis=1)
    out[rows:, :] = jnp.broadcast_to(line, (EXTRA, lanes)).astype(out.dtype)
    copy.wait()


def attach(step, tokens, scales):
    groups, rows = scales.shape
    depth = tokens.shape[1]
    return pl.pallas_call(
        functools.partial(attach_kernel, step),
        out_shape=jax.ShapeDtypeStruct((rows + EXTRA, depth), tokens.dtype),
        in_specs=[WHOLE, VMEM],
        out_specs=VMEM,
        scratch_shapes=[DMA],
        compiler_params=PARAMS,
        cost_estimate=cost(0, 2 * rows * depth),
        name="attach_weights",
    )(pltpu.with_memory_space_constraint(tokens, pltpu.HBM), scales)


def order_kernel(*refs):
    blocks, panel, sems = refs[:-2], refs[-2], refs[-1]
    mine = lax.axis_index("blk")
    copy_all([(block, panel.at[jnp.bitwise_xor(mine, j)]) for j, block in enumerate(blocks)], sems)


def in_order(blocks):
    n = len(blocks)
    return pl.pallas_call(
        order_kernel,
        out_shape=jax.ShapeDtypeStruct((n, *blocks[0].shape), blocks[0].dtype),
        in_specs=[WHOLE] * n,
        out_specs=VMEM,
        scratch_shapes=[DMA((n,))],
        compiler_params=PARAMS,
        cost_estimate=cost(0, 2 * n * blocks[0].size),
        name="weights_in_order",
    )(*blocks)


def swap(x, axis, bit):
    return lax.ppermute(x, axis, [(i, i ^ bit) for i in range(lax.axis_size(axis))])


def along(step, moves, straight=()):
    groups = lax.axis_size("grp")
    pairs = []
    for g in range(groups):
        pairs += [(g * 4 + a, (g + step) % groups * 4 + b) for a, b in moves]
        pairs += [(g * 4 + a, g * 4 + b) for a, b in straight]
    return pairs


def ring(block, step):
    right = lax.ppermute(block, ("grp", "tp"), along(step, [(i, (i + 1) % 4) for i in range(4)]))
    left = lax.ppermute(block, ("grp", "tp"), along(step, [(i, (i + 3) % 4) for i in range(4)]))
    return right, left


def choose_kernel(here, right, left, out):
    place = lax.axis_index("tp")
    inner = jnp.where(place == 2, right[...], left[...])
    out[...] = jnp.where(jnp.logical_or(place == 0, place == 3), here[...], inner)


def choose(here, right, left):
    return pl.pallas_call(
        choose_kernel,
        out_shape=jax.ShapeDtypeStruct(here.shape, here.dtype),
        in_specs=[VMEM] * 3,
        out_specs=VMEM,
        compiler_params=PARAMS,
        cost_estimate=cost(8000000000, 4 * here.size),
        name="choose",
    )(here, right, left)


def middle(block, step):
    return lax.ppermute(block, ("grp", "tp"), along(step, [(0, 2), (3, 1)], [(2, 3), (1, 0)]))


def product(panel, chunk, k):
    depth, high = chunk.shape[1], panel.shape[2]
    total = 0
    for i in range(depth // high):
        part = chunk[:, i * high : (i + 1) * high]
        total += lax.dot_general(
            panel[k * (depth // high) + i], part, (((1,), (1,)), ((), ())), preferred_element_type=jnp.float32
        )
    return total


def near_sum(place, panel, right, left):
    return product(panel, right[...], lax.rem(place + 3, 4)) + product(panel, left[...], lax.rem(place + 1, 4))


def finish(place, panel, total, x, opposite, weight):
    total += product(panel, x, place)
    total += product(panel, opposite, lax.rem(place + 2, 4))
    hid = total.shape[0] // 2
    gate, up = total[:hid], total[hid:]
    return gate / (1.0 + jnp.exp(-gate)) * up * weight


def hidden_kernel(panel, right, left, x, opposite, scales, out):
    place = lax.axis_index("tp")
    total = near_sum(place, panel, right, left)
    out[...] = finish(place, panel, total, x[...], opposite[...], scales[:1, :]).astype(out.dtype)


def sum_kernel(panel, right, left, out):
    out[...] = near_sum(lax.axis_index("tp"), panel, right, left)


def finish_kernel(panel, total, x, opposite, out):
    rows = out.shape[1]
    weight = x[rows : rows + 1, :rows].astype(jnp.float32)
    out[...] = finish(lax.axis_index("tp"), panel, total[...], x[:rows, :], opposite[...], weight).astype(out.dtype)


def call_rows(kernel, chunks, name, out, panel, *operands):
    share = chunks * panel.size // 4
    return pl.pallas_call(
        kernel,
        out_shape=out,
        in_specs=[VMEM] * (1 + len(operands)),
        out_specs=VMEM,
        compiler_params=PARAMS,
        cost_estimate=cost(2 * out.shape[1] * share, share),
        name=name,
    )(panel, *operands)


def down_kernel(step, groups, *refs):
    hiddens = refs[:4]
    down, out, together, rows_here, sems = refs[-5:]
    place, group = lax.axis_index("tp"), lax.axis_index("grp")
    hid, rows = hiddens[0].shape
    for s, hidden in zip(DISTANCES, hiddens):
        together[rows_at(lax.rem(place - s + 4, 4), hid), :] = hidden[...]
    to = rows_at(lax.rem(group - step + groups, groups), rows)
    wide = rows_here.shape[1] // DOWN_BLOCKS
    copies = []
    for i in range(DOWN_BLOCKS):
        at = slice(i * wide, (i + 1) * wide)
        total = lax.dot_general(
            together[...], down[:, at], (((0,), (0,)), ((), ())), preferred_element_type=jnp.float32
        )
        rows_here[:, at] = total.astype(rows_here.dtype)
        copies.append(pltpu.make_async_copy(rows_here.at[:, at], out.at[to, at], sems.at[i]))
        copies[-1].start()
    for copy in copies:
        copy.wait()


def project_down(step, groups, hiddens, down, out):
    hid, rows = hiddens[0].shape
    wide = down.shape[1]
    earlier = [] if out is None else [out]
    return pl.pallas_call(
        functools.partial(down_kernel, step, groups),
        out_shape=jax.ShapeDtypeStruct((groups * rows, wide), jnp.bfloat16),
        in_specs=[VMEM] * 4 + [WHOLE] * len(earlier) + [VMEM],
        out_specs=WHOLE,
        scratch_shapes=[pltpu.VMEM((4 * hid, rows), jnp.bfloat16), pltpu.VMEM((rows, wide), jnp.bfloat16), DMA((DOWN_BLOCKS,))],
        input_output_aliases={4: 0} if earlier else {},
        compiler_params=PARAMS,
        cost_estimate=cost(2 * rows * down.size, down.size + rows * wide),
        name="project_down",
    )(*hiddens, *earlier, down)


def everywhere(hidden):
    return [lax.ppermute(hidden, "tp", [(i, (i + s) % 4) for i in range(4)]) if s else hidden for s in DISTANCES]


def local(dispatched, route_prob, peer_rows, gate_weight, up_weight, down_weight):
    groups, blks = lax.axis_size("grp"), lax.axis_size("blk")
    per_peer = dispatched.shape[0] // groups
    hid = gate_weight.shape[2]

    rows, weight = prepare(dispatched, gate_weight[0].T, up_weight[0].T, groups)
    hops = [ring(rows[step], step) for step in range(groups)]
    opposites = [middle(choose(rows[step], *hops[step]), step) for step in range(groups)]

    scales = weigh(route_prob.reshape(groups, per_peer), peer_rows)
    for step in range(1, groups):
        block = attach(step, after(dispatched, *hops[0]), scales)
        rows[step] = lax.ppermute(block, "grp", [(i, (i + step) % groups) for i in range(groups)])

    have = {0: weight}
    bit = blks // 2
    while bit:
        for j in list(have):
            have[j ^ bit] = swap(have[j], "blk", bit)
        if bit == blks // 2:
            have[bit] = after(have[bit], *hops[0])
            have[0] = after(have[0], have[bit])
        bit //= 2
    panel = in_order([have[j] for j in range(blks)])

    sums = jax.ShapeDtypeStruct((2 * hid, per_peer), jnp.float32)
    hidden = jax.ShapeDtypeStruct((hid, per_peer), jnp.bfloat16)
    out = None
    for step, (x, (right, left), opposite) in enumerate(zip(rows, hops, opposites)):
        if step == 0:
            done = call_rows(hidden_kernel, 4, "hidden_rows", hidden, panel, right, left, x, opposite, scales)
        else:
            total = call_rows(sum_kernel, 2, "chunk_sums", sums, panel, right, left)
            done = call_rows(finish_kernel, 2, "last_chunks", hidden, panel, total, x, opposite)
        out = project_down(step, groups, everywhere(done), down_weight[0], out)
    return out


def solution(mesh):
    return jax.shard_map(
        local,
        mesh=mesh,
        in_specs=(
            P(("blk", "grp"), "tp"),
            P(("blk", "grp")),
            P(("blk", "grp")),
            P("grp", "blk", "tp"),
            P("grp", "blk", "tp"),
            P("grp", None, "tp"),
        ),
        out_specs=P(("blk", "grp"), "tp"),
        check_vma=False,
    )
```

```python
import functools

import jax
import jax.numpy as jnp
from jax import lax
from jax.experimental import pallas as pl
from jax.experimental.pallas import tpu as pltpu
from jax.sharding import PartitionSpec as P

PARAMS = pltpu.CompilerParams(vmem_limit_bytes=6 << 20)
VMEM = pl.BlockSpec(memory_space=pltpu.VMEM)
WHOLE = pl.BlockSpec(memory_space=pl.ANY)
DMA = pltpu.SemaphoreType.DMA
EXTRA = 16
DISTANCES = (0, 1, 3, 2)


def cost(flops, values, exps=0):
    return pl.CostEstimate(flops=flops, bytes_accessed=2 * values, transcendentals=exps)


def rows_at(index, size):
    return pl.ds(pl.multiple_of(index * size, size), size)


def after(x, *done):
    return lax.optimization_barrier((x, *done))[0]


def copy_all(pairs, sems):
    copies = [pltpu.make_async_copy(source, to, sems.at[i]) for i, (source, to) in enumerate(pairs)]
    for copy in copies:
        copy.start()
    for copy in copies:
        copy.wait()


def mine_kernel(tokens, out, sem):
    copy = pltpu.make_async_copy(tokens.at[rows_at(lax.axis_index("grp"), out.shape[0]), :], out, sem)
    copy.start()
    copy.wait()


def rest_kernel(groups, tokens, gate, up, first, *refs):
    outs, panel, sems = refs[: groups - 1], refs[groups - 1], refs[groups]
    group = lax.axis_index("grp")
    rows, hid = tokens.shape[0] // groups, gate.shape[0]
    pairs = [(tokens.at[rows_at(lax.rem(group + step, groups), rows), :], out) for step, out in enumerate(outs, 1)]
    copy_all(pairs + [(gate, panel.at[:hid, :]), (up, panel.at[hid:, :])], sems)


def prepare(tokens, gate, up, groups):
    rows, depth = tokens.shape
    hid, high = gate.shape
    block = jax.ShapeDtypeStruct((rows // groups, depth), tokens.dtype)
    tokens, gate, up = (pltpu.with_memory_space_constraint(x, pltpu.HBM) for x in (tokens, gate, up))
    mine = pl.pallas_call(
        mine_kernel,
        out_shape=block,
        in_specs=[WHOLE],
        out_specs=VMEM,
        scratch_shapes=[DMA],
        compiler_params=PARAMS,
        cost_estimate=cost(0, 2 * block.size),
        name="own_rows",
    )(tokens)
    *others, panel = pl.pallas_call(
        functools.partial(rest_kernel, groups),
        out_shape=[block] * (groups - 1) + [jax.ShapeDtypeStruct((2 * hid, high), gate.dtype)],
        in_specs=[WHOLE] * 4,
        out_specs=[VMEM] * groups,
        scratch_shapes=[DMA((groups + 1,))],
        compiler_params=PARAMS,
        cost_estimate=cost(0, 2 * rows * depth + 4 * high * hid),
        name="other_rows_and_weights",
    )(tokens, gate, up, mine)
    return [mine, *others], panel


def weigh_kernel(chances, counts, out):
    group, (groups, rows) = lax.axis_index("grp"), chances.shape
    every = chances[...].astype(jnp.float32)
    line = lax.broadcasted_iota(jnp.int32, every.shape, 0)
    slot = lax.broadcasted_iota(jnp.int32, (1, rows), 1)
    for step in range(groups):
        index = lax.rem(group + step, groups)
        chance = jnp.sum(jnp.where(line == index, every, 0.0), axis=0, keepdims=True)
        out[step : step + 1, :] = jnp.where(slot < counts[index], chance, 0.0)


def weigh(chances, counts):
    return pl.pallas_call(
        weigh_kernel,
        out_shape=jax.ShapeDtypeStruct(chances.shape, jnp.float32),
        in_specs=[VMEM, pl.BlockSpec(memory_space=pltpu.SMEM)],
        out_specs=VMEM,
        compiler_params=PARAMS,
        cost_estimate=cost(0, chances.size),
        name="weigh",
    )(chances, counts)


def attach_kernel(step, tokens, scales, out, sem):
    groups, rows = scales.shape
    index = lax.rem(lax.axis_index("grp") + step, groups)
    copy = pltpu.make_async_copy(tokens.at[rows_at(index, rows), :], out.at[:rows, :], sem)
    copy.start()
    lanes = out.shape[1]
    line = jnp.concatenate([scales[step : step + 1, :], jnp.zeros((1, lanes - rows), jnp.float32)], axis=1)
    out[rows:, :] = jnp.broadcast_to(line, (EXTRA, lanes)).astype(out.dtype)
    copy.wait()


def attach(step, tokens, scales):
    groups, rows = scales.shape
    depth = tokens.shape[1]
    return pl.pallas_call(
        functools.partial(attach_kernel, step),
        out_shape=jax.ShapeDtypeStruct((rows + EXTRA, depth), tokens.dtype),
        in_specs=[WHOLE, VMEM],
        out_specs=VMEM,
        scratch_shapes=[DMA],
        compiler_params=PARAMS,
        cost_estimate=cost(0, 2 * rows * depth),
        name="attach_weights",
    )(pltpu.with_memory_space_constraint(tokens, pltpu.HBM), scales)


def order_kernel(*refs):
    blocks, panel, sems = refs[:-2], refs[-2], refs[-1]
    mine = lax.axis_index("blk")
    copy_all([(block, panel.at[jnp.bitwise_xor(mine, j)]) for j, block in enumerate(blocks)], sems)


def in_order(blocks):
    n = len(blocks)
    return pl.pallas_call(
        order_kernel,
        out_shape=jax.ShapeDtypeStruct((n, *blocks[0].shape), blocks[0].dtype),
        in_specs=[WHOLE] * n,
        out_specs=VMEM,
        scratch_shapes=[DMA((n,))],
        compiler_params=PARAMS,
        cost_estimate=cost(0, 2 * n * blocks[0].size),
        name="weights_in_order",
    )(*blocks)


def swap(x, axis, bit):
    return lax.ppermute(x, axis, [(i, i ^ bit) for i in range(lax.axis_size(axis))])


def along(step, moves, straight=()):
    groups = lax.axis_size("grp")
    pairs = []
    for g in range(groups):
        pairs += [(g * 4 + a, (g + step) % groups * 4 + b) for a, b in moves]
        pairs += [(g * 4 + a, g * 4 + b) for a, b in straight]
    return pairs


def ring(block, step):
    right = lax.ppermute(block, ("grp", "tp"), along(step, [(i, (i + 1) % 4) for i in range(4)]))
    left = lax.ppermute(block, ("grp", "tp"), along(step, [(i, (i + 3) % 4) for i in range(4)]))
    return right, left


def choose_kernel(here, right, left, out):
    place = lax.axis_index("tp")
    inner = jnp.where(place == 2, right[...], left[...])
    out[...] = jnp.where(jnp.logical_or(place == 0, place == 3), here[...], inner)


def choose(here, right, left):
    return pl.pallas_call(
        choose_kernel,
        out_shape=jax.ShapeDtypeStruct(here.shape, here.dtype),
        in_specs=[VMEM] * 3,
        out_specs=VMEM,
        compiler_params=PARAMS,
        cost_estimate=cost(8000000000, 4 * here.size),
        name="choose",
    )(here, right, left)


def middle(block, step):
    return lax.ppermute(block, ("grp", "tp"), along(step, [(0, 2), (3, 1)], [(2, 3), (1, 0)]))


def product(panel, chunk, k):
    depth, high = chunk.shape[1], panel.shape[2]
    total = 0
    for i in range(depth // high):
        part = chunk[:, i * high : (i + 1) * high]
        total += lax.dot_general(
            panel[k * (depth // high) + i], part, (((1,), (1,)), ((), ())), preferred_element_type=jnp.float32
        )
    return total


def near_sum(place, panel, right, left):
    return product(panel, right[...], lax.rem(place + 3, 4)) + product(panel, left[...], lax.rem(place + 1, 4))


def finish(place, panel, total, x, opposite, weight):
    total += product(panel, x, place)
    total += product(panel, opposite, lax.rem(place + 2, 4))
    hid = total.shape[0] // 2
    gate, up = total[:hid], total[hid:]
    return gate / (1.0 + jnp.exp(-gate)) * up * weight


def hidden_kernel(panel, right, left, x, opposite, scales, out):
    place = lax.axis_index("tp")
    total = near_sum(place, panel, right, left)
    out[...] = finish(place, panel, total, x[...], opposite[...], scales[:1, :]).astype(out.dtype)


def sum_kernel(panel, right, left, out):
    out[...] = near_sum(lax.axis_index("tp"), panel, right, left)


def finish_kernel(groups, panel, earlier, *refs):
    out, place = refs[-1], lax.axis_index("tp")
    rows = earlier.shape[1]
    out[:, :rows] = earlier[...]
    for step in range(1, groups):
        total, x, opposite = refs[3 * step - 3 : 3 * step]
        weight = x[rows : rows + 1, :rows].astype(jnp.float32)
        done = finish(place, panel, total[...], x[:rows, :], opposite[...], weight)
        out[:, step * rows : (step + 1) * rows] = done.astype(out.dtype)


def call_rows(kernel, chunks, name, out, panel, *operands):
    share = chunks * panel.size // 4
    return pl.pallas_call(
        kernel,
        out_shape=out,
        in_specs=[VMEM] * (1 + len(operands)),
        out_specs=VMEM,
        compiler_params=PARAMS,
        cost_estimate=cost(2 * out.shape[1] * share, share),
        name=name,
    )(panel, *operands)


def down_kernel(groups, *refs):
    hiddens = refs[:4]
    down, out, together, rows_here, sems = refs[4:]
    place, group = lax.axis_index("tp"), lax.axis_index("grp")
    hid, rows = hiddens[0].shape[0], hiddens[0].shape[1] // groups
    for s, hidden in zip(DISTANCES, hiddens):
        together[rows_at(lax.rem(place - s + 4, 4), hid), :] = hidden[...]
    total = lax.dot_general(
        together[...], down[...], (((0,), (0,)), ((), ())), preferred_element_type=jnp.float32
    )
    rows_here[...] = total.astype(rows_here.dtype)
    pairs = []
    for step in range(groups):
        to = out.at[rows_at(lax.rem(group - step + groups, groups), rows), :]
        pairs.append((rows_here.at[step * rows : (step + 1) * rows, :], to))
    copy_all(pairs, sems)


def project_down(groups, hiddens, down):
    hid, rows = hiddens[0].shape
    wide = down.shape[1]
    return pl.pallas_call(
        functools.partial(down_kernel, groups),
        out_shape=jax.ShapeDtypeStruct((rows, wide), jnp.bfloat16),
        in_specs=[VMEM] * 5,
        out_specs=WHOLE,
        scratch_shapes=[pltpu.VMEM((4 * hid, rows), jnp.bfloat16), pltpu.VMEM((rows, wide), jnp.bfloat16), DMA((groups,))],
        compiler_params=PARAMS,
        cost_estimate=cost(2 * rows * down.size, down.size + rows * wide),
        name="project_down",
    )(*hiddens, down)


def everywhere(hidden):
    return [lax.ppermute(hidden, "tp", [(i, (i + s) % 4) for i in range(4)]) if s else hidden for s in DISTANCES]


def local(dispatched, route_prob, peer_rows, gate_weight, up_weight, down_weight):
    groups, blks = lax.axis_size("grp"), lax.axis_size("blk")
    per_peer = dispatched.shape[0] // groups
    hid = gate_weight.shape[2]

    rows, weight = prepare(dispatched, gate_weight[0].T, up_weight[0].T, groups)
    hops = [ring(rows[step], step) for step in range(groups)]
    opposites = [middle(choose(rows[step], *hops[step]), step) for step in range(groups)]

    scales = weigh(route_prob.reshape(groups, per_peer), peer_rows)
    for step in range(1, groups):
        block = attach(step, after(dispatched, *hops[0]), scales)
        rows[step] = lax.ppermute(block, "grp", [(i, (i + step) % groups) for i in range(groups)])

    have = {0: weight}
    bit = blks // 2
    while bit:
        for j in list(have):
            have[j ^ bit] = swap(have[j], "blk", bit)
        if bit == blks // 2:
            have[bit] = after(have[bit], *hops[0])
            have[0] = after(have[0], have[bit])
        bit //= 2
    panel = in_order([have[j] for j in range(blks)])

    sums = jax.ShapeDtypeStruct((2 * hid, per_peer), jnp.float32)
    hidden = jax.ShapeDtypeStruct((hid, per_peer), jnp.bfloat16)
    every = jax.ShapeDtypeStruct((hid, groups * per_peer), jnp.bfloat16)
    last = []
    for step in range(1, groups):
        last += [call_rows(sum_kernel, 2, "chunk_sums", sums, panel, *hops[step]), rows[step], opposites[step]]
    mine = call_rows(hidden_kernel, 4, "hidden_rows", hidden, panel, *hops[0], rows[0], opposites[0], scales)
    done = call_rows(functools.partial(finish_kernel, groups), 2, "last_chunks", every, panel, mine, *last)
    return project_down(groups, everywhere(done), down_weight[0])


def solution(mesh):
    return jax.shard_map(
        local,
        mesh=mesh,
        in_specs=(
            P(("blk", "grp"), "tp"),
            P(("blk", "grp")),
            P(("blk", "grp")),
            P("grp", "blk", "tp"),
            P("grp", "blk", "tp"),
            P("grp", None, "tp"),
        ),
        out_specs=P(("blk", "grp"), "tp"),
        check_vma=False,
    )
```

```python
import functools

import jax
import jax.numpy as jnp
from jax import lax
from jax.experimental import pallas as pl
from jax.experimental.pallas import tpu as pltpu
from jax.sharding import PartitionSpec as P

PARAMS = pltpu.CompilerParams(vmem_limit_bytes=6 << 20)
VMEM = pl.BlockSpec(memory_space=pltpu.VMEM)
WHOLE = pl.BlockSpec(memory_space=pl.ANY)
DMA = pltpu.SemaphoreType.DMA
AHEAD = 3
EXTRA = 16
DISTANCES = (0, 1, 3, 2)


def cost(flops, values, exps=0):
    return pl.CostEstimate(flops=flops, bytes_accessed=2 * values, transcendentals=exps)


def rows_at(index, size):
    return pl.ds(pl.multiple_of(index * size, size), size)


def after(x, *done):
    return lax.optimization_barrier((x, *done))[0]


def copy_all(pairs, sems):
    copies = [pltpu.make_async_copy(source, to, sems.at[i]) for i, (source, to) in enumerate(pairs)]
    for copy in copies:
        copy.start()
    for copy in copies:
        copy.wait()


def mine_kernel(tokens, out, sem):
    copy = pltpu.make_async_copy(tokens.at[rows_at(lax.axis_index("grp"), out.shape[0]), :], out, sem)
    copy.start()
    copy.wait()


def rest_kernel(groups, tokens, gate, up, first, *refs):
    outs, panel, sems = refs[: groups - 1], refs[groups - 1], refs[groups]
    group = lax.axis_index("grp")
    rows, hid = tokens.shape[0] // groups, gate.shape[0]
    pairs = [(tokens.at[rows_at(lax.rem(group + step, groups), rows), :], out) for step, out in enumerate(outs, 1)]
    copy_all(pairs + [(gate, panel.at[:hid, :]), (up, panel.at[hid:, :])], sems)


def prepare(tokens, gate, up, groups):
    rows, depth = tokens.shape
    hid, high = gate.shape
    block = jax.ShapeDtypeStruct((rows // groups, depth), tokens.dtype)
    tokens, gate, up = (pltpu.with_memory_space_constraint(x, pltpu.HBM) for x in (tokens, gate, up))
    mine = pl.pallas_call(
        mine_kernel,
        out_shape=block,
        in_specs=[WHOLE],
        out_specs=VMEM,
        scratch_shapes=[DMA],
        compiler_params=PARAMS,
        cost_estimate=cost(0, 2 * block.size),
        name="own_rows",
    )(tokens)
    *others, panel = pl.pallas_call(
        functools.partial(rest_kernel, groups),
        out_shape=[block] * (groups - 1) + [jax.ShapeDtypeStruct((2 * hid, high), gate.dtype)],
        in_specs=[WHOLE] * 4,
        out_specs=[VMEM] * groups,
        scratch_shapes=[DMA((groups + 1,))],
        compiler_params=PARAMS,
        cost_estimate=cost(0, 2 * rows * depth + 4 * high * hid),
        name="other_rows_and_weights",
    )(tokens, gate, up, mine)
    return [mine, *others], panel


def weigh_kernel(chances, counts, out):
    group, (groups, rows) = lax.axis_index("grp"), chances.shape
    every = chances[...].astype(jnp.float32)
    line = lax.broadcasted_iota(jnp.int32, every.shape, 0)
    slot = lax.broadcasted_iota(jnp.int32, (1, rows), 1)
    for step in range(groups):
        index = lax.rem(group + step, groups)
        chance = jnp.sum(jnp.where(line == index, every, 0.0), axis=0, keepdims=True)
        out[step : step + 1, :] = jnp.where(slot < counts[index], chance, 0.0)


def weigh(chances, counts):
    return pl.pallas_call(
        weigh_kernel,
        out_shape=jax.ShapeDtypeStruct(chances.shape, jnp.float32),
        in_specs=[VMEM, pl.BlockSpec(memory_space=pltpu.SMEM)],
        out_specs=VMEM,
        compiler_params=PARAMS,
        cost_estimate=cost(0, chances.size),
        name="weigh",
    )(chances, counts)


def attach_kernel(step, tokens, scales, out, sem):
    groups, rows = scales.shape
    index = lax.rem(lax.axis_index("grp") + step, groups)
    copy = pltpu.make_async_copy(tokens.at[rows_at(index, rows), :], out.at[:rows, :], sem)
    copy.start()
    lanes = out.shape[1]
    line = jnp.concatenate([scales[step : step + 1, :], jnp.zeros((1, lanes - rows), jnp.float32)], axis=1)
    out[rows:, :] = jnp.broadcast_to(line, (EXTRA, lanes)).astype(out.dtype)
    copy.wait()


def attach(step, tokens, scales):
    groups, rows = scales.shape
    depth = tokens.shape[1]
    return pl.pallas_call(
        functools.partial(attach_kernel, step),
        out_shape=jax.ShapeDtypeStruct((rows + EXTRA, depth), tokens.dtype),
        in_specs=[WHOLE, VMEM],
        out_specs=VMEM,
        scratch_shapes=[DMA],
        compiler_params=PARAMS,
        cost_estimate=cost(0, 2 * rows * depth),
        name="attach_weights",
    )(pltpu.with_memory_space_constraint(tokens, pltpu.HBM), scales)


def order_kernel(*refs):
    blocks, panel, sems = refs[:-2], refs[-2], refs[-1]
    mine = lax.axis_index("blk")
    copy_all([(block, panel.at[jnp.bitwise_xor(mine, j)]) for j, block in enumerate(blocks)], sems)


def in_order(blocks):
    n = len(blocks)
    return pl.pallas_call(
        order_kernel,
        out_shape=jax.ShapeDtypeStruct((n, *blocks[0].shape), blocks[0].dtype),
        in_specs=[WHOLE] * n,
        out_specs=VMEM,
        scratch_shapes=[DMA((n,))],
        compiler_params=PARAMS,
        cost_estimate=cost(0, 2 * n * blocks[0].size),
        name="weights_in_order",
    )(*blocks)


def swap(x, axis, bit):
    return lax.ppermute(x, axis, [(i, i ^ bit) for i in range(lax.axis_size(axis))])


def along(step, moves, straight=()):
    groups = lax.axis_size("grp")
    pairs = []
    for g in range(groups):
        pairs += [(g * 4 + a, (g + step) % groups * 4 + b) for a, b in moves]
        pairs += [(g * 4 + a, g * 4 + b) for a, b in straight]
    return pairs


def ring(block, step):
    right = lax.ppermute(block, ("grp", "tp"), along(step, [(i, (i + 1) % 4) for i in range(4)]))
    left = lax.ppermute(block, ("grp", "tp"), along(step, [(i, (i + 3) % 4) for i in range(4)]))
    return right, left


def choose_kernel(here, right, left, out):
    place = lax.axis_index("tp")
    inner = jnp.where(place == 2, right[...], left[...])
    out[...] = jnp.where(jnp.logical_or(place == 0, place == 3), here[...], inner)


def choose(here, right, left):
    return pl.pallas_call(
        choose_kernel,
        out_shape=jax.ShapeDtypeStruct(here.shape, here.dtype),
        in_specs=[VMEM] * 3,
        out_specs=VMEM,
        compiler_params=PARAMS,
        cost_estimate=cost(8000000000, 4 * here.size),
        name="choose",
    )(here, right, left)


def middle(block, step):
    return lax.ppermute(block, ("grp", "tp"), along(step, [(0, 2), (3, 1)], [(2, 3), (1, 0)]))


def product(panel, chunk, k):
    depth, high = chunk.shape[1], panel.shape[2]
    total = 0
    for i in range(depth // high):
        part = chunk[:, i * high : (i + 1) * high]
        total += lax.dot_general(
            panel[k * (depth // high) + i], part, (((1,), (1,)), ((), ())), preferred_element_type=jnp.float32
        )
    return total


def near_sum(place, panel, right, left):
    return product(panel, right[...], lax.rem(place + 3, 4)) + product(panel, left[...], lax.rem(place + 1, 4))


def finish(place, panel, total, x, opposite, weight):
    total += product(panel, x, place)
    total += product(panel, opposite, lax.rem(place + 2, 4))
    hid = total.shape[0] // 2
    gate, up = total[:hid], total[hid:]
    return gate / (1.0 + jnp.exp(-gate)) * up * weight


def hidden_kernel(panel, right, left, x, opposite, scales, out):
    place = lax.axis_index("tp")
    total = near_sum(place, panel, right, left)
    out[...] = finish(place, panel, total, x[...], opposite[...], scales[:1, :]).astype(out.dtype)


def sum_kernel(panel, right, left, out):
    out[...] = near_sum(lax.axis_index("tp"), panel, right, left)


def finish_kernel(panel, total, x, opposite, out):
    rows = out.shape[1]
    weight = x[rows : rows + 1, :rows].astype(jnp.float32)
    out[...] = finish(lax.axis_index("tp"), panel, total[...], x[:rows, :], opposite[...], weight).astype(out.dtype)


def call_rows(kernel, chunks, name, out, panel, *operands):
    share = chunks * panel.size // 4
    return pl.pallas_call(
        kernel,
        out_shape=out,
        in_specs=[VMEM] * (1 + len(operands)),
        out_specs=VMEM,
        compiler_params=PARAMS,
        cost_estimate=cost(2 * out.shape[1] * share, share),
        name=name,
    )(panel, *operands)


def down_sum(hiddens, distances, down):
    place = lax.axis_index("tp")
    hid = hiddens[0].shape[0]
    total = 0
    for hidden, s in zip(hiddens, distances):
        part = down[rows_at(lax.rem(place - s + 4, 4), hid), :]
        total += lax.dot_general(hidden[...], part, (((0,), (0,)), ((), ())), preferred_element_type=jnp.float32)
    return total


def early_kernel(distances, *refs):
    refs[-1][...] = down_sum(refs[:-2], distances, refs[-2])


def down_kernel(step, groups, distances, *refs):
    count = len(distances)
    hiddens, down = refs[:count], refs[count]
    out, rows_here, sem = refs[-3:]
    group = lax.axis_index("grp")
    rows = hiddens[0].shape[1]
    total = down_sum(hiddens, distances, down)
    if count < 4:
        total += refs[count + 1][...]
    rows_here[...] = total.astype(rows_here.dtype)
    to = out.at[rows_at(lax.rem(group - step + groups, groups), rows), :]
    copy = pltpu.make_async_copy(rows_here, to, sem)
    copy.start()
    copy.wait()


def early_sum(hiddens, distances, down):
    rows, wide = hiddens[0].shape[1], down.shape[1]
    return pl.pallas_call(
        functools.partial(early_kernel, distances),
        out_shape=jax.ShapeDtypeStruct((rows, wide), jnp.float32),
        in_specs=[VMEM] * (len(hiddens) + 1),
        out_specs=VMEM,
        compiler_params=PARAMS,
        cost_estimate=cost(0, 0),
        name="early_down",
    )(*hiddens, down)


def project_down(step, groups, hiddens, down, out, ahead):
    rows, wide = hiddens[0].shape[1], down.shape[1]
    distances = DISTANCES
    earlier = [] if out is None else [out]
    sums = []
    if ahead:
        sums = [early_sum(hiddens[:ahead], distances[:ahead], down)]
        hiddens, distances = hiddens[ahead:], distances[ahead:]
    count = len(hiddens)
    return pl.pallas_call(
        functools.partial(down_kernel, step, groups, distances),
        out_shape=jax.ShapeDtypeStruct((groups * rows, wide), jnp.bfloat16),
        in_specs=[VMEM] * (count + 1 + len(sums)) + [WHOLE] * len(earlier),
        out_specs=WHOLE,
        scratch_shapes=[pltpu.VMEM((rows, wide), jnp.bfloat16), DMA],
        input_output_aliases={count + 1 + len(sums): 0} if earlier else {},
        compiler_params=PARAMS,
        cost_estimate=cost(rows * down.size if ahead else 8000000000, down.size + rows * wide),
        name="project_down",
    )(*hiddens, down, *sums, *earlier)


def everywhere(hidden):
    return [lax.ppermute(hidden, "tp", [(i, (i + s) % 4) for i in range(4)]) if s else hidden for s in DISTANCES]


def local(dispatched, route_prob, peer_rows, gate_weight, up_weight, down_weight):
    groups, blks = lax.axis_size("grp"), lax.axis_size("blk")
    per_peer = dispatched.shape[0] // groups
    hid = gate_weight.shape[2]

    rows, weight = prepare(dispatched, gate_weight[0].T, up_weight[0].T, groups)
    hops = [ring(rows[step], step) for step in range(groups)]
    opposites = [middle(choose(rows[step], *hops[step]), step) for step in range(groups)]

    scales = weigh(route_prob.reshape(groups, per_peer), peer_rows)
    for step in range(1, groups):
        block = attach(step, after(dispatched, *hops[0]), scales)
        rows[step] = lax.ppermute(block, "grp", [(i, (i + step) % groups) for i in range(groups)])

    have = {0: weight}
    bit = blks // 2
    while bit:
        for j in list(have):
            have[j ^ bit] = swap(have[j], "blk", bit)
        if bit == blks // 2:
            have[bit] = after(have[bit], *hops[0])
            have[0] = after(have[0], have[bit])
        bit //= 2
    panel = in_order([have[j] for j in range(blks)])

    sums = jax.ShapeDtypeStruct((2 * hid, per_peer), jnp.float32)
    hidden = jax.ShapeDtypeStruct((hid, per_peer), jnp.bfloat16)
    out = None
    totals = {step: call_rows(sum_kernel, 2, "chunk_sums", sums, panel, *hops[step]) for step in range(1, groups)}
    for step, (x, (right, left), opposite) in enumerate(zip(rows, hops, opposites)):
        if step == 0:
            done = call_rows(hidden_kernel, 4, "hidden_rows", hidden, panel, right, left, x, opposite, scales)
        else:
            done = call_rows(finish_kernel, 2, "last_chunks", hidden, panel, totals[step], x, opposite)
        out = project_down(step, groups, everywhere(done), down_weight[0], out, AHEAD if step == groups - 1 else 0)
    return out


def solution(mesh):
    return jax.shard_map(
        local,
        mesh=mesh,
        in_specs=(
            P(("blk", "grp"), "tp"),
            P(("blk", "grp")),
            P(("blk", "grp")),
            P("grp", "blk", "tp"),
            P("grp", "blk", "tp"),
            P("grp", None, "tp"),
        ),
        out_specs=P(("blk", "grp"), "tp"),
        check_vma=False,
    )
```

```python
import functools

import jax
import jax.numpy as jnp
from jax import lax
from jax.experimental import pallas as pl
from jax.experimental.pallas import tpu as pltpu
from jax.sharding import PartitionSpec as P

PARAMS = pltpu.CompilerParams(vmem_limit_bytes=6 << 20)
VMEM = pl.BlockSpec(memory_space=pltpu.VMEM)
WHOLE = pl.BlockSpec(memory_space=pl.ANY)
DMA = pltpu.SemaphoreType.DMA
AHEAD = 3
EXTRA = 16
DISTANCES = (0, 1, 3, 2)


def cost(flops, values, exps=0):
    return pl.CostEstimate(flops=flops, bytes_accessed=2 * values, transcendentals=exps)


def rows_at(index, size):
    return pl.ds(pl.multiple_of(index * size, size), size)


def after(x, *done):
    return lax.optimization_barrier((x, *done))[0]


def copy_all(pairs, sems):
    copies = [pltpu.make_async_copy(source, to, sems.at[i]) for i, (source, to) in enumerate(pairs)]
    for copy in copies:
        copy.start()
    for copy in copies:
        copy.wait()


def split_kernel(tokens, *refs):
    outs, sems = refs[:-1], refs[-1]
    group, groups = lax.axis_index("grp"), len(outs)
    rows = outs[0].shape[0]
    sources = [tokens.at[rows_at(lax.rem(group + step, groups), rows), :] for step in range(groups)]
    copy_all(zip(sources, outs), sems)


def split_rows(tokens, groups):
    rows, depth = tokens.shape
    return pl.pallas_call(
        split_kernel,
        out_shape=[jax.ShapeDtypeStruct((rows // groups, depth), tokens.dtype)] * groups,
        in_specs=[WHOLE],
        out_specs=[VMEM] * groups,
        scratch_shapes=[DMA((groups,))],
        compiler_params=PARAMS,
        cost_estimate=cost(0, 2 * rows * depth),
        name="split_rows",
    )(pltpu.with_memory_space_constraint(tokens, pltpu.HBM))


def stack_kernel(gate, up, first, out, sems):
    hid = gate.shape[0]
    copy_all([(gate, out.at[:hid, :]), (up, out.at[hid:, :])], sems)


def stack(gate, up, first):
    hid, high = gate.shape
    gate, up = (pltpu.with_memory_space_constraint(x, pltpu.HBM) for x in (gate, up))
    return pl.pallas_call(
        stack_kernel,
        out_shape=jax.ShapeDtypeStruct((2 * hid, high), gate.dtype),
        in_specs=[WHOLE] * 3,
        out_specs=VMEM,
        scratch_shapes=[DMA((2,))],
        compiler_params=PARAMS,
        cost_estimate=cost(0, 4 * high * hid),
        name="gate_above_up",
    )(gate, up, first)


def weigh_kernel(chances, counts, out):
    group, (groups, rows) = lax.axis_index("grp"), chances.shape
    every = chances[...].astype(jnp.float32)
    line = lax.broadcasted_iota(jnp.int32, every.shape, 0)
    slot = lax.broadcasted_iota(jnp.int32, (1, rows), 1)
    for step in range(groups):
        index = lax.rem(group + step, groups)
        chance = jnp.sum(jnp.where(line == index, every, 0.0), axis=0, keepdims=True)
        out[step : step + 1, :] = jnp.where(slot < counts[index], chance, 0.0)


def weigh(chances, counts):
    return pl.pallas_call(
        weigh_kernel,
        out_shape=jax.ShapeDtypeStruct(chances.shape, jnp.float32),
        in_specs=[VMEM, pl.BlockSpec(memory_space=pltpu.SMEM)],
        out_specs=VMEM,
        compiler_params=PARAMS,
        cost_estimate=cost(0, chances.size),
        name="weigh",
    )(chances, counts)


def attach_kernel(step, tokens, scales, out, sem):
    groups, rows = scales.shape
    index = lax.rem(lax.axis_index("grp") + step, groups)
    copy = pltpu.make_async_copy(tokens.at[rows_at(index, rows), :], out.at[:rows, :], sem)
    copy.start()
    lanes = out.shape[1]
    line = jnp.concatenate([scales[step : step + 1, :], jnp.zeros((1, lanes - rows), jnp.float32)], axis=1)
    out[rows:, :] = jnp.broadcast_to(line, (EXTRA, lanes)).astype(out.dtype)
    copy.wait()


def attach(step, tokens, scales):
    groups, rows = scales.shape
    depth = tokens.shape[1]
    return pl.pallas_call(
        functools.partial(attach_kernel, step),
        out_shape=jax.ShapeDtypeStruct((rows + EXTRA, depth), tokens.dtype),
        in_specs=[WHOLE, VMEM],
        out_specs=VMEM,
        scratch_shapes=[DMA],
        compiler_params=PARAMS,
        cost_estimate=cost(0, 2 * rows * depth),
        name="attach_weights",
    )(pltpu.with_memory_space_constraint(tokens, pltpu.HBM), scales)


def order_kernel(*refs):
    blocks, panel, sems = refs[:-2], refs[-2], refs[-1]
    mine = lax.axis_index("blk")
    copy_all([(block, panel.at[jnp.bitwise_xor(mine, j)]) for j, block in enumerate(blocks)], sems)


def in_order(blocks):
    n = len(blocks)
    return pl.pallas_call(
        order_kernel,
        out_shape=jax.ShapeDtypeStruct((n, *blocks[0].shape), blocks[0].dtype),
        in_specs=[WHOLE] * n,
        out_specs=VMEM,
        scratch_shapes=[DMA((n,))],
        compiler_params=PARAMS,
        cost_estimate=cost(0, 2 * n * blocks[0].size),
        name="weights_in_order",
    )(*blocks)


def swap(x, axis, bit):
    return lax.ppermute(x, axis, [(i, i ^ bit) for i in range(lax.axis_size(axis))])


def along(step, moves, straight=()):
    groups = lax.axis_size("grp")
    pairs = []
    for g in range(groups):
        pairs += [(g * 4 + a, (g + step) % groups * 4 + b) for a, b in moves]
        pairs += [(g * 4 + a, g * 4 + b) for a, b in straight]
    return pairs


def ring(block, step):
    right = lax.ppermute(block, ("grp", "tp"), along(step, [(i, (i + 1) % 4) for i in range(4)]))
    left = lax.ppermute(block, ("grp", "tp"), along(step, [(i, (i + 3) % 4) for i in range(4)]))
    return right, left


def choose_kernel(here, right, left, out):
    place = lax.axis_index("tp")
    inner = jnp.where(place == 2, right[...], left[...])
    out[...] = jnp.where(jnp.logical_or(place == 0, place == 3), here[...], inner)


def choose(here, right, left):
    return pl.pallas_call(
        choose_kernel,
        out_shape=jax.ShapeDtypeStruct(here.shape, here.dtype),
        in_specs=[VMEM] * 3,
        out_specs=VMEM,
        compiler_params=PARAMS,
        cost_estimate=cost(12000000000, 4 * here.size),
        name="choose",
    )(here, right, left)


def middle(block, step):
    return lax.ppermute(block, ("grp", "tp"), along(step, [(0, 2), (3, 1)], [(2, 3), (1, 0)]))


def product(panel, chunk, k):
    depth, high = chunk.shape[1], panel.shape[2]
    total = 0
    for i in range(depth // high):
        part = chunk[:, i * high : (i + 1) * high]
        total += lax.dot_general(
            panel[k * (depth // high) + i], part, (((1,), (1,)), ((), ())), preferred_element_type=jnp.float32
        )
    return total


def near_sum(place, panel, right, left):
    return product(panel, right[...], lax.rem(place + 3, 4)) + product(panel, left[...], lax.rem(place + 1, 4))


def finish(place, panel, total, x, opposite, weight):
    total += product(panel, x, place)
    total += product(panel, opposite, lax.rem(place + 2, 4))
    hid = total.shape[0] // 2
    gate, up = total[:hid], total[hid:]
    return gate / (1.0 + jnp.exp(-gate)) * up * weight


def hidden_kernel(panel, right, left, x, opposite, scales, out):
    place = lax.axis_index("tp")
    total = near_sum(place, panel, right, left)
    out[...] = finish(place, panel, total, x[...], opposite[...], scales[:1, :]).astype(out.dtype)


def sum_kernel(panel, right, left, out):
    out[...] = near_sum(lax.axis_index("tp"), panel, right, left)


def finish_kernel(panel, total, x, opposite, out):
    rows = out.shape[1]
    weight = x[rows : rows + 1, :rows].astype(jnp.float32)
    out[...] = finish(lax.axis_index("tp"), panel, total[...], x[:rows, :], opposite[...], weight).astype(out.dtype)


def call_rows(kernel, chunks, name, out, panel, *operands):
    share = chunks * panel.size // 4
    return pl.pallas_call(
        kernel,
        out_shape=out,
        in_specs=[VMEM] * (1 + len(operands)),
        out_specs=VMEM,
        compiler_params=PARAMS,
        cost_estimate=cost(2 * out.shape[1] * share, share),
        name=name,
    )(panel, *operands)


def down_sum(hiddens, distances, down):
    place = lax.axis_index("tp")
    hid = hiddens[0].shape[0]
    total = 0
    for hidden, s in zip(hiddens, distances):
        part = down[rows_at(lax.rem(place - s + 4, 4), hid), :]
        total += lax.dot_general(hidden[...], part, (((0,), (0,)), ((), ())), preferred_element_type=jnp.float32)
    return total


def early_kernel(distances, *refs):
    refs[-1][...] = down_sum(refs[:-2], distances, refs[-2])


def down_kernel(step, groups, distances, *refs):
    count = len(distances)
    hiddens, down = refs[:count], refs[count]
    out, rows_here, sem = refs[-3:]
    group = lax.axis_index("grp")
    rows = hiddens[0].shape[1]
    total = down_sum(hiddens, distances, down)
    if count < 4:
        total += refs[count + 1][...]
    rows_here[...] = total.astype(rows_here.dtype)
    to = out.at[rows_at(lax.rem(group - step + groups, groups), rows), :]
    copy = pltpu.make_async_copy(rows_here, to, sem)
    copy.start()
    copy.wait()


def early_sum(hiddens, distances, down):
    rows, wide = hiddens[0].shape[1], down.shape[1]
    return pl.pallas_call(
        functools.partial(early_kernel, distances),
        out_shape=jax.ShapeDtypeStruct((rows, wide), jnp.float32),
        in_specs=[VMEM] * (len(hiddens) + 1),
        out_specs=VMEM,
        compiler_params=PARAMS,
        cost_estimate=cost(0, 0),
        name="early_down",
    )(*hiddens, down)


def project_down(step, groups, hiddens, down, out, ahead):
    rows, wide = hiddens[0].shape[1], down.shape[1]
    distances = DISTANCES
    earlier = [] if out is None else [out]
    sums = []
    if ahead:
        sums = [early_sum(hiddens[:ahead], distances[:ahead], down)]
        hiddens, distances = hiddens[ahead:], distances[ahead:]
    count = len(hiddens)
    return pl.pallas_call(
        functools.partial(down_kernel, step, groups, distances),
        out_shape=jax.ShapeDtypeStruct((groups * rows, wide), jnp.bfloat16),
        in_specs=[VMEM] * (count + 1 + len(sums)) + [WHOLE] * len(earlier),
        out_specs=WHOLE,
        scratch_shapes=[pltpu.VMEM((rows, wide), jnp.bfloat16), DMA],
        input_output_aliases={count + 1 + len(sums): 0} if earlier else {},
        compiler_params=PARAMS,
        cost_estimate=cost(rows * down.size if ahead else 8000000000, down.size + rows * wide),
        name="project_down",
    )(*hiddens, down, *sums, *earlier)


def everywhere(hidden):
    return [lax.ppermute(hidden, "tp", [(i, (i + s) % 4) for i in range(4)]) if s else hidden for s in DISTANCES]


def local(dispatched, route_prob, peer_rows, gate_weight, up_weight, down_weight):
    groups, blks = lax.axis_size("grp"), lax.axis_size("blk")
    per_peer = dispatched.shape[0] // groups
    hid = gate_weight.shape[2]

    rows = list(split_rows(dispatched, groups))
    hops = [ring(rows[step], step) for step in range(groups)]
    opposites = [middle(choose(rows[step], *hops[step]), step) for step in range(groups)]

    scales = weigh(route_prob.reshape(groups, per_peer), peer_rows)
    for step in range(1, groups):
        block = attach(step, after(dispatched, *hops[0]), scales)
        rows[step] = lax.ppermute(block, "grp", [(i, (i + step) % groups) for i in range(groups)])

    have = {0: stack(gate_weight[0].T, up_weight[0].T, rows[0])}
    bit = blks // 2
    while bit:
        for j in list(have):
            have[j ^ bit] = swap(have[j], "blk", bit)
        if bit == blks // 2:
            have[bit] = after(have[bit], *hops[0])
            have[0] = after(have[0], have[bit])
        bit //= 2
    panel = in_order([have[j] for j in range(blks)])

    sums = jax.ShapeDtypeStruct((2 * hid, per_peer), jnp.float32)
    hidden = jax.ShapeDtypeStruct((hid, per_peer), jnp.bfloat16)
    out = None
    totals = {step: call_rows(sum_kernel, 2, "chunk_sums", sums, panel, *hops[step]) for step in range(1, groups)}
    for step, (x, (right, left), opposite) in enumerate(zip(rows, hops, opposites)):
        if step == 0:
            done = call_rows(hidden_kernel, 4, "hidden_rows", hidden, panel, right, left, x, opposite, scales)
        else:
            done = call_rows(finish_kernel, 2, "last_chunks", hidden, panel, totals[step], x, opposite)
        out = project_down(step, groups, everywhere(done), down_weight[0], out, AHEAD if step == groups - 1 else 0)
    return out


def solution(mesh):
    return jax.shard_map(
        local,
        mesh=mesh,
        in_specs=(
            P(("blk", "grp"), "tp"),
            P(("blk", "grp")),
            P(("blk", "grp")),
            P("grp", "blk", "tp"),
            P("grp", "blk", "tp"),
            P("grp", None, "tp"),
        ),
        out_specs=P(("blk", "grp"), "tp"),
        check_vma=False,
    )
```

```python
import functools

import jax
import jax.numpy as jnp
from jax import lax
from jax.experimental import pallas as pl
from jax.experimental.pallas import tpu as pltpu
from jax.sharding import PartitionSpec as P

PARAMS = pltpu.CompilerParams(vmem_limit_bytes=6 << 20)
VMEM = pl.BlockSpec(memory_space=pltpu.VMEM)
WHOLE = pl.BlockSpec(memory_space=pl.ANY)
DMA = pltpu.SemaphoreType.DMA
AHEAD = 3
EXTRA = 16
DISTANCES = (0, 1, 3, 2)


def cost(flops, values, exps=0):
    return pl.CostEstimate(flops=flops, bytes_accessed=2 * values, transcendentals=exps)


def rows_at(index, size):
    return pl.ds(pl.multiple_of(index * size, size), size)


def after(x, *done):
    return lax.optimization_barrier((x, *done))[0]


def copy_all(pairs, sems):
    copies = [pltpu.make_async_copy(source, to, sems.at[i]) for i, (source, to) in enumerate(pairs)]
    for copy in copies:
        copy.start()
    for copy in copies:
        copy.wait()


def mine_kernel(tokens, out, sem):
    copy = pltpu.make_async_copy(tokens.at[rows_at(lax.axis_index("grp"), out.shape[0]), :], out, sem)
    copy.start()
    copy.wait()


def rest_kernel(groups, tokens, gate, up, first, *refs):
    outs, panel, sems = refs[: groups - 1], refs[groups - 1], refs[groups]
    group = lax.axis_index("grp")
    rows, hid = tokens.shape[0] // groups, gate.shape[0]
    pairs = [(tokens.at[rows_at(lax.rem(group + step, groups), rows), :], out) for step, out in enumerate(outs, 1)]
    copy_all(pairs + [(gate, panel.at[:hid, :]), (up, panel.at[hid:, :])], sems)


def prepare(tokens, gate, up, groups):
    rows, depth = tokens.shape
    hid, high = gate.shape
    block = jax.ShapeDtypeStruct((rows // groups, depth), tokens.dtype)
    tokens, gate, up = (pltpu.with_memory_space_constraint(x, pltpu.HBM) for x in (tokens, gate, up))
    mine = pl.pallas_call(
        mine_kernel,
        out_shape=block,
        in_specs=[WHOLE],
        out_specs=VMEM,
        scratch_shapes=[DMA],
        compiler_params=PARAMS,
        cost_estimate=cost(0, 2 * block.size),
        name="own_rows",
    )(tokens)
    *others, panel = pl.pallas_call(
        functools.partial(rest_kernel, groups),
        out_shape=[block] * (groups - 1) + [jax.ShapeDtypeStruct((2 * hid, high), gate.dtype)],
        in_specs=[WHOLE] * 4,
        out_specs=[VMEM] * groups,
        scratch_shapes=[DMA((groups + 1,))],
        compiler_params=PARAMS,
        cost_estimate=cost(0, 2 * rows * depth + 4 * high * hid),
        name="other_rows_and_weights",
    )(tokens, gate, up, mine)
    return [mine, *others], panel


def weigh_kernel(chances, counts, out):
    group, (groups, rows) = lax.axis_index("grp"), chances.shape
    every = chances[...].astype(jnp.float32)
    line = lax.broadcasted_iota(jnp.int32, every.shape, 0)
    slot = lax.broadcasted_iota(jnp.int32, (1, rows), 1)
    for step in range(groups):
        index = lax.rem(group + step, groups)
        chance = jnp.sum(jnp.where(line == index, every, 0.0), axis=0, keepdims=True)
        out[step : step + 1, :] = jnp.where(slot < counts[index], chance, 0.0)


def weigh(chances, counts):
    return pl.pallas_call(
        weigh_kernel,
        out_shape=jax.ShapeDtypeStruct(chances.shape, jnp.float32),
        in_specs=[VMEM, pl.BlockSpec(memory_space=pltpu.SMEM)],
        out_specs=VMEM,
        compiler_params=PARAMS,
        cost_estimate=cost(0, chances.size),
        name="weigh",
    )(chances, counts)


def attach_kernel(step, tokens, scales, out, sem):
    groups, rows = scales.shape
    index = lax.rem(lax.axis_index("grp") + step, groups)
    copy = pltpu.make_async_copy(tokens.at[rows_at(index, rows), :], out.at[:rows, :], sem)
    copy.start()
    lanes = out.shape[1]
    line = jnp.concatenate([scales[step : step + 1, :], jnp.zeros((1, lanes - rows), jnp.float32)], axis=1)
    out[rows:, :] = jnp.broadcast_to(line, (EXTRA, lanes)).astype(out.dtype)
    copy.wait()


def attach(step, tokens, scales):
    groups, rows = scales.shape
    depth = tokens.shape[1]
    return pl.pallas_call(
        functools.partial(attach_kernel, step),
        out_shape=jax.ShapeDtypeStruct((rows + EXTRA, depth), tokens.dtype),
        in_specs=[WHOLE, VMEM],
        out_specs=VMEM,
        scratch_shapes=[DMA],
        compiler_params=PARAMS,
        cost_estimate=cost(0, 2 * rows * depth),
        name="attach_weights",
    )(pltpu.with_memory_space_constraint(tokens, pltpu.HBM), scales)


def order_kernel(*refs):
    blocks, panel, sems = refs[:-2], refs[-2], refs[-1]
    mine = lax.axis_index("blk")
    copy_all([(block, panel.at[jnp.bitwise_xor(mine, j)]) for j, block in enumerate(blocks)], sems)


def in_order(blocks):
    n = len(blocks)
    return pl.pallas_call(
        order_kernel,
        out_shape=jax.ShapeDtypeStruct((n, *blocks[0].shape), blocks[0].dtype),
        in_specs=[WHOLE] * n,
        out_specs=VMEM,
        scratch_shapes=[DMA((n,))],
        compiler_params=PARAMS,
        cost_estimate=cost(0, 2 * n * blocks[0].size),
        name="weights_in_order",
    )(*blocks)


def swap(x, axis, bit):
    return lax.ppermute(x, axis, [(i, i ^ bit) for i in range(lax.axis_size(axis))])


def along(step, moves, straight=()):
    groups = lax.axis_size("grp")
    pairs = []
    for g in range(groups):
        pairs += [(g * 4 + a, (g + step) % groups * 4 + b) for a, b in moves]
        pairs += [(g * 4 + a, g * 4 + b) for a, b in straight]
    return pairs


def ring(block, step):
    right = lax.ppermute(block, ("grp", "tp"), along(step, [(i, (i + 1) % 4) for i in range(4)]))
    left = lax.ppermute(block, ("grp", "tp"), along(step, [(i, (i + 3) % 4) for i in range(4)]))
    return right, left


def choose_kernel(here, right, left, out):
    place = lax.axis_index("tp")
    inner = jnp.where(place == 2, right[...], left[...])
    out[...] = jnp.where(jnp.logical_or(place == 0, place == 3), here[...], inner)


def choose(here, right, left):
    return pl.pallas_call(
        choose_kernel,
        out_shape=jax.ShapeDtypeStruct(here.shape, here.dtype),
        in_specs=[VMEM] * 3,
        out_specs=VMEM,
        compiler_params=PARAMS,
        cost_estimate=cost(8000000000, 4 * here.size),
        name="choose",
    )(here, right, left)


def middle(block, step):
    return lax.ppermute(block, ("grp", "tp"), along(step, [(0, 2), (3, 1)], [(2, 3), (1, 0)]))


def product(panel, chunk, k):
    depth, high = chunk.shape[1], panel.shape[2]
    total = 0
    for i in range(depth // high):
        part = chunk[:, i * high : (i + 1) * high]
        total += lax.dot_general(
            panel[k * (depth // high) + i], part, (((1,), (1,)), ((), ())), preferred_element_type=jnp.float32
        )
    return total


def near_sum(place, panel, right, left):
    return product(panel, right[...], lax.rem(place + 3, 4)) + product(panel, left[...], lax.rem(place + 1, 4))


def finish(place, panel, total, x, opposite, weight):
    total += product(panel, x, place)
    total += product(panel, opposite, lax.rem(place + 2, 4))
    hid = total.shape[0] // 2
    gate, up = total[:hid], total[hid:]
    return gate / (1.0 + jnp.exp(-gate)) * up * weight


def hidden_kernel(panel, right, left, x, opposite, scales, *refs):
    place, count = lax.axis_index("tp"), len(refs) // 3
    others, out, sums = refs[: 2 * count], refs[2 * count], refs[2 * count + 1 :]
    total = near_sum(place, panel, right, left)
    out[...] = finish(place, panel, total, x[...], opposite[...], scales[:1, :]).astype(out.dtype)
    for i, to in enumerate(sums):
        to[...] = near_sum(place, panel, *others[2 * i : 2 * i + 2])


def finish_kernel(panel, total, x, opposite, out):
    rows = out.shape[1]
    weight = x[rows : rows + 1, :rows].astype(jnp.float32)
    out[...] = finish(lax.axis_index("tp"), panel, total[...], x[:rows, :], opposite[...], weight).astype(out.dtype)


def call_rows(kernel, chunks, name, outs, panel, *operands):
    share = chunks * panel.size // 4
    return pl.pallas_call(
        kernel,
        out_shape=outs,
        in_specs=[VMEM] * (1 + len(operands)),
        out_specs=[VMEM] * len(outs),
        compiler_params=PARAMS,
        cost_estimate=cost(2 * outs[0].shape[1] * share, share),
        name=name,
    )(panel, *operands)


def down_sum(hiddens, distances, down):
    place = lax.axis_index("tp")
    hid = hiddens[0].shape[0]
    total = 0
    for hidden, s in zip(hiddens, distances):
        part = down[rows_at(lax.rem(place - s + 4, 4), hid), :]
        total += lax.dot_general(hidden[...], part, (((0,), (0,)), ((), ())), preferred_element_type=jnp.float32)
    return total


def early_kernel(distances, *refs):
    refs[-1][...] = down_sum(refs[:-2], distances, refs[-2])


def down_kernel(step, groups, distances, *refs):
    count = len(distances)
    hiddens, down = refs[:count], refs[count]
    out, rows_here, sem = refs[-3:]
    group = lax.axis_index("grp")
    rows = hiddens[0].shape[1]
    total = down_sum(hiddens, distances, down)
    if count < 4:
        total += refs[count + 1][...]
    rows_here[...] = total.astype(rows_here.dtype)
    to = out.at[rows_at(lax.rem(group - step + groups, groups), rows), :]
    copy = pltpu.make_async_copy(rows_here, to, sem)
    copy.start()
    copy.wait()


def early_sum(hiddens, distances, down):
    rows, wide = hiddens[0].shape[1], down.shape[1]
    return pl.pallas_call(
        functools.partial(early_kernel, distances),
        out_shape=jax.ShapeDtypeStruct((rows, wide), jnp.float32),
        in_specs=[VMEM] * (len(hiddens) + 1),
        out_specs=VMEM,
        compiler_params=PARAMS,
        cost_estimate=cost(0, 0),
        name="early_down",
    )(*hiddens, down)


def project_down(step, groups, hiddens, down, out, ahead):
    rows, wide = hiddens[0].shape[1], down.shape[1]
    distances = DISTANCES
    earlier = [] if out is None else [out]
    sums = []
    if ahead:
        sums = [early_sum(hiddens[:ahead], distances[:ahead], down)]
        hiddens, distances = hiddens[ahead:], distances[ahead:]
    count = len(hiddens)
    return pl.pallas_call(
        functools.partial(down_kernel, step, groups, distances),
        out_shape=jax.ShapeDtypeStruct((groups * rows, wide), jnp.bfloat16),
        in_specs=[VMEM] * (count + 1 + len(sums)) + [WHOLE] * len(earlier),
        out_specs=WHOLE,
        scratch_shapes=[pltpu.VMEM((rows, wide), jnp.bfloat16), DMA],
        input_output_aliases={count + 1 + len(sums): 0} if earlier else {},
        compiler_params=PARAMS,
        cost_estimate=cost(rows * down.size if ahead else 8000000000, down.size + rows * wide),
        name="project_down",
    )(*hiddens, down, *sums, *earlier)


def everywhere(hidden):
    return [lax.ppermute(hidden, "tp", [(i, (i + s) % 4) for i in range(4)]) if s else hidden for s in DISTANCES]


def local(dispatched, route_prob, peer_rows, gate_weight, up_weight, down_weight):
    groups, blks = lax.axis_size("grp"), lax.axis_size("blk")
    per_peer = dispatched.shape[0] // groups
    hid = gate_weight.shape[2]

    rows, weight = prepare(dispatched, gate_weight[0].T, up_weight[0].T, groups)
    hops = [ring(rows[step], step) for step in range(groups)]
    opposites = [middle(choose(rows[step], *hops[step]), step) for step in range(groups)]

    scales = weigh(route_prob.reshape(groups, per_peer), peer_rows)
    for step in range(1, groups):
        block = attach(step, after(dispatched, *hops[0]), scales)
        rows[step] = lax.ppermute(block, "grp", [(i, (i + step) % groups) for i in range(groups)])

    have = {0: weight}
    bit = blks // 2
    while bit:
        for j in list(have):
            have[j ^ bit] = swap(have[j], "blk", bit)
        if bit == blks // 2:
            have[bit] = after(have[bit], *hops[0])
            have[0] = after(have[0], have[bit])
        bit //= 2
    panel = in_order([have[j] for j in range(blks)])

    sums = jax.ShapeDtypeStruct((2 * hid, per_peer), jnp.float32)
    hidden = jax.ShapeDtypeStruct((hid, per_peer), jnp.bfloat16)
    near = [chunk for hop in hops[1:] for chunk in hop]
    mine, *totals = call_rows(
        hidden_kernel, 4, "hidden_rows", [hidden] + [sums] * (groups - 1),
        panel, *hops[0], rows[0], opposites[0], scales, *near,
    )
    out = None
    for step in range(groups):
        done = mine
        if step:
            operands = totals[step - 1], rows[step], opposites[step]
            [done] = call_rows(finish_kernel, 2, "last_chunks", [hidden], panel, *operands)
        out = project_down(step, groups, everywhere(done), down_weight[0], out, AHEAD if step == groups - 1 else 0)
    return out


def solution(mesh):
    return jax.shard_map(
        local,
        mesh=mesh,
        in_specs=(
            P(("blk", "grp"), "tp"),
            P(("blk", "grp")),
            P(("blk", "grp")),
            P("grp", "blk", "tp"),
            P("grp", "blk", "tp"),
            P("grp", None, "tp"),
        ),
        out_specs=P(("blk", "grp"), "tp"),
        check_vma=False,
    )
```

```python
import functools

import jax
import jax.numpy as jnp
from jax import lax
from jax.experimental import pallas as pl
from jax.experimental.pallas import tpu as pltpu
from jax.sharding import PartitionSpec as P

PARAMS = pltpu.CompilerParams(vmem_limit_bytes=6 << 20)
VMEM = pl.BlockSpec(memory_space=pltpu.VMEM)
WHOLE = pl.BlockSpec(memory_space=pl.ANY)
DMA = pltpu.SemaphoreType.DMA
AHEAD = 3
EXTRA = 16
DISTANCES = (0, 1, 3, 2)


def cost(flops, values, exps=0):
    return pl.CostEstimate(flops=flops, bytes_accessed=2 * values, transcendentals=exps)


def rows_at(index, size):
    return pl.ds(pl.multiple_of(index * size, size), size)


def after(x, *done):
    return lax.optimization_barrier((x, *done))[0]


def copy_all(pairs, sems):
    copies = [pltpu.make_async_copy(source, to, sems.at[i]) for i, (source, to) in enumerate(pairs)]
    for copy in copies:
        copy.start()
    for copy in copies:
        copy.wait()


def split_kernel(tokens, *refs):
    outs, sems = refs[:-1], refs[-1]
    group, groups = lax.axis_index("grp"), len(outs)
    rows = outs[0].shape[0]
    sources = [tokens.at[rows_at(lax.rem(group + step, groups), rows), :] for step in range(groups)]
    copy_all(zip(sources, outs), sems)


def split_rows(tokens, groups):
    rows, depth = tokens.shape
    return pl.pallas_call(
        split_kernel,
        out_shape=[jax.ShapeDtypeStruct((rows // groups, depth), tokens.dtype)] * groups,
        in_specs=[WHOLE],
        out_specs=[VMEM] * groups,
        scratch_shapes=[DMA((groups,))],
        compiler_params=PARAMS,
        cost_estimate=cost(0, 2 * rows * depth),
        name="split_rows",
    )(pltpu.with_memory_space_constraint(tokens, pltpu.HBM))


def stack_kernel(gate, up, first, out, sems):
    hid = gate.shape[0]
    copy_all([(gate, out.at[:hid, :]), (up, out.at[hid:, :])], sems)


def stack(gate, up, first):
    hid, high = gate.shape
    gate, up = (pltpu.with_memory_space_constraint(x, pltpu.HBM) for x in (gate, up))
    return pl.pallas_call(
        stack_kernel,
        out_shape=jax.ShapeDtypeStruct((2 * hid, high), gate.dtype),
        in_specs=[WHOLE] * 3,
        out_specs=VMEM,
        scratch_shapes=[DMA((2,))],
        compiler_params=PARAMS,
        cost_estimate=cost(0, 4 * high * hid),
        name="gate_above_up",
    )(gate, up, first)


def weigh_kernel(chances, counts, out):
    group, (groups, rows) = lax.axis_index("grp"), chances.shape
    every = chances[...].astype(jnp.float32)
    line = lax.broadcasted_iota(jnp.int32, every.shape, 0)
    slot = lax.broadcasted_iota(jnp.int32, (1, rows), 1)
    for step in range(groups):
        index = lax.rem(group + step, groups)
        chance = jnp.sum(jnp.where(line == index, every, 0.0), axis=0, keepdims=True)
        out[step : step + 1, :] = jnp.where(slot < counts[index], chance, 0.0)


def weigh(chances, counts):
    return pl.pallas_call(
        weigh_kernel,
        out_shape=jax.ShapeDtypeStruct(chances.shape, jnp.float32),
        in_specs=[VMEM, pl.BlockSpec(memory_space=pltpu.SMEM)],
        out_specs=VMEM,
        compiler_params=PARAMS,
        cost_estimate=cost(0, chances.size),
        name="weigh",
    )(chances, counts)


def attach_kernel(step, tokens, scales, out, sem):
    groups, rows = scales.shape
    index = lax.rem(lax.axis_index("grp") + step, groups)
    copy = pltpu.make_async_copy(tokens.at[rows_at(index, rows), :], out.at[:rows, :], sem)
    copy.start()
    lanes = out.shape[1]
    line = jnp.concatenate([scales[step : step + 1, :], jnp.zeros((1, lanes - rows), jnp.float32)], axis=1)
    out[rows:, :] = jnp.broadcast_to(line, (EXTRA, lanes)).astype(out.dtype)
    copy.wait()


def attach(step, tokens, scales):
    groups, rows = scales.shape
    depth = tokens.shape[1]
    return pl.pallas_call(
        functools.partial(attach_kernel, step),
        out_shape=jax.ShapeDtypeStruct((rows + EXTRA, depth), tokens.dtype),
        in_specs=[WHOLE, VMEM],
        out_specs=VMEM,
        scratch_shapes=[DMA],
        compiler_params=PARAMS,
        cost_estimate=cost(0, 2 * rows * depth),
        name="attach_weights",
    )(pltpu.with_memory_space_constraint(tokens, pltpu.HBM), scales)


def order_kernel(*refs):
    blocks, panel, sems = refs[:-2], refs[-2], refs[-1]
    mine = lax.axis_index("blk")
    copy_all([(block, panel.at[jnp.bitwise_xor(mine, j)]) for j, block in enumerate(blocks)], sems)


def in_order(blocks):
    n = len(blocks)
    return pl.pallas_call(
        order_kernel,
        out_shape=jax.ShapeDtypeStruct((n, *blocks[0].shape), blocks[0].dtype),
        in_specs=[WHOLE] * n,
        out_specs=VMEM,
        scratch_shapes=[DMA((n,))],
        compiler_params=PARAMS,
        cost_estimate=cost(0, 2 * n * blocks[0].size),
        name="weights_in_order",
    )(*blocks)


def swap(x, axis, bit):
    return lax.ppermute(x, axis, [(i, i ^ bit) for i in range(lax.axis_size(axis))])


def along(step, moves, straight=()):
    groups = lax.axis_size("grp")
    pairs = []
    for g in range(groups):
        pairs += [(g * 4 + a, (g + step) % groups * 4 + b) for a, b in moves]
        pairs += [(g * 4 + a, g * 4 + b) for a, b in straight]
    return pairs


def ring(block, step):
    right = lax.ppermute(block, ("grp", "tp"), along(step, [(i, (i + 1) % 4) for i in range(4)]))
    left = lax.ppermute(block, ("grp", "tp"), along(step, [(i, (i + 3) % 4) for i in range(4)]))
    return right, left


def choose_kernel(here, right, left, out):
    place = lax.axis_index("tp")
    inner = jnp.where(place == 2, right[...], left[...])
    out[...] = jnp.where(jnp.logical_or(place == 0, place == 3), here[...], inner)


def choose(here, right, left):
    return pl.pallas_call(
        choose_kernel,
        out_shape=jax.ShapeDtypeStruct(here.shape, here.dtype),
        in_specs=[VMEM] * 3,
        out_specs=VMEM,
        compiler_params=PARAMS,
        cost_estimate=cost(8000000000, 4 * here.size),
        name="choose",
    )(here, right, left)


def middle(block, step):
    return lax.ppermute(block, ("grp", "tp"), along(step, [(0, 2), (3, 1)], [(2, 3), (1, 0)]))


def product(panel, chunk, k):
    depth, high = chunk.shape[1], panel.shape[2]
    total = 0
    for i in range(depth // high):
        part = chunk[:, i * high : (i + 1) * high]
        total += lax.dot_general(
            panel[k * (depth // high) + i], part, (((1,), (1,)), ((), ())), preferred_element_type=jnp.float32
        )
    return total


def near_sum(place, panel, right, left):
    return product(panel, right[...], lax.rem(place + 3, 4)) + product(panel, left[...], lax.rem(place + 1, 4))


def finish(place, panel, total, x, opposite, weight):
    total += product(panel, x, place)
    total += product(panel, opposite, lax.rem(place + 2, 4))
    hid = total.shape[0] // 2
    gate, up = total[:hid], total[hid:]
    return gate / (1.0 + jnp.exp(-gate)) * up * weight


def weight_of(chunk, scales, rows):
    if chunk.shape[0] == rows:
        return scales[:1, :]
    return chunk[rows : rows + 1, :rows].astype(jnp.float32)


def hidden_kernel(panel, right, left, x, opposite, scales, out):
    place, rows = lax.axis_index("tp"), out.shape[1]
    total = near_sum(place, panel, right, left)
    weight = weight_of(x, scales, rows)
    out[...] = finish(place, panel, total, x[:rows, :], opposite[...], weight).astype(out.dtype)


def sum_kernel(panel, right, left, out):
    out[...] = near_sum(lax.axis_index("tp"), panel, right, left)


def finish_kernel(panel, total, x, opposite, scales, out):
    rows = out.shape[1]
    weight = weight_of(x, scales, rows)
    out[...] = finish(lax.axis_index("tp"), panel, total[...], x[:rows, :], opposite[...], weight).astype(out.dtype)


def call_rows(kernel, chunks, name, out, panel, *operands):
    share = chunks * panel.size // 4
    return pl.pallas_call(
        kernel,
        out_shape=out,
        in_specs=[VMEM] * (1 + len(operands)),
        out_specs=VMEM,
        compiler_params=PARAMS,
        cost_estimate=cost(2 * out.shape[1] * share, share),
        name=name,
    )(panel, *operands)


def down_sum(hiddens, distances, down):
    place = lax.axis_index("tp")
    hid = hiddens[0].shape[0]
    total = 0
    for hidden, s in zip(hiddens, distances):
        part = down[rows_at(lax.rem(place - s + 4, 4), hid), :]
        total += lax.dot_general(hidden[...], part, (((0,), (0,)), ((), ())), preferred_element_type=jnp.float32)
    return total


def early_kernel(distances, *refs):
    refs[-1][...] = down_sum(refs[:-2], distances, refs[-2])


def down_kernel(step, groups, distances, *refs):
    count = len(distances)
    hiddens, down = refs[:count], refs[count]
    out, rows_here, sem = refs[-3:]
    group = lax.axis_index("grp")
    rows = hiddens[0].shape[1]
    total = down_sum(hiddens, distances, down)
    if count < 4:
        total += refs[count + 1][...]
    rows_here[...] = total.astype(rows_here.dtype)
    to = out.at[rows_at(lax.rem(group - step + groups, groups), rows), :]
    copy = pltpu.make_async_copy(rows_here, to, sem)
    copy.start()
    copy.wait()


def early_sum(hiddens, distances, down):
    rows, wide = hiddens[0].shape[1], down.shape[1]
    return pl.pallas_call(
        functools.partial(early_kernel, distances),
        out_shape=jax.ShapeDtypeStruct((rows, wide), jnp.float32),
        in_specs=[VMEM] * (len(hiddens) + 1),
        out_specs=VMEM,
        compiler_params=PARAMS,
        cost_estimate=cost(0, 0),
        name="early_down",
    )(*hiddens, down)


def project_down(step, groups, hiddens, down, out, ahead):
    rows, wide = hiddens[0].shape[1], down.shape[1]
    distances = DISTANCES
    earlier = [] if out is None else [out]
    sums = []
    if ahead:
        sums = [early_sum(hiddens[:ahead], distances[:ahead], down)]
        hiddens, distances = hiddens[ahead:], distances[ahead:]
    count = len(hiddens)
    return pl.pallas_call(
        functools.partial(down_kernel, step, groups, distances),
        out_shape=jax.ShapeDtypeStruct((groups * rows, wide), jnp.bfloat16),
        in_specs=[VMEM] * (count + 1 + len(sums)) + [WHOLE] * len(earlier),
        out_specs=WHOLE,
        scratch_shapes=[pltpu.VMEM((rows, wide), jnp.bfloat16), DMA],
        input_output_aliases={count + 1 + len(sums): 0} if earlier else {},
        compiler_params=PARAMS,
        cost_estimate=cost(rows * down.size if ahead else 8000000000, down.size + rows * wide),
        name="project_down",
    )(*hiddens, down, *sums, *earlier)


def everywhere(hidden):
    return [lax.ppermute(hidden, "tp", [(i, (i + s) % 4) for i in range(4)]) if s else hidden for s in DISTANCES]


def local(dispatched, route_prob, peer_rows, gate_weight, up_weight, down_weight):
    groups, blks = lax.axis_size("grp"), lax.axis_size("blk")
    per_peer = dispatched.shape[0] // groups
    hid = gate_weight.shape[2]

    rows = list(split_rows(dispatched, groups))
    order = list(range(1, groups)) + [0]
    hops = [ring(rows[step], step) for step in range(groups)]
    opposites = [middle(choose(rows[step], *hops[step]), step) for step in range(groups)]

    scales = weigh(route_prob.reshape(groups, per_peer), peer_rows)
    for step in range(1, groups):
        block = attach(step, after(dispatched, *hops[order[0]]), scales)
        rows[step] = lax.ppermute(block, "grp", [(i, (i + step) % groups) for i in range(groups)])

    have = {0: stack(gate_weight[0].T, up_weight[0].T, rows[0])}
    bit = blks // 2
    while bit:
        for j in list(have):
            have[j ^ bit] = swap(have[j], "blk", bit)
        if bit == blks // 2:
            have[bit] = after(have[bit], *hops[order[0]])
            have[0] = after(have[0], have[bit])
        bit //= 2
    panel = in_order([have[j] for j in range(blks)])

    sums = jax.ShapeDtypeStruct((2 * hid, per_peer), jnp.float32)
    hidden = jax.ShapeDtypeStruct((hid, per_peer), jnp.bfloat16)
    out = None
    for step in order:
        x, (right, left), opposite = rows[step], hops[step], opposites[step]
        if step != order[-1]:
            done = call_rows(hidden_kernel, 4, "hidden_rows", hidden, panel, right, left, x, opposite, scales)
        else:
            total = call_rows(sum_kernel, 2, "chunk_sums", sums, panel, right, left)
            done = call_rows(finish_kernel, 2, "last_chunks", hidden, panel, total, x, opposite, scales)
        out = project_down(step, groups, everywhere(done), down_weight[0], out, AHEAD if step == order[-1] else 0)
    return out


def solution(mesh):
    return jax.shard_map(
        local,
        mesh=mesh,
        in_specs=(
            P(("blk", "grp"), "tp"),
            P(("blk", "grp")),
            P(("blk", "grp")),
            P("grp", "blk", "tp"),
            P("grp", "blk", "tp"),
            P("grp", None, "tp"),
        ),
        out_specs=P(("blk", "grp"), "tp"),
        check_vma=False,
    )
```

```python
import functools

import jax
import jax.numpy as jnp
from jax import lax
from jax.experimental import pallas as pl
from jax.experimental.pallas import tpu as pltpu
from jax.sharding import PartitionSpec as P

PARAMS = pltpu.CompilerParams(vmem_limit_bytes=6 << 20)
VMEM = pl.BlockSpec(memory_space=pltpu.VMEM)
WHOLE = pl.BlockSpec(memory_space=pl.ANY)
DMA = pltpu.SemaphoreType.DMA
EXTRA = 16
PLACES = (0, 3, 2, 1)


def cost(flops, values, exps=0):
    return pl.CostEstimate(flops=flops, bytes_accessed=2 * values, transcendentals=exps)


def rows_at(index, size):
    return pl.ds(pl.multiple_of(index * size, size), size)


def after(x, *done):
    return lax.optimization_barrier((x, *done))[0]


def copy_all(pairs, sems):
    copies = [pltpu.make_async_copy(source, to, sems.at[i]) for i, (source, to) in enumerate(pairs)]
    for copy in copies:
        copy.start()
    for copy in copies:
        copy.wait()


def mine_kernel(tokens, out, sem):
    copy = pltpu.make_async_copy(tokens.at[rows_at(lax.axis_index("grp"), out.shape[0]), :], out, sem)
    copy.start()
    copy.wait()


def rest_kernel(groups, tokens, gate, up, first, *refs):
    outs, panel, sems = refs[: groups - 1], refs[groups - 1], refs[groups]
    group = lax.axis_index("grp")
    rows, hid = tokens.shape[0] // groups, gate.shape[0]
    pairs = [(tokens.at[rows_at(lax.rem(group + step, groups), rows), :], out) for step, out in enumerate(outs, 1)]
    copy_all(pairs + [(gate, panel.at[:hid, :]), (up, panel.at[hid:, :])], sems)


def prepare(tokens, gate, up, groups):
    rows, depth = tokens.shape
    hid, high = gate.shape
    block = jax.ShapeDtypeStruct((rows // groups, depth), tokens.dtype)
    tokens, gate, up = (pltpu.with_memory_space_constraint(x, pltpu.HBM) for x in (tokens, gate, up))
    mine = pl.pallas_call(
        mine_kernel,
        out_shape=block,
        in_specs=[WHOLE],
        out_specs=VMEM,
        scratch_shapes=[DMA],
        compiler_params=PARAMS,
        cost_estimate=cost(0, 2 * block.size),
        name="own_rows",
    )(tokens)
    *others, panel = pl.pallas_call(
        functools.partial(rest_kernel, groups),
        out_shape=[block] * (groups - 1) + [jax.ShapeDtypeStruct((2 * hid, high), gate.dtype)],
        in_specs=[WHOLE] * 4,
        out_specs=[VMEM] * groups,
        scratch_shapes=[DMA((groups + 1,))],
        compiler_params=PARAMS,
        cost_estimate=cost(0, 2 * rows * depth + 4 * high * hid),
        name="other_rows_and_weights",
    )(tokens, gate, up, mine)
    return [mine, *others], panel


def weigh_kernel(chances, counts, out):
    group, (groups, rows) = lax.axis_index("grp"), chances.shape
    every = chances[...].astype(jnp.float32)
    line = lax.broadcasted_iota(jnp.int32, every.shape, 0)
    slot = lax.broadcasted_iota(jnp.int32, (1, rows), 1)
    for step in range(groups):
        index = lax.rem(group + step, groups)
        chance = jnp.sum(jnp.where(line == index, every, 0.0), axis=0, keepdims=True)
        out[step : step + 1, :] = jnp.where(slot < counts[index], chance, 0.0)


def weigh(chances, counts):
    return pl.pallas_call(
        weigh_kernel,
        out_shape=jax.ShapeDtypeStruct(chances.shape, jnp.float32),
        in_specs=[VMEM, pl.BlockSpec(memory_space=pltpu.SMEM)],
        out_specs=VMEM,
        compiler_params=PARAMS,
        cost_estimate=cost(0, chances.size),
        name="weigh",
    )(chances, counts)


def attach_kernel(step, tokens, scales, out, sem):
    groups, rows = scales.shape
    index = lax.rem(lax.axis_index("grp") + step, groups)
    copy = pltpu.make_async_copy(tokens.at[rows_at(index, rows), :], out.at[:rows, :], sem)
    copy.start()
    lanes = out.shape[1]
    line = jnp.concatenate([scales[step : step + 1, :], jnp.zeros((1, lanes - rows), jnp.float32)], axis=1)
    out[rows:, :] = jnp.broadcast_to(line, (EXTRA, lanes)).astype(out.dtype)
    copy.wait()


def attach(step, tokens, scales):
    groups, rows = scales.shape
    depth = tokens.shape[1]
    return pl.pallas_call(
        functools.partial(attach_kernel, step),
        out_shape=jax.ShapeDtypeStruct((rows + EXTRA, depth), tokens.dtype),
        in_specs=[WHOLE, VMEM],
        out_specs=VMEM,
        scratch_shapes=[DMA],
        compiler_params=PARAMS,
        cost_estimate=cost(0, 2 * rows * depth),
        name="attach_weights",
    )(pltpu.with_memory_space_constraint(tokens, pltpu.HBM), scales)


def order_kernel(*refs):
    blocks, panel, sems = refs[:-2], refs[-2], refs[-1]
    mine = lax.axis_index("blk")
    copy_all([(block, panel.at[jnp.bitwise_xor(mine, j)]) for j, block in enumerate(blocks)], sems)


def in_order(blocks):
    n = len(blocks)
    return pl.pallas_call(
        order_kernel,
        out_shape=jax.ShapeDtypeStruct((n, *blocks[0].shape), blocks[0].dtype),
        in_specs=[WHOLE] * n,
        out_specs=VMEM,
        scratch_shapes=[DMA((n,))],
        compiler_params=PARAMS,
        cost_estimate=cost(0, 2 * n * blocks[0].size),
        name="weights_in_order",
    )(*blocks)


def swap(x, axis, bit):
    return lax.ppermute(x, axis, [(i, i ^ bit) for i in range(lax.axis_size(axis))])


def along(step, moves, straight=()):
    groups = lax.axis_size("grp")
    pairs = []
    for g in range(groups):
        pairs += [(g * 4 + a, (g + step) % groups * 4 + b) for a, b in moves]
        pairs += [(g * 4 + a, g * 4 + b) for a, b in straight]
    return pairs


def ring(block, step):
    right = lax.ppermute(block, ("grp", "tp"), along(step, [(i, (i + 1) % 4) for i in range(4)]))
    left = lax.ppermute(block, ("grp", "tp"), along(step, [(i, (i + 3) % 4) for i in range(4)]))
    return right, left


def choose_kernel(here, right, left, out):
    place = lax.axis_index("tp")
    inner = jnp.where(place == 2, right[...], left[...])
    out[...] = jnp.where(jnp.logical_or(place == 0, place == 3), here[...], inner)


def choose(here, right, left):
    return pl.pallas_call(
        choose_kernel,
        out_shape=jax.ShapeDtypeStruct(here.shape, here.dtype),
        in_specs=[VMEM] * 3,
        out_specs=VMEM,
        compiler_params=PARAMS,
        cost_estimate=cost(8000000000, 4 * here.size),
        name="choose",
    )(here, right, left)


def middle(block, step):
    return lax.ppermute(block, ("grp", "tp"), along(step, [(0, 2), (3, 1)], [(2, 3), (1, 0)]))


def product(panel, chunk, k):
    depth, high = chunk.shape[1], panel.shape[2]
    total = 0
    for i in range(depth // high):
        part = chunk[:, i * high : (i + 1) * high]
        total += lax.dot_general(
            panel[k * (depth // high) + i], part, (((1,), (1,)), ((), ())), preferred_element_type=jnp.float32
        )
    return total


def near_sum(place, panel, right, left):
    return product(panel, right[...], lax.rem(place + 3, 4)) + product(panel, left[...], lax.rem(place + 1, 4))


def finish(place, panel, total, x, opposite, weight):
    total += product(panel, x, place)
    total += product(panel, opposite, lax.rem(place + 2, 4))
    hid = total.shape[0] // 2
    gate, up = total[:hid], total[hid:]
    return gate / (1.0 + jnp.exp(-gate)) * up * weight


def hidden_kernel(panel, right, left, x, opposite, scales, *refs):
    place, count = lax.axis_index("tp"), len(refs) // 3
    others, out, sums = refs[: 2 * count], refs[2 * count], refs[2 * count + 1 :]
    total = near_sum(place, panel, right, left)
    out[...] = finish(place, panel, total, x[...], opposite[...], scales[:1, :]).astype(out.dtype)
    for i, to in enumerate(sums):
        to[...] = near_sum(place, panel, *others[2 * i : 2 * i + 2])


def finish_kernel(panel, total, x, opposite, out):
    rows = out.shape[1]
    weight = x[rows : rows + 1, :rows].astype(jnp.float32)
    out[...] = finish(lax.axis_index("tp"), panel, total[...], x[:rows, :], opposite[...], weight).astype(out.dtype)


def call_rows(kernel, chunks, name, outs, panel, *operands):
    share = chunks * panel.size // 4
    return pl.pallas_call(
        kernel,
        out_shape=outs,
        in_specs=[VMEM] * (1 + len(operands)),
        out_specs=[VMEM] * len(outs),
        compiler_params=PARAMS,
        cost_estimate=cost(2 * outs[0].shape[1] * share, share),
        name=name,
    )(panel, *operands)


def down_kernel(step, groups, *refs):
    hiddens = refs[:4]
    down, out, together, rows_here, sem = refs[-5:]
    place, group = lax.axis_index("tp"), lax.axis_index("grp")
    hid, rows = hiddens[0].shape
    for bits, hidden in zip(PLACES, hiddens):
        together[rows_at(place ^ bits, hid), :] = hidden[...]
    total = lax.dot_general(
        together[...], down[...], (((0,), (0,)), ((), ())), preferred_element_type=jnp.float32
    )
    rows_here[...] = total.astype(rows_here.dtype)
    to = out.at[rows_at(lax.rem(group - step + groups, groups), rows), :]
    copy = pltpu.make_async_copy(rows_here, to, sem)
    copy.start()
    copy.wait()


def project_down(step, groups, hiddens, down, out):
    hid, rows = hiddens[0].shape
    wide = down.shape[1]
    earlier = [] if out is None else [out]
    return pl.pallas_call(
        functools.partial(down_kernel, step, groups),
        out_shape=jax.ShapeDtypeStruct((groups * rows, wide), jnp.bfloat16),
        in_specs=[VMEM] * 4 + [WHOLE] * len(earlier) + [VMEM],
        out_specs=WHOLE,
        scratch_shapes=[pltpu.VMEM((4 * hid, rows), jnp.bfloat16), pltpu.VMEM((rows, wide), jnp.bfloat16), DMA],
        input_output_aliases={4: 0} if earlier else {},
        compiler_params=PARAMS,
        cost_estimate=cost(2 * rows * down.size, down.size + rows * wide),
        name="project_down",
    )(*hiddens, *earlier, down)


def everywhere(hidden):
    return [swap(hidden, "tp", bits) if bits else hidden for bits in PLACES]


def local(dispatched, route_prob, peer_rows, gate_weight, up_weight, down_weight):
    groups, blks = lax.axis_size("grp"), lax.axis_size("blk")
    per_peer = dispatched.shape[0] // groups
    hid = gate_weight.shape[2]

    rows, weight = prepare(dispatched, gate_weight[0].T, up_weight[0].T, groups)
    hops = [ring(rows[step], step) for step in range(groups)]
    opposites = [middle(choose(rows[step], *hops[step]), step) for step in range(groups)]

    scales = weigh(route_prob.reshape(groups, per_peer), peer_rows)
    for step in range(1, groups):
        block = attach(step, after(dispatched, *hops[0]), scales)
        rows[step] = lax.ppermute(block, "grp", [(i, (i + step) % groups) for i in range(groups)])

    have = {0: weight}
    bit = blks // 2
    while bit:
        for j in list(have):
            have[j ^ bit] = swap(have[j], "blk", bit)
        if bit == blks // 2:
            have[bit] = after(have[bit], *hops[0])
            have[0] = after(have[0], have[bit])
        bit //= 2
    panel = in_order([have[j] for j in range(blks)])

    sums = jax.ShapeDtypeStruct((2 * hid, per_peer), jnp.float32)
    hidden = jax.ShapeDtypeStruct((hid, per_peer), jnp.bfloat16)
    near = [chunk for hop in hops[1:] for chunk in hop]
    mine, *totals = call_rows(
        hidden_kernel, 4, "hidden_rows", [hidden] + [sums] * (groups - 1),
        panel, *hops[0], rows[0], opposites[0], scales, *near,
    )
    out = None
    for step in range(groups):
        done = mine
        if step:
            operands = totals[step - 1], rows[step], opposites[step]
            [done] = call_rows(finish_kernel, 2, "last_chunks", [hidden], panel, *operands)
        out = project_down(step, groups, everywhere(done), down_weight[0], out)
    return out


def solution(mesh):
    return jax.shard_map(
        local,
        mesh=mesh,
        in_specs=(
            P(("blk", "grp"), "tp"),
            P(("blk", "grp")),
            P(("blk", "grp")),
            P("grp", "blk", "tp"),
            P("grp", "blk", "tp"),
            P("grp", None, "tp"),
        ),
        out_specs=P(("blk", "grp"), "tp"),
        check_vma=False,
    )
```

```python
import functools

import jax
import jax.numpy as jnp
from jax import lax
from jax.experimental import pallas as pl
from jax.experimental.pallas import tpu as pltpu
from jax.sharding import PartitionSpec as P

PARAMS = pltpu.CompilerParams(vmem_limit_bytes=6 << 20)
VMEM = pl.BlockSpec(memory_space=pltpu.VMEM)
WHOLE = pl.BlockSpec(memory_space=pl.ANY)
DMA = pltpu.SemaphoreType.DMA
EXTRA = 16
FAR_FIRST, NEAR_FIRST = (0, 3, 2, 1), (0, 1, 2, 3)


def cost(flops, values, exps=0):
    return pl.CostEstimate(flops=flops, bytes_accessed=2 * values, transcendentals=exps)


def rows_at(index, size):
    return pl.ds(pl.multiple_of(index * size, size), size)


def after(x, *done):
    return lax.optimization_barrier((x, *done))[0]


def copy_all(pairs, sems):
    copies = [pltpu.make_async_copy(source, to, sems.at[i]) for i, (source, to) in enumerate(pairs)]
    for copy in copies:
        copy.start()
    for copy in copies:
        copy.wait()


def mine_kernel(tokens, out, sem):
    copy = pltpu.make_async_copy(tokens.at[rows_at(lax.axis_index("grp"), out.shape[0]), :], out, sem)
    copy.start()
    copy.wait()


def rest_kernel(groups, tokens, gate, up, first, *refs):
    outs, panel, sems = refs[: groups - 1], refs[groups - 1], refs[groups]
    group = lax.axis_index("grp")
    rows, hid = tokens.shape[0] // groups, gate.shape[0]
    pairs = [(tokens.at[rows_at(lax.rem(group + step, groups), rows), :], out) for step, out in enumerate(outs, 1)]
    copy_all(pairs + [(gate, panel.at[:hid, :]), (up, panel.at[hid:, :])], sems)


def prepare(tokens, gate, up, groups):
    rows, depth = tokens.shape
    hid, high = gate.shape
    block = jax.ShapeDtypeStruct((rows // groups, depth), tokens.dtype)
    tokens, gate, up = (pltpu.with_memory_space_constraint(x, pltpu.HBM) for x in (tokens, gate, up))
    mine = pl.pallas_call(
        mine_kernel,
        out_shape=block,
        in_specs=[WHOLE],
        out_specs=VMEM,
        scratch_shapes=[DMA],
        compiler_params=PARAMS,
        cost_estimate=cost(0, 2 * block.size),
        name="own_rows",
    )(tokens)
    *others, panel = pl.pallas_call(
        functools.partial(rest_kernel, groups),
        out_shape=[block] * (groups - 1) + [jax.ShapeDtypeStruct((2 * hid, high), gate.dtype)],
        in_specs=[WHOLE] * 4,
        out_specs=[VMEM] * groups,
        scratch_shapes=[DMA((groups + 1,))],
        compiler_params=PARAMS,
        cost_estimate=cost(0, 2 * rows * depth + 4 * high * hid),
        name="other_rows_and_weights",
    )(tokens, gate, up, mine)
    return [mine, *others], panel


def weigh_kernel(chances, counts, out):
    group, (groups, rows) = lax.axis_index("grp"), chances.shape
    every = chances[...].astype(jnp.float32)
    line = lax.broadcasted_iota(jnp.int32, every.shape, 0)
    slot = lax.broadcasted_iota(jnp.int32, (1, rows), 1)
    for step in range(groups):
        index = lax.rem(group + step, groups)
        chance = jnp.sum(jnp.where(line == index, every, 0.0), axis=0, keepdims=True)
        out[step : step + 1, :] = jnp.where(slot < counts[index], chance, 0.0)


def weigh(chances, counts):
    return pl.pallas_call(
        weigh_kernel,
        out_shape=jax.ShapeDtypeStruct(chances.shape, jnp.float32),
        in_specs=[VMEM, pl.BlockSpec(memory_space=pltpu.SMEM)],
        out_specs=VMEM,
        compiler_params=PARAMS,
        cost_estimate=cost(0, chances.size),
        name="weigh",
    )(chances, counts)


def attach_kernel(step, tokens, scales, out, sem):
    groups, rows = scales.shape
    index = lax.rem(lax.axis_index("grp") + step, groups)
    copy = pltpu.make_async_copy(tokens.at[rows_at(index, rows), :], out.at[:rows, :], sem)
    copy.start()
    lanes = out.shape[1]
    line = jnp.concatenate([scales[step : step + 1, :], jnp.zeros((1, lanes - rows), jnp.float32)], axis=1)
    out[rows:, :] = jnp.broadcast_to(line, (EXTRA, lanes)).astype(out.dtype)
    copy.wait()


def attach(step, tokens, scales):
    groups, rows = scales.shape
    depth = tokens.shape[1]
    return pl.pallas_call(
        functools.partial(attach_kernel, step),
        out_shape=jax.ShapeDtypeStruct((rows + EXTRA, depth), tokens.dtype),
        in_specs=[WHOLE, VMEM],
        out_specs=VMEM,
        scratch_shapes=[DMA],
        compiler_params=PARAMS,
        cost_estimate=cost(0, 2 * rows * depth),
        name="attach_weights",
    )(pltpu.with_memory_space_constraint(tokens, pltpu.HBM), scales)


def order_kernel(*refs):
    blocks, panel, sems = refs[:-2], refs[-2], refs[-1]
    mine = lax.axis_index("blk")
    copy_all([(block, panel.at[jnp.bitwise_xor(mine, j)]) for j, block in enumerate(blocks)], sems)


def in_order(blocks):
    n = len(blocks)
    return pl.pallas_call(
        order_kernel,
        out_shape=jax.ShapeDtypeStruct((n, *blocks[0].shape), blocks[0].dtype),
        in_specs=[WHOLE] * n,
        out_specs=VMEM,
        scratch_shapes=[DMA((n,))],
        compiler_params=PARAMS,
        cost_estimate=cost(0, 2 * n * blocks[0].size),
        name="weights_in_order",
    )(*blocks)


def swap(x, axis, bit):
    return lax.ppermute(x, axis, [(i, i ^ bit) for i in range(lax.axis_size(axis))])


def along(step, moves, straight=()):
    groups = lax.axis_size("grp")
    pairs = []
    for g in range(groups):
        pairs += [(g * 4 + a, (g + step) % groups * 4 + b) for a, b in moves]
        pairs += [(g * 4 + a, g * 4 + b) for a, b in straight]
    return pairs


def ring(block, step):
    right = lax.ppermute(block, ("grp", "tp"), along(step, [(i, (i + 1) % 4) for i in range(4)]))
    left = lax.ppermute(block, ("grp", "tp"), along(step, [(i, (i + 3) % 4) for i in range(4)]))
    return right, left


def choose_kernel(here, right, left, out):
    place = lax.axis_index("tp")
    inner = jnp.where(place == 2, right[...], left[...])
    out[...] = jnp.where(jnp.logical_or(place == 0, place == 3), here[...], inner)


def choose(here, right, left):
    return pl.pallas_call(
        choose_kernel,
        out_shape=jax.ShapeDtypeStruct(here.shape, here.dtype),
        in_specs=[VMEM] * 3,
        out_specs=VMEM,
        compiler_params=PARAMS,
        cost_estimate=cost(8000000000, 4 * here.size),
        name="choose",
    )(here, right, left)


def middle(block, step):
    return lax.ppermute(block, ("grp", "tp"), along(step, [(0, 2), (3, 1)], [(2, 3), (1, 0)]))


def product(panel, chunk, k):
    depth, high = chunk.shape[1], panel.shape[2]
    total = 0
    for i in range(depth // high):
        part = chunk[:, i * high : (i + 1) * high]
        total += lax.dot_general(
            panel[k * (depth // high) + i], part, (((1,), (1,)), ((), ())), preferred_element_type=jnp.float32
        )
    return total


def near_sum(place, panel, right, left):
    return product(panel, right[...], lax.rem(place + 3, 4)) + product(panel, left[...], lax.rem(place + 1, 4))


def finish(place, panel, total, x, opposite, weight):
    total += product(panel, x, place)
    total += product(panel, opposite, lax.rem(place + 2, 4))
    hid = total.shape[0] // 2
    gate, up = total[:hid], total[hid:]
    return gate / (1.0 + jnp.exp(-gate)) * up * weight


def hidden_kernel(panel, right, left, x, opposite, scales, *refs):
    place, count = lax.axis_index("tp"), len(refs) // 3
    others, out, sums = refs[: 2 * count], refs[2 * count], refs[2 * count + 1 :]
    total = near_sum(place, panel, right, left)
    out[...] = finish(place, panel, total, x[...], opposite[...], scales[:1, :]).astype(out.dtype)
    for i, to in enumerate(sums):
        to[...] = near_sum(place, panel, *others[2 * i : 2 * i + 2])


def finish_kernel(panel, total, x, opposite, out):
    rows = out.shape[1]
    weight = x[rows : rows + 1, :rows].astype(jnp.float32)
    out[...] = finish(lax.axis_index("tp"), panel, total[...], x[:rows, :], opposite[...], weight).astype(out.dtype)


def call_rows(kernel, chunks, name, outs, panel, *operands):
    share = chunks * panel.size // 4
    return pl.pallas_call(
        kernel,
        out_shape=outs,
        in_specs=[VMEM] * (1 + len(operands)),
        out_specs=[VMEM] * len(outs),
        compiler_params=PARAMS,
        cost_estimate=cost(2 * outs[0].shape[1] * share, share),
        name=name,
    )(panel, *operands)


def down_kernel(step, groups, places, *refs):
    hiddens = refs[:4]
    down, out, together, rows_here, sem = refs[-5:]
    place, group = lax.axis_index("tp"), lax.axis_index("grp")
    hid, rows = hiddens[0].shape
    for bits, hidden in zip(places, hiddens):
        together[rows_at(place ^ bits, hid), :] = hidden[...]
    total = lax.dot_general(
        together[...], down[...], (((0,), (0,)), ((), ())), preferred_element_type=jnp.float32
    )
    rows_here[...] = total.astype(rows_here.dtype)
    to = out.at[rows_at(lax.rem(group - step + groups, groups), rows), :]
    copy = pltpu.make_async_copy(rows_here, to, sem)
    copy.start()
    copy.wait()


def project_down(step, groups, places, hiddens, down, out):
    hid, rows = hiddens[0].shape
    wide = down.shape[1]
    earlier = [] if out is None else [out]
    return pl.pallas_call(
        functools.partial(down_kernel, step, groups, places),
        out_shape=jax.ShapeDtypeStruct((groups * rows, wide), jnp.bfloat16),
        in_specs=[VMEM] * 4 + [WHOLE] * len(earlier) + [VMEM],
        out_specs=WHOLE,
        scratch_shapes=[pltpu.VMEM((4 * hid, rows), jnp.bfloat16), pltpu.VMEM((rows, wide), jnp.bfloat16), DMA],
        input_output_aliases={4: 0} if earlier else {},
        compiler_params=PARAMS,
        cost_estimate=cost(2 * rows * down.size, down.size + rows * wide),
        name="project_down",
    )(*hiddens, *earlier, down)


def everywhere(hidden, places):
    return [swap(hidden, "tp", bits) if bits else hidden for bits in places]


def local(dispatched, route_prob, peer_rows, gate_weight, up_weight, down_weight):
    groups, blks = lax.axis_size("grp"), lax.axis_size("blk")
    per_peer = dispatched.shape[0] // groups
    hid = gate_weight.shape[2]

    rows, weight = prepare(dispatched, gate_weight[0].T, up_weight[0].T, groups)
    hops = [ring(rows[step], step) for step in range(groups)]
    opposites = [middle(choose(rows[step], *hops[step]), step) for step in range(groups)]

    scales = weigh(route_prob.reshape(groups, per_peer), peer_rows)
    for step in range(1, groups):
        block = attach(step, after(dispatched, *hops[0]), scales)
        rows[step] = lax.ppermute(block, "grp", [(i, (i + step) % groups) for i in range(groups)])

    have = {0: weight}
    bit = blks // 2
    while bit:
        for j in list(have):
            have[j ^ bit] = swap(have[j], "blk", bit)
        if bit == blks // 2:
            have[bit] = after(have[bit], *hops[0])
            have[0] = after(have[0], have[bit])
        bit //= 2
    panel = in_order([have[j] for j in range(blks)])

    sums = jax.ShapeDtypeStruct((2 * hid, per_peer), jnp.float32)
    hidden = jax.ShapeDtypeStruct((hid, per_peer), jnp.bfloat16)
    near = [chunk for hop in hops[1:] for chunk in hop]
    mine, *totals = call_rows(
        hidden_kernel, 4, "hidden_rows", [hidden] + [sums] * (groups - 1),
        panel, *hops[0], rows[0], opposites[0], scales, *near,
    )
    out = None
    for step in range(groups):
        done = mine
        if step:
            operands = totals[step - 1], rows[step], opposites[step]
            [done] = call_rows(finish_kernel, 2, "last_chunks", [hidden], panel, *operands)
        places = FAR_FIRST if step == groups - 1 else NEAR_FIRST
        out = project_down(step, groups, places, everywhere(done, places), down_weight[0], out)
    return out


def solution(mesh):
    return jax.shard_map(
        local,
        mesh=mesh,
        in_specs=(
            P(("blk", "grp"), "tp"),
            P(("blk", "grp")),
            P(("blk", "grp")),
            P("grp", "blk", "tp"),
            P("grp", "blk", "tp"),
            P("grp", None, "tp"),
        ),
        out_specs=P(("blk", "grp"), "tp"),
        check_vma=False,
    )
```

```python
import functools

import jax
import jax.numpy as jnp
from jax import lax
from jax.experimental import pallas as pl
from jax.experimental.pallas import tpu as pltpu
from jax.sharding import PartitionSpec as P

PARAMS = pltpu.CompilerParams(vmem_limit_bytes=6 << 20)
VMEM = pl.BlockSpec(memory_space=pltpu.VMEM)
WHOLE = pl.BlockSpec(memory_space=pl.ANY)
DMA = pltpu.SemaphoreType.DMA
EXTRA = 16
FIRST, LAST = (0, 3, 2, 1), (0, 1, 3, 2)


def cost(flops, values, exps=0):
    return pl.CostEstimate(flops=flops, bytes_accessed=2 * values, transcendentals=exps)


def rows_at(index, size):
    return pl.ds(pl.multiple_of(index * size, size), size)


def after(x, *done):
    return lax.optimization_barrier((x, *done))[0]


def copy_all(pairs, sems):
    copies = [pltpu.make_async_copy(source, to, sems.at[i]) for i, (source, to) in enumerate(pairs)]
    for copy in copies:
        copy.start()
    for copy in copies:
        copy.wait()


def mine_kernel(tokens, out, sem):
    copy = pltpu.make_async_copy(tokens.at[rows_at(lax.axis_index("grp"), out.shape[0]), :], out, sem)
    copy.start()
    copy.wait()


def rest_kernel(groups, tokens, gate, up, first, *refs):
    outs, panel, sems = refs[: groups - 1], refs[groups - 1], refs[groups]
    group = lax.axis_index("grp")
    rows, hid = tokens.shape[0] // groups, gate.shape[0]
    pairs = [(tokens.at[rows_at(lax.rem(group + step, groups), rows), :], out) for step, out in enumerate(outs, 1)]
    copy_all(pairs + [(gate, panel.at[:hid, :]), (up, panel.at[hid:, :])], sems)


def prepare(tokens, gate, up, groups):
    rows, depth = tokens.shape
    hid, high = gate.shape
    block = jax.ShapeDtypeStruct((rows // groups, depth), tokens.dtype)
    tokens, gate, up = (pltpu.with_memory_space_constraint(x, pltpu.HBM) for x in (tokens, gate, up))
    mine = pl.pallas_call(
        mine_kernel,
        out_shape=block,
        in_specs=[WHOLE],
        out_specs=VMEM,
        scratch_shapes=[DMA],
        compiler_params=PARAMS,
        cost_estimate=cost(0, 2 * block.size),
        name="own_rows",
    )(tokens)
    *others, panel = pl.pallas_call(
        functools.partial(rest_kernel, groups),
        out_shape=[block] * (groups - 1) + [jax.ShapeDtypeStruct((2 * hid, high), gate.dtype)],
        in_specs=[WHOLE] * 4,
        out_specs=[VMEM] * groups,
        scratch_shapes=[DMA((groups + 1,))],
        compiler_params=PARAMS,
        cost_estimate=cost(0, 2 * rows * depth + 4 * high * hid),
        name="other_rows_and_weights",
    )(tokens, gate, up, mine)
    return [mine, *others], panel


def weigh_kernel(chances, counts, out):
    group, (groups, rows) = lax.axis_index("grp"), chances.shape
    every = chances[...].astype(jnp.float32)
    line = lax.broadcasted_iota(jnp.int32, every.shape, 0)
    slot = lax.broadcasted_iota(jnp.int32, (1, rows), 1)
    for step in range(groups):
        index = lax.rem(group + step, groups)
        chance = jnp.sum(jnp.where(line == index, every, 0.0), axis=0, keepdims=True)
        out[step : step + 1, :] = jnp.where(slot < counts[index], chance, 0.0)


def weigh(chances, counts):
    return pl.pallas_call(
        weigh_kernel,
        out_shape=jax.ShapeDtypeStruct(chances.shape, jnp.float32),
        in_specs=[VMEM, pl.BlockSpec(memory_space=pltpu.SMEM)],
        out_specs=VMEM,
        compiler_params=PARAMS,
        cost_estimate=cost(0, chances.size),
        name="weigh",
    )(chances, counts)


def attach_kernel(step, tokens, scales, out, sem):
    groups, rows = scales.shape
    index = lax.rem(lax.axis_index("grp") + step, groups)
    copy = pltpu.make_async_copy(tokens.at[rows_at(index, rows), :], out.at[:rows, :], sem)
    copy.start()
    lanes = out.shape[1]
    line = jnp.concatenate([scales[step : step + 1, :], jnp.zeros((1, lanes - rows), jnp.float32)], axis=1)
    out[rows:, :] = jnp.broadcast_to(line, (EXTRA, lanes)).astype(out.dtype)
    copy.wait()


def attach(step, tokens, scales):
    groups, rows = scales.shape
    depth = tokens.shape[1]
    return pl.pallas_call(
        functools.partial(attach_kernel, step),
        out_shape=jax.ShapeDtypeStruct((rows + EXTRA, depth), tokens.dtype),
        in_specs=[WHOLE, VMEM],
        out_specs=VMEM,
        scratch_shapes=[DMA],
        compiler_params=PARAMS,
        cost_estimate=cost(0, 2 * rows * depth),
        name="attach_weights",
    )(pltpu.with_memory_space_constraint(tokens, pltpu.HBM), scales)


def order_kernel(*refs):
    blocks, panel, sems = refs[:-2], refs[-2], refs[-1]
    mine = lax.axis_index("blk")
    copy_all([(block, panel.at[jnp.bitwise_xor(mine, j)]) for j, block in enumerate(blocks)], sems)


def in_order(blocks):
    n = len(blocks)
    return pl.pallas_call(
        order_kernel,
        out_shape=jax.ShapeDtypeStruct((n, *blocks[0].shape), blocks[0].dtype),
        in_specs=[WHOLE] * n,
        out_specs=VMEM,
        scratch_shapes=[DMA((n,))],
        compiler_params=PARAMS,
        cost_estimate=cost(0, 2 * n * blocks[0].size),
        name="weights_in_order",
    )(*blocks)


def swap(x, axis, bit):
    return lax.ppermute(x, axis, [(i, i ^ bit) for i in range(lax.axis_size(axis))])


def along(step, moves, straight=()):
    groups = lax.axis_size("grp")
    pairs = []
    for g in range(groups):
        pairs += [(g * 4 + a, (g + step) % groups * 4 + b) for a, b in moves]
        pairs += [(g * 4 + a, g * 4 + b) for a, b in straight]
    return pairs


def ring(block, step):
    right = lax.ppermute(block, ("grp", "tp"), along(step, [(i, (i + 1) % 4) for i in range(4)]))
    left = lax.ppermute(block, ("grp", "tp"), along(step, [(i, (i + 3) % 4) for i in range(4)]))
    return right, left


def choose_kernel(here, right, left, out):
    place = lax.axis_index("tp")
    inner = jnp.where(place == 2, right[...], left[...])
    out[...] = jnp.where(jnp.logical_or(place == 0, place == 3), here[...], inner)


def choose(here, right, left):
    return pl.pallas_call(
        choose_kernel,
        out_shape=jax.ShapeDtypeStruct(here.shape, here.dtype),
        in_specs=[VMEM] * 3,
        out_specs=VMEM,
        compiler_params=PARAMS,
        cost_estimate=cost(12000000000, 4 * here.size),
        name="choose",
    )(here, right, left)


def middle(block, step):
    return lax.ppermute(block, ("grp", "tp"), along(step, [(0, 2), (3, 1)], [(2, 3), (1, 0)]))


def product(panel, chunk, k):
    depth, high = chunk.shape[1], panel.shape[2]
    total = 0
    for i in range(depth // high):
        part = chunk[:, i * high : (i + 1) * high]
        total += lax.dot_general(
            panel[k * (depth // high) + i], part, (((1,), (1,)), ((), ())), preferred_element_type=jnp.float32
        )
    return total


def near_sum(place, panel, right, left):
    return product(panel, right[...], lax.rem(place + 3, 4)) + product(panel, left[...], lax.rem(place + 1, 4))


def finish(place, panel, total, opposite, weight):
    total += product(panel, opposite, place ^ 2)
    hid = total.shape[0] // 2
    gate, up = total[:hid], total[hid:]
    return gate / (1.0 + jnp.exp(-gate)) * up * weight


def sums_kernel(panel, x, *refs):
    place, count = lax.axis_index("tp"), len(refs) // 3
    near, outs = refs[: 2 * count], refs[2 * count :]
    for i, out in enumerate(outs):
        total = near_sum(place, panel, *near[2 * i : 2 * i + 2])
        out[...] = total if i else total + product(panel, x[...], place)


def hidden_kernel(panel, total, opposite, scales, out):
    place = lax.axis_index("tp")
    out[...] = finish(place, panel, total[...], opposite[...], scales[:1, :]).astype(out.dtype)


def finish_kernel(panel, total, x, opposite, out):
    place, rows = lax.axis_index("tp"), out.shape[1]
    weight = x[rows : rows + 1, :rows].astype(jnp.float32)
    here = total[...] + product(panel, x[:rows, :], place)
    out[...] = finish(place, panel, here, opposite[...], weight).astype(out.dtype)


def call_rows(kernel, chunks, name, outs, panel, *operands):
    share = chunks * panel.size // 4
    return pl.pallas_call(
        kernel,
        out_shape=outs,
        in_specs=[VMEM] * (1 + len(operands)),
        out_specs=[VMEM] * len(outs),
        compiler_params=PARAMS,
        cost_estimate=cost(2 * outs[0].shape[1] * share, share),
        name=name,
    )(panel, *operands)


def down_kernel(step, groups, places, *refs):
    hiddens = refs[:4]
    down, out, together, rows_here, sem = refs[-5:]
    place, group = lax.axis_index("tp"), lax.axis_index("grp")
    hid, rows = hiddens[0].shape
    for bits, hidden in zip(places, hiddens):
        together[rows_at(place ^ bits, hid), :] = hidden[...]
    total = lax.dot_general(
        together[...], down[...], (((0,), (0,)), ((), ())), preferred_element_type=jnp.float32
    )
    rows_here[...] = total.astype(rows_here.dtype)
    to = out.at[rows_at(lax.rem(group - step + groups, groups), rows), :]
    copy = pltpu.make_async_copy(rows_here, to, sem)
    copy.start()
    copy.wait()


def project_down(step, groups, places, hiddens, down, out):
    hid, rows = hiddens[0].shape
    wide = down.shape[1]
    earlier = [] if out is None else [out]
    return pl.pallas_call(
        functools.partial(down_kernel, step, groups, places),
        out_shape=jax.ShapeDtypeStruct((groups * rows, wide), jnp.bfloat16),
        in_specs=[VMEM] * 4 + [WHOLE] * len(earlier) + [VMEM],
        out_specs=WHOLE,
        scratch_shapes=[pltpu.VMEM((4 * hid, rows), jnp.bfloat16), pltpu.VMEM((rows, wide), jnp.bfloat16), DMA],
        input_output_aliases={4: 0} if earlier else {},
        compiler_params=PARAMS,
        cost_estimate=cost(2 * rows * down.size, down.size + rows * wide),
        name="project_down",
    )(*hiddens, *earlier, down)


def everywhere(hidden, places):
    return [swap(hidden, "tp", bits) if bits else hidden for bits in places]


def local(dispatched, route_prob, peer_rows, gate_weight, up_weight, down_weight):
    groups, blks = lax.axis_size("grp"), lax.axis_size("blk")
    per_peer = dispatched.shape[0] // groups
    hid = gate_weight.shape[2]

    rows, weight = prepare(dispatched, gate_weight[0].T, up_weight[0].T, groups)
    hops = [ring(rows[step], step) for step in range(groups)]
    opposites = [middle(choose(rows[step], *hops[step]), step) for step in range(groups)]

    scales = weigh(route_prob.reshape(groups, per_peer), peer_rows)
    for step in range(1, groups):
        block = attach(step, after(dispatched, *hops[0]), scales)
        rows[step] = lax.ppermute(block, "grp", [(i, (i + step) % groups) for i in range(groups)])

    have = {0: weight}
    bit = blks // 2
    while bit:
        for j in list(have):
            have[j ^ bit] = swap(have[j], "blk", bit)
        if bit == blks // 2:
            have[bit] = after(have[bit], *hops[0])
            have[0] = after(have[0], have[bit])
        bit //= 2
    panel = in_order([have[j] for j in range(blks)])

    sums = jax.ShapeDtypeStruct((2 * hid, per_peer), jnp.float32)
    hidden = jax.ShapeDtypeStruct((hid, per_peer), jnp.bfloat16)
    near = [chunk for hop in hops for chunk in hop]
    totals = call_rows(sums_kernel, 5, "chunk_sums", [sums] * groups, panel, rows[0], *near)
    out = None
    for step in range(groups):
        if step:
            operands = totals[step], rows[step], opposites[step]
            [done] = call_rows(finish_kernel, 2, "last_chunks", [hidden], panel, *operands)
        else:
            operands = totals[0], opposites[0], scales
            [done] = call_rows(hidden_kernel, 1, "hidden_rows", [hidden], panel, *operands)
        places = LAST if step == groups - 1 else FIRST
        out = project_down(step, groups, places, everywhere(done, places), down_weight[0], out)
    return out


def solution(mesh):
    return jax.shard_map(
        local,
        mesh=mesh,
        in_specs=(
            P(("blk", "grp"), "tp"),
            P(("blk", "grp")),
            P(("blk", "grp")),
            P("grp", "blk", "tp"),
            P("grp", "blk", "tp"),
            P("grp", None, "tp"),
        ),
        out_specs=P(("blk", "grp"), "tp"),
        check_vma=False,
    )
```

```python
import functools

import jax
import jax.numpy as jnp
from jax import lax
from jax.experimental import pallas as pl
from jax.experimental.pallas import tpu as pltpu
from jax.sharding import PartitionSpec as P

PARAMS = pltpu.CompilerParams(vmem_limit_bytes=6 << 20)
VMEM = pl.BlockSpec(memory_space=pltpu.VMEM)
WHOLE = pl.BlockSpec(memory_space=pl.ANY)
DMA = pltpu.SemaphoreType.DMA
AHEAD = 2
EXTRA = 16
PLACES = (0, 3, 2, 1)


def cost(flops, values, exps=0):
    return pl.CostEstimate(flops=flops, bytes_accessed=2 * values, transcendentals=exps)


def rows_at(index, size):
    return pl.ds(pl.multiple_of(index * size, size), size)


def after(x, *done):
    return lax.optimization_barrier((x, *done))[0]


def copy_all(pairs, sems):
    copies = [pltpu.make_async_copy(source, to, sems.at[i]) for i, (source, to) in enumerate(pairs)]
    for copy in copies:
        copy.start()
    for copy in copies:
        copy.wait()


def mine_kernel(tokens, out, sem):
    copy = pltpu.make_async_copy(tokens.at[rows_at(lax.axis_index("grp"), out.shape[0]), :], out, sem)
    copy.start()
    copy.wait()


def rest_kernel(groups, tokens, gate, up, first, *refs):
    outs, panel, sems = refs[: groups - 1], refs[groups - 1], refs[groups]
    group = lax.axis_index("grp")
    rows, hid = tokens.shape[0] // groups, gate.shape[0]
    pairs = [(tokens.at[rows_at(lax.rem(group + step, groups), rows), :], out) for step, out in enumerate(outs, 1)]
    copy_all(pairs + [(gate, panel.at[:hid, :]), (up, panel.at[hid:, :])], sems)


def prepare(tokens, gate, up, groups):
    rows, depth = tokens.shape
    hid, high = gate.shape
    block = jax.ShapeDtypeStruct((rows // groups, depth), tokens.dtype)
    tokens, gate, up = (pltpu.with_memory_space_constraint(x, pltpu.HBM) for x in (tokens, gate, up))
    mine = pl.pallas_call(
        mine_kernel,
        out_shape=block,
        in_specs=[WHOLE],
        out_specs=VMEM,
        scratch_shapes=[DMA],
        compiler_params=PARAMS,
        cost_estimate=cost(0, 2 * block.size),
        name="own_rows",
    )(tokens)
    *others, panel = pl.pallas_call(
        functools.partial(rest_kernel, groups),
        out_shape=[block] * (groups - 1) + [jax.ShapeDtypeStruct((2 * hid, high), gate.dtype)],
        in_specs=[WHOLE] * 4,
        out_specs=[VMEM] * groups,
        scratch_shapes=[DMA((groups + 1,))],
        compiler_params=PARAMS,
        cost_estimate=cost(0, 2 * rows * depth + 4 * high * hid),
        name="other_rows_and_weights",
    )(tokens, gate, up, mine)
    return [mine, *others], panel


def weigh_kernel(chances, counts, out):
    group, (groups, rows) = lax.axis_index("grp"), chances.shape
    every = chances[...].astype(jnp.float32)
    line = lax.broadcasted_iota(jnp.int32, every.shape, 0)
    slot = lax.broadcasted_iota(jnp.int32, (1, rows), 1)
    for step in range(groups):
        index = lax.rem(group + step, groups)
        chance = jnp.sum(jnp.where(line == index, every, 0.0), axis=0, keepdims=True)
        out[step : step + 1, :] = jnp.where(slot < counts[index], chance, 0.0)


def weigh(chances, counts):
    return pl.pallas_call(
        weigh_kernel,
        out_shape=jax.ShapeDtypeStruct(chances.shape, jnp.float32),
        in_specs=[VMEM, pl.BlockSpec(memory_space=pltpu.SMEM)],
        out_specs=VMEM,
        compiler_params=PARAMS,
        cost_estimate=cost(0, chances.size),
        name="weigh",
    )(chances, counts)


def attach_kernel(step, tokens, scales, out, sem):
    groups, rows = scales.shape
    index = lax.rem(lax.axis_index("grp") + step, groups)
    copy = pltpu.make_async_copy(tokens.at[rows_at(index, rows), :], out.at[:rows, :], sem)
    copy.start()
    lanes = out.shape[1]
    line = jnp.concatenate([scales[step : step + 1, :], jnp.zeros((1, lanes - rows), jnp.float32)], axis=1)
    out[rows:, :] = jnp.broadcast_to(line, (EXTRA, lanes)).astype(out.dtype)
    copy.wait()


def attach(step, tokens, scales):
    groups, rows = scales.shape
    depth = tokens.shape[1]
    return pl.pallas_call(
        functools.partial(attach_kernel, step),
        out_shape=jax.ShapeDtypeStruct((rows + EXTRA, depth), tokens.dtype),
        in_specs=[WHOLE, VMEM],
        out_specs=VMEM,
        scratch_shapes=[DMA],
        compiler_params=PARAMS,
        cost_estimate=cost(0, 2 * rows * depth),
        name="attach_weights",
    )(pltpu.with_memory_space_constraint(tokens, pltpu.HBM), scales)


def order_kernel(*refs):
    blocks, panel, sems = refs[:-2], refs[-2], refs[-1]
    mine = lax.axis_index("blk")
    copy_all([(block, panel.at[jnp.bitwise_xor(mine, j)]) for j, block in enumerate(blocks)], sems)


def in_order(blocks):
    n = len(blocks)
    return pl.pallas_call(
        order_kernel,
        out_shape=jax.ShapeDtypeStruct((n, *blocks[0].shape), blocks[0].dtype),
        in_specs=[WHOLE] * n,
        out_specs=VMEM,
        scratch_shapes=[DMA((n,))],
        compiler_params=PARAMS,
        cost_estimate=cost(0, 2 * n * blocks[0].size),
        name="weights_in_order",
    )(*blocks)


def swap(x, axis, bit):
    return lax.ppermute(x, axis, [(i, i ^ bit) for i in range(lax.axis_size(axis))])


def along(step, moves, straight=()):
    groups = lax.axis_size("grp")
    pairs = []
    for g in range(groups):
        pairs += [(g * 4 + a, (g + step) % groups * 4 + b) for a, b in moves]
        pairs += [(g * 4 + a, g * 4 + b) for a, b in straight]
    return pairs


def ring(block, step):
    right = lax.ppermute(block, ("grp", "tp"), along(step, [(i, (i + 1) % 4) for i in range(4)]))
    left = lax.ppermute(block, ("grp", "tp"), along(step, [(i, (i + 3) % 4) for i in range(4)]))
    return right, left


def choose_kernel(here, right, left, out):
    place = lax.axis_index("tp")
    inner = jnp.where(place == 2, right[...], left[...])
    out[...] = jnp.where(jnp.logical_or(place == 0, place == 3), here[...], inner)


def choose(here, right, left):
    return pl.pallas_call(
        choose_kernel,
        out_shape=jax.ShapeDtypeStruct(here.shape, here.dtype),
        in_specs=[VMEM] * 3,
        out_specs=VMEM,
        compiler_params=PARAMS,
        cost_estimate=cost(8000000000, 4 * here.size),
        name="choose",
    )(here, right, left)


def middle(block, step):
    return lax.ppermute(block, ("grp", "tp"), along(step, [(0, 2), (3, 1)], [(2, 3), (1, 0)]))


def product(panel, chunk, k):
    depth, high = chunk.shape[1], panel.shape[2]
    total = 0
    for i in range(depth // high):
        part = chunk[:, i * high : (i + 1) * high]
        total += lax.dot_general(
            panel[k * (depth // high) + i], part, (((1,), (1,)), ((), ())), preferred_element_type=jnp.float32
        )
    return total


def near_sum(place, panel, right, left):
    return product(panel, right[...], lax.rem(place + 3, 4)) + product(panel, left[...], lax.rem(place + 1, 4))


def finish(place, panel, total, x, opposite, weight):
    total += product(panel, x, place)
    total += product(panel, opposite, lax.rem(place + 2, 4))
    hid = total.shape[0] // 2
    gate, up = total[:hid], total[hid:]
    return gate / (1.0 + jnp.exp(-gate)) * up * weight


def hidden_kernel(panel, right, left, x, opposite, scales, *refs):
    place, count = lax.axis_index("tp"), len(refs) // 3
    others, out, sums = refs[: 2 * count], refs[2 * count], refs[2 * count + 1 :]
    total = near_sum(place, panel, right, left)
    out[...] = finish(place, panel, total, x[...], opposite[...], scales[:1, :]).astype(out.dtype)
    for i, to in enumerate(sums):
        to[...] = near_sum(place, panel, *others[2 * i : 2 * i + 2])


def finish_kernel(panel, total, x, opposite, out):
    rows = out.shape[1]
    weight = x[rows : rows + 1, :rows].astype(jnp.float32)
    out[...] = finish(lax.axis_index("tp"), panel, total[...], x[:rows, :], opposite[...], weight).astype(out.dtype)


def call_rows(kernel, chunks, name, outs, panel, *operands):
    share = chunks * panel.size // 4
    return pl.pallas_call(
        kernel,
        out_shape=outs,
        in_specs=[VMEM] * (1 + len(operands)),
        out_specs=[VMEM] * len(outs),
        compiler_params=PARAMS,
        cost_estimate=cost(2 * outs[0].shape[1] * share, share),
        name=name,
    )(panel, *operands)


def down_sum(hiddens, places, down):
    place = lax.axis_index("tp")
    hid = hiddens[0].shape[0]
    total = 0
    for hidden, bits in zip(hiddens, places):
        part = down[rows_at(place ^ bits, hid), :]
        total += lax.dot_general(hidden[...], part, (((0,), (0,)), ((), ())), preferred_element_type=jnp.float32)
    return total


def early_kernel(places, *refs):
    refs[-1][...] = down_sum(refs[:-2], places, refs[-2])


def down_kernel(step, groups, places, *refs):
    count = len(places)
    hiddens, down = refs[:count], refs[count]
    out, rows_here, sem = refs[-3:]
    group = lax.axis_index("grp")
    rows = hiddens[0].shape[1]
    total = down_sum(hiddens, places, down)
    if count < 4:
        total += refs[count + 1][...]
    rows_here[...] = total.astype(rows_here.dtype)
    to = out.at[rows_at(lax.rem(group - step + groups, groups), rows), :]
    copy = pltpu.make_async_copy(rows_here, to, sem)
    copy.start()
    copy.wait()


def early_sum(hiddens, places, down):
    rows, wide = hiddens[0].shape[1], down.shape[1]
    return pl.pallas_call(
        functools.partial(early_kernel, places),
        out_shape=jax.ShapeDtypeStruct((rows, wide), jnp.float32),
        in_specs=[VMEM] * (len(hiddens) + 1),
        out_specs=VMEM,
        compiler_params=PARAMS,
        cost_estimate=cost(0, 0),
        name="early_down",
    )(*hiddens, down)


def project_down(step, groups, hiddens, down, out, ahead):
    rows, wide = hiddens[0].shape[1], down.shape[1]
    places = PLACES
    earlier = [] if out is None else [out]
    sums = []
    if ahead:
        sums = [early_sum(hiddens[:ahead], places[:ahead], down)]
        hiddens, places = hiddens[ahead:], places[ahead:]
    count = len(hiddens)
    return pl.pallas_call(
        functools.partial(down_kernel, step, groups, places),
        out_shape=jax.ShapeDtypeStruct((groups * rows, wide), jnp.bfloat16),
        in_specs=[VMEM] * (count + 1 + len(sums)) + [WHOLE] * len(earlier),
        out_specs=WHOLE,
        scratch_shapes=[pltpu.VMEM((rows, wide), jnp.bfloat16), DMA],
        input_output_aliases={count + 1 + len(sums): 0} if earlier else {},
        compiler_params=PARAMS,
        cost_estimate=cost(rows * down.size if ahead else 8000000000, down.size + rows * wide),
        name="project_down",
    )(*hiddens, down, *sums, *earlier)


def everywhere(hidden):
    return [swap(hidden, "tp", bits) if bits else hidden for bits in PLACES]


def local(dispatched, route_prob, peer_rows, gate_weight, up_weight, down_weight):
    groups, blks = lax.axis_size("grp"), lax.axis_size("blk")
    per_peer = dispatched.shape[0] // groups
    hid = gate_weight.shape[2]

    rows, weight = prepare(dispatched, gate_weight[0].T, up_weight[0].T, groups)
    hops = [ring(rows[step], step) for step in range(groups)]
    opposites = [middle(choose(rows[step], *hops[step]), step) for step in range(groups)]

    scales = weigh(route_prob.reshape(groups, per_peer), peer_rows)
    for step in range(1, groups):
        block = attach(step, after(dispatched, *hops[0]), scales)
        rows[step] = lax.ppermute(block, "grp", [(i, (i + step) % groups) for i in range(groups)])

    have = {0: weight}
    bit = blks // 2
    while bit:
        for j in list(have):
            have[j ^ bit] = swap(have[j], "blk", bit)
        if bit == blks // 2:
            have[bit] = after(have[bit], *hops[0])
            have[0] = after(have[0], have[bit])
        bit //= 2
    panel = in_order([have[j] for j in range(blks)])

    sums = jax.ShapeDtypeStruct((2 * hid, per_peer), jnp.float32)
    hidden = jax.ShapeDtypeStruct((hid, per_peer), jnp.bfloat16)
    near = [chunk for hop in hops[1:] for chunk in hop]
    mine, *totals = call_rows(
        hidden_kernel, 4, "hidden_rows", [hidden] + [sums] * (groups - 1),
        panel, *hops[0], rows[0], opposites[0], scales, *near,
    )
    out = None
    for step in range(groups):
        done = mine
        if step:
            operands = totals[step - 1], rows[step], opposites[step]
            [done] = call_rows(finish_kernel, 2, "last_chunks", [hidden], panel, *operands)
        out = project_down(step, groups, everywhere(done), down_weight[0], out, AHEAD if step == groups - 1 else 0)
    return out


def solution(mesh):
    return jax.shard_map(
        local,
        mesh=mesh,
        in_specs=(
            P(("blk", "grp"), "tp"),
            P(("blk", "grp")),
            P(("blk", "grp")),
            P("grp", "blk", "tp"),
            P("grp", "blk", "tp"),
            P("grp", None, "tp"),
        ),
        out_specs=P(("blk", "grp"), "tp"),
        check_vma=False,
    )
```

```python
import functools

import jax
import jax.numpy as jnp
from jax import lax
from jax.experimental import pallas as pl
from jax.experimental.pallas import tpu as pltpu
from jax.sharding import PartitionSpec as P

PARAMS = pltpu.CompilerParams(vmem_limit_bytes=6 << 20)
VMEM = pl.BlockSpec(memory_space=pltpu.VMEM)
WHOLE = pl.BlockSpec(memory_space=pl.ANY)
DMA = pltpu.SemaphoreType.DMA
AHEAD = 3
EXTRA = 16
PLACES = (0, 3, 2, 1)


def cost(flops, values, exps=0):
    return pl.CostEstimate(flops=flops, bytes_accessed=2 * values, transcendentals=exps)


def rows_at(index, size):
    return pl.ds(pl.multiple_of(index * size, size), size)


def after(x, *done):
    return lax.optimization_barrier((x, *done))[0]


def copy_all(pairs, sems):
    copies = [pltpu.make_async_copy(source, to, sems.at[i]) for i, (source, to) in enumerate(pairs)]
    for copy in copies:
        copy.start()
    for copy in copies:
        copy.wait()


def mine_kernel(tokens, out, sem):
    copy = pltpu.make_async_copy(tokens.at[rows_at(lax.axis_index("grp"), out.shape[0]), :], out, sem)
    copy.start()
    copy.wait()


def rest_kernel(groups, tokens, gate, up, first, *refs):
    outs, panel, sems = refs[: groups - 1], refs[groups - 1], refs[groups]
    group = lax.axis_index("grp")
    rows, hid = tokens.shape[0] // groups, gate.shape[0]
    pairs = [(tokens.at[rows_at(lax.rem(group + step, groups), rows), :], out) for step, out in enumerate(outs, 1)]
    copy_all(pairs + [(gate, panel.at[:hid, :]), (up, panel.at[hid:, :])], sems)


def prepare(tokens, gate, up, groups):
    rows, depth = tokens.shape
    hid, high = gate.shape
    block = jax.ShapeDtypeStruct((rows // groups, depth), tokens.dtype)
    tokens, gate, up = (pltpu.with_memory_space_constraint(x, pltpu.HBM) for x in (tokens, gate, up))
    mine = pl.pallas_call(
        mine_kernel,
        out_shape=block,
        in_specs=[WHOLE],
        out_specs=VMEM,
        scratch_shapes=[DMA],
        compiler_params=PARAMS,
        cost_estimate=cost(0, 2 * block.size),
        name="own_rows",
    )(tokens)
    *others, panel = pl.pallas_call(
        functools.partial(rest_kernel, groups),
        out_shape=[block] * (groups - 1) + [jax.ShapeDtypeStruct((2 * hid, high), gate.dtype)],
        in_specs=[WHOLE] * 4,
        out_specs=[VMEM] * groups,
        scratch_shapes=[DMA((groups + 1,))],
        compiler_params=PARAMS,
        cost_estimate=cost(0, 2 * rows * depth + 4 * high * hid),
        name="other_rows_and_weights",
    )(tokens, gate, up, mine)
    return [mine, *others], panel


def weigh_kernel(chances, counts, out):
    group, (groups, rows) = lax.axis_index("grp"), chances.shape
    every = chances[...].astype(jnp.float32)
    line = lax.broadcasted_iota(jnp.int32, every.shape, 0)
    slot = lax.broadcasted_iota(jnp.int32, (1, rows), 1)
    for step in range(groups):
        index = lax.rem(group + step, groups)
        chance = jnp.sum(jnp.where(line == index, every, 0.0), axis=0, keepdims=True)
        out[step : step + 1, :] = jnp.where(slot < counts[index], chance, 0.0)


def weigh(chances, counts):
    return pl.pallas_call(
        weigh_kernel,
        out_shape=jax.ShapeDtypeStruct(chances.shape, jnp.float32),
        in_specs=[VMEM, pl.BlockSpec(memory_space=pltpu.SMEM)],
        out_specs=VMEM,
        compiler_params=PARAMS,
        cost_estimate=cost(0, chances.size),
        name="weigh",
    )(chances, counts)


def attach_kernel(step, tokens, scales, out, sem):
    groups, rows = scales.shape
    index = lax.rem(lax.axis_index("grp") + step, groups)
    copy = pltpu.make_async_copy(tokens.at[rows_at(index, rows), :], out.at[:rows, :], sem)
    copy.start()
    lanes = out.shape[1]
    line = jnp.concatenate([scales[step : step + 1, :], jnp.zeros((1, lanes - rows), jnp.float32)], axis=1)
    out[rows:, :] = jnp.broadcast_to(line, (EXTRA, lanes)).astype(out.dtype)
    copy.wait()


def attach(step, tokens, scales):
    groups, rows = scales.shape
    depth = tokens.shape[1]
    return pl.pallas_call(
        functools.partial(attach_kernel, step),
        out_shape=jax.ShapeDtypeStruct((rows + EXTRA, depth), tokens.dtype),
        in_specs=[WHOLE, VMEM],
        out_specs=VMEM,
        scratch_shapes=[DMA],
        compiler_params=PARAMS,
        cost_estimate=cost(0, 2 * rows * depth),
        name="attach_weights",
    )(pltpu.with_memory_space_constraint(tokens, pltpu.HBM), scales)


def order_kernel(*refs):
    blocks, panel, sems = refs[:-2], refs[-2], refs[-1]
    mine = lax.axis_index("blk")
    copy_all([(block, panel.at[jnp.bitwise_xor(mine, j)]) for j, block in enumerate(blocks)], sems)


def in_order(blocks):
    n = len(blocks)
    return pl.pallas_call(
        order_kernel,
        out_shape=jax.ShapeDtypeStruct((n, *blocks[0].shape), blocks[0].dtype),
        in_specs=[WHOLE] * n,
        out_specs=VMEM,
        scratch_shapes=[DMA((n,))],
        compiler_params=PARAMS,
        cost_estimate=cost(0, 2 * n * blocks[0].size),
        name="weights_in_order",
    )(*blocks)


def swap(x, axis, bit):
    return lax.ppermute(x, axis, [(i, i ^ bit) for i in range(lax.axis_size(axis))])


def along(step, moves, straight=()):
    groups = lax.axis_size("grp")
    pairs = []
    for g in range(groups):
        pairs += [(g * 4 + a, (g + step) % groups * 4 + b) for a, b in moves]
        pairs += [(g * 4 + a, g * 4 + b) for a, b in straight]
    return pairs


def ring(block, step):
    right = lax.ppermute(block, ("grp", "tp"), along(step, [(i, (i + 1) % 4) for i in range(4)]))
    left = lax.ppermute(block, ("grp", "tp"), along(step, [(i, (i + 3) % 4) for i in range(4)]))
    return right, left


def choose_kernel(here, right, left, out):
    place = lax.axis_index("tp")
    inner = jnp.where(place == 2, right[...], left[...])
    out[...] = jnp.where(jnp.logical_or(place == 0, place == 3), here[...], inner)


def choose(here, right, left):
    return pl.pallas_call(
        choose_kernel,
        out_shape=jax.ShapeDtypeStruct(here.shape, here.dtype),
        in_specs=[VMEM] * 3,
        out_specs=VMEM,
        compiler_params=PARAMS,
        cost_estimate=cost(8000000000, 4 * here.size),
        name="choose",
    )(here, right, left)


def middle(block, step):
    return lax.ppermute(block, ("grp", "tp"), along(step, [(0, 2), (3, 1)], [(2, 3), (1, 0)]))


def product(panel, chunk, k):
    depth, high = chunk.shape[1], panel.shape[2]
    total = 0
    for i in range(depth // high):
        part = chunk[:, i * high : (i + 1) * high]
        total += lax.dot_general(
            panel[k * (depth // high) + i], part, (((1,), (1,)), ((), ())), preferred_element_type=jnp.float32
        )
    return total


def near_sum(place, panel, right, left):
    return product(panel, right[...], lax.rem(place + 3, 4)) + product(panel, left[...], lax.rem(place + 1, 4))


def finish(place, panel, total, x, opposite, weight):
    total += product(panel, x, place)
    total += product(panel, opposite, lax.rem(place + 2, 4))
    hid = total.shape[0] // 2
    gate, up = total[:hid], total[hid:]
    return gate / (1.0 + jnp.exp(-gate)) * up * weight


def hidden_kernel(panel, right, left, x, opposite, scales, *refs):
    place, count = lax.axis_index("tp"), len(refs) // 3
    others, out, sums = refs[: 2 * count], refs[2 * count], refs[2 * count + 1 :]
    total = near_sum(place, panel, right, left)
    out[...] = finish(place, panel, total, x[...], opposite[...], scales[:1, :]).astype(out.dtype)
    for i, to in enumerate(sums):
        to[...] = near_sum(place, panel, *others[2 * i : 2 * i + 2])


def finish_kernel(panel, total, x, opposite, out):
    rows = out.shape[1]
    weight = x[rows : rows + 1, :rows].astype(jnp.float32)
    out[...] = finish(lax.axis_index("tp"), panel, total[...], x[:rows, :], opposite[...], weight).astype(out.dtype)


def call_rows(kernel, chunks, name, outs, panel, *operands):
    share = chunks * panel.size // 4
    return pl.pallas_call(
        kernel,
        out_shape=outs,
        in_specs=[VMEM] * (1 + len(operands)),
        out_specs=[VMEM] * len(outs),
        compiler_params=PARAMS,
        cost_estimate=cost(2 * outs[0].shape[1] * share, share),
        name=name,
    )(panel, *operands)


def down_sum(hiddens, places, down):
    place = lax.axis_index("tp")
    hid = hiddens[0].shape[0]
    total = 0
    for hidden, bits in zip(hiddens, places):
        part = down[rows_at(place ^ bits, hid), :]
        total += lax.dot_general(hidden[...], part, (((0,), (0,)), ((), ())), preferred_element_type=jnp.float32)
    return total


def early_kernel(places, *refs):
    refs[-1][...] = down_sum(refs[:-2], places, refs[-2])


def down_kernel(step, groups, places, *refs):
    count = len(places)
    hiddens, down = refs[:count], refs[count]
    out, rows_here, sem = refs[-3:]
    group = lax.axis_index("grp")
    rows = hiddens[0].shape[1]
    total = down_sum(hiddens, places, down)
    if count < 4:
        total += refs[count + 1][...]
    rows_here[...] = total.astype(rows_here.dtype)
    to = out.at[rows_at(lax.rem(group - step + groups, groups), rows), :]
    copy = pltpu.make_async_copy(rows_here, to, sem)
    copy.start()
    copy.wait()


def early_sum(hiddens, places, down):
    rows, wide = hiddens[0].shape[1], down.shape[1]
    return pl.pallas_call(
        functools.partial(early_kernel, places),
        out_shape=jax.ShapeDtypeStruct((rows, wide), jnp.float32),
        in_specs=[VMEM] * (len(hiddens) + 1),
        out_specs=VMEM,
        compiler_params=PARAMS,
        cost_estimate=cost(0, 0),
        name="early_down",
    )(*hiddens, down)


def project_down(step, groups, hiddens, down, out, ahead):
    rows, wide = hiddens[0].shape[1], down.shape[1]
    places = PLACES
    earlier = [] if out is None else [out]
    sums = []
    if ahead:
        sums = [early_sum(hiddens[:ahead], places[:ahead], down)]
        hiddens, places = hiddens[ahead:], places[ahead:]
    count = len(hiddens)
    return pl.pallas_call(
        functools.partial(down_kernel, step, groups, places),
        out_shape=jax.ShapeDtypeStruct((groups * rows, wide), jnp.bfloat16),
        in_specs=[VMEM] * (count + 1 + len(sums)) + [WHOLE] * len(earlier),
        out_specs=WHOLE,
        scratch_shapes=[pltpu.VMEM((rows, wide), jnp.bfloat16), DMA],
        input_output_aliases={count + 1 + len(sums): 0} if earlier else {},
        compiler_params=PARAMS,
        cost_estimate=cost(rows * down.size if ahead else 8000000000, down.size + rows * wide),
        name="project_down",
    )(*hiddens, down, *sums, *earlier)


def everywhere(hidden):
    return [swap(hidden, "tp", bits) if bits else hidden for bits in PLACES]


def local(dispatched, route_prob, peer_rows, gate_weight, up_weight, down_weight):
    groups, blks = lax.axis_size("grp"), lax.axis_size("blk")
    per_peer = dispatched.shape[0] // groups
    hid = gate_weight.shape[2]

    rows, weight = prepare(dispatched, gate_weight[0].T, up_weight[0].T, groups)
    hops = [ring(rows[step], step) for step in range(groups)]
    opposites = [middle(choose(rows[step], *hops[step]), step) for step in range(groups)]

    scales = weigh(route_prob.reshape(groups, per_peer), peer_rows)
    for step in range(1, groups):
        block = attach(step, after(dispatched, *hops[0]), scales)
        rows[step] = lax.ppermute(block, "grp", [(i, (i + step) % groups) for i in range(groups)])

    have = {0: weight}
    bit = blks // 2
    while bit:
        for j in list(have):
            have[j ^ bit] = swap(have[j], "blk", bit)
        if bit == blks // 2:
            have[bit] = after(have[bit], *hops[0])
            have[0] = after(have[0], have[bit])
        bit //= 2
    panel = in_order([have[j] for j in range(blks)])

    sums = jax.ShapeDtypeStruct((2 * hid, per_peer), jnp.float32)
    hidden = jax.ShapeDtypeStruct((hid, per_peer), jnp.bfloat16)
    near = [chunk for hop in hops[1:] for chunk in hop]
    mine, *totals = call_rows(
        hidden_kernel, 4, "hidden_rows", [hidden] + [sums] * (groups - 1),
        panel, *hops[0], rows[0], opposites[0], scales, *near,
    )
    out = None
    for step in range(groups):
        done = mine
        if step:
            operands = totals[step - 1], rows[step], opposites[step]
            [done] = call_rows(finish_kernel, 2, "last_chunks", [hidden], panel, *operands)
        out = project_down(step, groups, everywhere(done), down_weight[0], out, AHEAD if step == groups - 1 else 0)
    return out


def solution(mesh):
    return jax.shard_map(
        local,
        mesh=mesh,
        in_specs=(
            P(("blk", "grp"), "tp"),
            P(("blk", "grp")),
            P(("blk", "grp")),
            P("grp", "blk", "tp"),
            P("grp", "blk", "tp"),
            P("grp", None, "tp"),
        ),
        out_specs=P(("blk", "grp"), "tp"),
        check_vma=False,
    )
```
